32 devices in a mesh: dp: 8 (over y, x, core), fsdp: 4 (over z).
Axes of the slice: x: 2, y: 2, z: 4, core: 2. Of those that a mesh axis runs over, the one named last changes fastest.
Arguments:
- tokens: bfloat16 [3, 16384, 512], P(None, ('dp', 'fsdp')), may hold values from -6 to 6
- memory: bfloat16 [3, 16384, 512], P(None, ('dp', 'fsdp')), may hold values from -6 to 6
- cotangent: bfloat16 [3, 16384, 512], P(None, ('dp', 'fsdp')), may hold values from -6 to 6
- lengths: int32 [3, 8, 4], P(None, 'dp'), may hold values from 1 to 1024, 2048 in all within a row
- seq_order: int32 [3, 8, 4], P(None, 'dp'), may hold values from 0 to 3, each once within a row
- memory_pick: int32 [3, 8, 4], P(None, 'dp'), may hold values from 0 to 1
- self_attn: bfloat16 [2048, 512], P(('dp', 'fsdp'))
- cross_attn: bfloat16 [2048, 512], P(('dp', 'fsdp'))
- ffn_in: bfloat16 [512, 2048], P(('dp', 'fsdp')), may hold values from -0.25 to 0.25
- ffn_in_bias: bfloat16 [2048], P(('dp', 'fsdp')), may hold values from -1.75 to 1.75
- ffn_out: bfloat16 [2048, 512], P(('dp', 'fsdp')), may hold values from -0.125 to 0.125
- ffn_out_bias: bfloat16 [512], P(('dp', 'fsdp')), may hold values from -1.75 to 1.75
- norm_gain: bfloat16 [512, 3], P(('dp', 'fsdp')), may hold values from 0.5 to 1.5
- norm_bias: bfloat16 [512, 3], P(('dp', 'fsdp')), may hold values from -1.75 to 1.75
Outputs:
- layer_output: float32 [3, 16384, 512], P(None, ('dp', 'fsdp'))
- input_grad: float32 [3, 16384, 512], P(None, ('dp', 'fsdp'))
- memory_grad: float32 [3, 16384, 512], P(None, ('dp', 'fsdp'))
- self_attn_grad: float32 [2048, 512], P(('dp', 'fsdp'))
- cross_attn_grad: float32 [2048, 512], P(('dp', 'fsdp'))
- ffn_in_grad: float32 [512, 2048], P(('dp', 'fsdp'))
- ffn_in_bias_grad: float32 [2048], P(('dp', 'fsdp'))
- ffn_out_grad: float32 [2048, 512], P(('dp', 'fsdp'))
- ffn_out_bias_grad: float32 [512], P(('dp', 'fsdp'))
- norm_gain_grad: float32 [512, 3], P(('dp', 'fsdp'))
- norm_bias_grad: float32 [512, 3], P(('dp', 'fsdp'))
The draws below stay inside these ranges and needn't reach their ends.
Inputs may be any that keep to these rules, and one draw needn't show every extreme that they name: Each row holds the 4 sequence lengths of one group; they sum to 2048 and the longest is exactly 1024. `seq_order`: each row is a permutation of the 4 sequences of one group.
All inputs are finite; a program needn't handle non-finite values.
Results may differ from the reference program's by a relative error of at most 0.025.
The reference program's roundings to bfloat16 on the way count: a program that leaves them out, or rounds other values in their place, can miss the bound.
Values may be sent and summed in bfloat16 or wider, within the bound.
No kernel may reach another device: no remote copies, remote signals or barrier semaphores. Data moves between devices by JAX's collectives and lax.ppermute only.
A program may use at most 576 MiB of HBM per device.

```python
import math
import jax
import jax.numpy as jnp
import numpy as np
from jax import lax

D = 512
HEADS = 8
HEAD_DIM = 64
FF = 2048
MICRO = 3
SEQS = 4
NMEM = 2
MEM_LEN = 1024
GROUP = 2048
LONGEST = 1024
TOKENS = 16384
MEM_ROWS = 16384
N_DP = 8


def attention_stack(seed_key, query_scale):
    scales = jnp.array([query_scale, 1.0, 1.0, 4.0], jnp.float32)
    standard = jax.random.normal(seed_key, (4, D, D), jnp.float32)
    return (standard * scales[:, None, None] * D ** (-0.5)).reshape(4 * D, D).astype(jnp.bfloat16)


def draw_self_attn(key, part):
    return attention_stack(jax.random.fold_in(key, 11), 1.5)


def draw_cross_attn(key, part):
    return attention_stack(jax.random.fold_in(key, 23), 1.5)


def set_ends(values, own_key, least, high):
    dims = values.shape
    spot = [jax.random.randint(jax.random.fold_in(own_key, axis), (), 0, dims[axis]) for axis in range(len(dims))]
    values = values.at[tuple(spot)].set(least)
    longest = dims.index(max(dims))
    spot[longest] = (spot[longest] + 1) % dims[longest]
    return values.at[tuple(spot)].set(high)


def level_of(own_key, shape, split, smallest, high):
    def one(dim, shards_of):
        steps = jax.random.uniform(jax.random.fold_in(jax.random.fold_in(own_key, 6), dim), (shards_of,), jnp.float32, smallest / len(split), high / len(split))
        return jnp.repeat(jnp.exp(steps), shape[dim] // shards_of).reshape((-1,) + (1,) * (len(shape) - dim - 1))

    level = one(*split[0])
    for cut in split[1:]:
        level = level * one(*cut)
    return level


def length_profile(number_of, total, reach, slope):
    weights = [(1 << 20) // math.isqrt(standing ** slope) + 1 for standing in range(2, number_of + 1)]
    rest, counts = total - reach - (number_of - 1), [1] * (number_of - 1)
    while rest > 0:
        free = [i for i in range(number_of - 1) if counts[i] < reach]
        mass, budget = sum([weights[i] for i in free]), rest
        for i in free:
            more = min(reach - counts[i], max(1, budget * weights[i] // mass), rest)
            counts[i] = counts[i] + more
            rest = rest - more
    return np.array([reach] + counts)


def uneven_parts(rng, count, total, bound, slope):
    if count == 2:
        one = jax.random.randint(rng, (), max(1, total - bound), min(bound, total - 1) + 1)
        return jnp.stack([one, total - one])
    sizes = jnp.asarray(length_profile(count, total, bound, slope), jnp.int32)
    twos = (count - 1) // 2
    giver, taker = sizes[1:1 + 2 * twos:2], sizes[2:2 + 2 * twos:2]
    room = jnp.minimum(giver - 1, bound - taker)
    passed = jax.random.randint(jax.random.fold_in(rng, 1), (twos,), 0, 1 << 20) % (room + 1)
    sizes = sizes.at[1:1 + 2 * twos:2].set(giver - passed).at[2:2 + 2 * twos:2].set(taker + passed)
    return sizes[jax.random.permutation(jax.random.fold_in(rng, 2), count)]


def centred(key, shape, scale, limit, shards=(), kind=jnp.bfloat16):
    values = jax.random.normal(key, shape, jnp.float32) * scale
    if len(shards) > 0:
        values = level_of(key, shape, shards, -0.22, 0.18) * values
    return jnp.clip(values, min=-limit, max=limit).astype(kind)


def setup_inputs(seed: int = 0) -> dict:
    streams_of = jax.random.split(jax.random.key(seed), 15)
    tokens = centred(streams_of[0], (MICRO, TOKENS, D), 1.0, 6.0, ((1, 32),))
    memory = centred(streams_of[1], (MICRO, MEM_ROWS, D), 1.0, 6.0, ((1, 32),))
    cotangent = centred(streams_of[2], (MICRO, TOKENS, D), 1.0, 6.0, ((1, 32),))
    lengths = jax.vmap(lambda own: uneven_parts(own, SEQS, GROUP, LONGEST, 2))(jax.random.split(streams_of[3], MICRO * N_DP)).reshape((MICRO, N_DP, SEQS)).astype(jnp.int32)
    seq_order = jax.vmap(lambda own: jax.random.permutation(own, SEQS))(jax.random.split(streams_of[4], MICRO * N_DP)).reshape((MICRO, N_DP, SEQS)).astype(jnp.int32)
    memory_pick = set_ends(jax.random.randint(streams_of[5], (MICRO, N_DP, SEQS), 0, NMEM), jax.random.fold_in(streams_of[5], 1), 0, NMEM - 1).astype(jnp.int32)
    self_attn = draw_self_attn(jax.random.fold_in(streams_of[14], 71), 0)
    cross_attn = draw_cross_attn(jax.random.fold_in(streams_of[14], 71), 0)
    ffn_in = centred(streams_of[8], (D, FF), D ** -0.5, 0.25, ((0, 32),))
    ffn_in_bias = centred(streams_of[9], (FF,), 0.3, 1.75, ((0, 32),))
    ffn_out = centred(streams_of[10], (FF, D), FF ** -0.5, 0.125, ((0, 32),))
    ffn_out_bias = centred(streams_of[11], (D,), 0.3, 1.75, ((0, 32),))
    norm_gain = jnp.clip(1.0 + 0.1 * jax.random.normal(streams_of[12], (D, 3), jnp.float32), 0.5, 1.5).astype(jnp.bfloat16)
    norm_bias = centred(streams_of[13], (D, 3), 0.3, 1.75, ((0, 32),))
    return dict(tokens=tokens, memory=memory, cotangent=cotangent, lengths=lengths, seq_order=seq_order, memory_pick=memory_pick, self_attn=self_attn, cross_attn=cross_attn, ffn_in=ffn_in, ffn_in_bias=ffn_in_bias, ffn_out=ffn_out, ffn_out_bias=ffn_out_bias, norm_gain=norm_gain, norm_bias=norm_bias)


@jax.custom_vjp
def low(v):
    return lax.optimization_barrier(v.astype(jnp.bfloat16)).astype(jnp.float32)

@jax.custom_vjp
def low_back(v):
    return v

def low_keep(v):
    return (low(v), None)

def low_pass(kept, grad):
    return (grad,)

def back_keep(v):
    return (v, None)

def back_low(kept, grad):
    return (low(grad),)
low.defvjp(low_keep, low_pass)
low_back.defvjp(back_keep, back_low)
precise = lax.Precision.HIGHEST

def matmul_full(left, right):
    return jnp.dot(left, right, precision=precise)

def rounded(value):
    return low(low_back(value))

def layer_norm(resid, gain, shift):
    center = resid - lax.optimization_barrier(jnp.mean(resid, axis=-1, keepdims=True))
    spread = lax.optimization_barrier(jnp.mean(center * center, axis=-1, keepdims=True))
    return center * lax.rsqrt(spread + 1e-06) * gain + shift

def attend(queries, key_rows, value_rows, allowed):
    row_count = queries.shape[0]
    key_count = key_rows.shape[0]
    query_heads = queries.reshape(row_count, HEADS, HEAD_DIM)
    key_heads = key_rows.reshape(key_count, HEADS, HEAD_DIM)
    value_heads = value_rows.reshape(key_count, HEADS, HEAD_DIM)
    scores = jnp.einsum('qhd,khd->hqk', query_heads, key_heads, precision=precise) * HEAD_DIM ** (-0.5)
    scores = low_back(scores)
    scores = jnp.where(allowed[None], scores, -1e+30)
    highest = lax.optimization_barrier(jnp.max(scores, axis=-1, keepdims=True))
    exponent = jnp.exp(scores - highest)
    softmax_w = exponent / lax.optimization_barrier(jnp.sum(exponent, axis=-1, keepdims=True))
    mixed = jnp.einsum('hqk,khd->qhd', low(softmax_w), value_heads, precision=precise)
    return mixed.reshape(row_count, HEADS * HEAD_DIM)

def processing_rows(seq_lengths, seq_rows):
    position = jnp.arange(GROUP, dtype=jnp.int32)
    seq_lengths = seq_lengths.astype(jnp.int32)
    ends = jnp.cumsum(seq_lengths).astype(jnp.int32)
    starts = (ends - seq_lengths).astype(jnp.int32)
    proc_len = seq_lengths[seq_rows]
    proc_end = jnp.cumsum(proc_len).astype(jnp.int32)
    proc_start = (proc_end - proc_len).astype(jnp.int32)
    slot = lax.optimization_barrier(jnp.sum((position[:, None] >= proc_end[None, :]).astype(jnp.int32), axis=1)).astype(jnp.int32)
    seg_proc = seq_rows[slot].astype(jnp.int32)
    order_rows = (starts[seg_proc] + position - proc_start[slot]).astype(jnp.int32)
    return (seg_proc, order_rows)

def group_layer(params, pieces):
    token_rows, memory_rows, seq_lengths, seq_rows, pick_rows = pieces
    self_w, cross_w, first_w, first_b, second_w, second_b, gains, shifts = params
    position = jnp.arange(GROUP, dtype=jnp.int32)
    seg_proc, order_rows = processing_rows(seq_lengths, seq_rows)
    memory_of = pick_rows[seg_proc]
    memory_owner = jnp.arange(NMEM * MEM_LEN, dtype=jnp.int32) // MEM_LEN
    self_query, self_key, self_value, self_out = [self_w[block_index * D:(block_index + 1) * D] for block_index in range(4)]
    cross_query, cross_key, cross_value, cross_out = [cross_w[block_index * D:(block_index + 1) * D] for block_index in range(4)]
    queries = rounded(matmul_full(token_rows, self_query))
    key_rows = rounded(matmul_full(token_rows, self_key))
    value_rows = rounded(matmul_full(token_rows, self_value))
    attended = rounded(attend(queries, key_rows, value_rows, seg_proc[:, None] == seg_proc[None, :]))
    branch_one = low_back(matmul_full(attended, self_out))
    hidden_one = layer_norm(token_rows + branch_one, gains[:, 0], shifts[:, 0])
    cross_queries = rounded(matmul_full(low(hidden_one), cross_query))
    cross_keys = rounded(matmul_full(memory_rows, cross_key))
    cross_values = rounded(matmul_full(memory_rows, cross_value))
    cross_mixed = rounded(attend(cross_queries, cross_keys, cross_values, memory_of[:, None] == memory_owner[None, :]))
    branch_two = low_back(matmul_full(cross_mixed, cross_out))
    hidden_two = layer_norm(hidden_one + branch_two, gains[:, 1], shifts[:, 1])
    pre_act = low_back(matmul_full(low(hidden_two), first_w) + first_b)
    active = low(jax.nn.gelu(pre_act, approximate=True))
    branch_three = low_back(matmul_full(active, second_w) + second_b)
    result = layer_norm(hidden_two + branch_three, gains[:, 2], shifts[:, 2])
    inverse = jnp.zeros((GROUP,), jnp.int32).at[order_rows].set(position)
    return result[inverse]

def reference(tokens, memory, cotangent, lengths, seq_order, memory_pick, self_attn, cross_attn, ffn_in, ffn_in_bias, ffn_out, ffn_out_bias, norm_gain, norm_bias):
    params = tuple((array_in.astype(jnp.float32) for array_in in (self_attn, cross_attn, ffn_in, ffn_in_bias, ffn_out, ffn_out_bias, norm_gain, norm_bias)))
    groups = MICRO * N_DP
    token_f = tokens.astype(jnp.float32).reshape(groups, GROUP, D)
    memory_f = memory.astype(jnp.float32).reshape(groups, NMEM * MEM_LEN, D)
    length_all = lengths.reshape(groups, SEQS)
    order_all = seq_order.reshape(groups, SEQS)
    pick_all = memory_pick.reshape(groups, SEQS)

    def forward(weights, token_in, memory_in):

        def one_group(pieces):
            return group_layer(weights, pieces)
        return lax.map(jax.checkpoint(one_group), (token_in, memory_in, length_all, order_all, pick_all))
    result, pullback = jax.vjp(forward, params, token_f, memory_f)
    weight_grads, token_grad, memory_grad = pullback(cotangent.astype(jnp.float32).reshape(groups, GROUP, D))
    return (result.reshape(MICRO, N_DP * GROUP, D), token_grad.reshape(MICRO, N_DP * GROUP, D), memory_grad.reshape(MICRO, N_DP * NMEM * MEM_LEN, D), weight_grads[0], weight_grads[1], weight_grads[2], weight_grads[3], weight_grads[4], weight_grads[5], weight_grads[6], weight_grads[7])
```

```python
import functools
import math

import jax
import jax.numpy as jnp
from jax import lax
from jax.experimental import pallas as pl
from jax.experimental.pallas import tpu as pltpu
from jax.sharding import PartitionSpec as P

D = 512
HEADS = 8
HEAD_DIM = 64
FF = 2048
MEM_LEN = 1024
SEQS = 4
NMEM = 2
GROUP = 2048
PIECE = 512
PIECES = GROUP // PIECE
QB = 256
KB = 256
NEG = -1e30
BLOCKS = 32
BROWS = D * 4 // BLOCKS
bf16 = jnp.bfloat16
f32 = jnp.float32
VMEM_LIMIT = 58 << 20


def dot(left, right, cl=1, cr=0):
    return lax.dot_general(
        left, right, (((cl,), (cr,)), ((), ())), preferred_element_type=f32
    )


def place_ends(info):
    ends, total = [], 0
    for j in range(SEQS):
        total = total + info[info[SEQS + j]]
        ends.append(total)
    return ends


def place_picks(info):
    return [info[2 * SEQS + info[SEQS + j]] for j in range(SEQS)]


def place_shifts(info, ends):
    shifts = []
    for j in range(SEQS):
        seq = info[SEQS + j]
        start = 0
        for s in range(SEQS):
            start = start + jnp.where(s < seq, info[s], 0)
        shifts.append(start - (ends[j - 1] if j else 0))
    return shifts


def by_place(rows, ends, values):
    out = jnp.full(rows.shape, values[0], jnp.int32)
    for j in range(SEQS - 1):
        out = jnp.where(rows >= ends[j], values[j + 1], out)
    return out


def piece_row(info, k):
    return pl.multiple_of(lax.rem(info[3 * SEQS] - k + PIECES, PIECES) * PIECE, PIECE)


def weight(ref, first, count, offset, rows):
    return ref[first : first + count, offset : offset + rows, :].reshape(count * rows, D)


def square(ref, index, offset=0):
    per = BLOCKS // 4
    return weight(ref, index * per, per, offset, BROWS)


def project_kernel(with_query, info, x0, x1, x2, x3, w, x_out, *outs):
    base = 0
    if with_query:
        qt_out, k_out, v_out = outs
        wq = square(w, 0, base)
    else:
        k_out, v_out = outs
    wk, wv = square(w, 1, base), square(w, 2, base)
    for k, piece in enumerate((x0, x1, x2, x3)):
        r0 = piece_row(info, k)
        rows = pl.ds(r0, PIECE)
        x = piece[...]
        x_out[rows, :] = x
        if with_query:
            q = dot(x, wq).astype(bf16) * jnp.asarray(HEAD_DIM**-0.5, bf16)
            qt_out[:, rows] = q.T
        k_out[rows, :] = dot(x, wk).astype(bf16)
        v_out[rows, :] = dot(x, wv).astype(bf16)


def key_loop(info, cross, q0, tile):
    ends = place_ends(info)
    rows = q0 + lax.broadcasted_iota(jnp.int32, (1, QB), 1)
    if cross:
        picks = place_picks(info)
        picked = by_place(rows, ends, picks)
        for mem in range(NMEM):
            need = jnp.bool_(False)
            for j in range(SEQS):
                start = ends[j - 1] if j else 0
                need = need | ((start < q0 + QB) & (ends[j] > q0) & (picks[j] == mem))
            allowed = picked == mem

            def step(j, carry, mem=mem, allowed=allowed):
                tile(pl.multiple_of(mem * MEM_LEN + j * KB, KB), None, allowed)
                return carry

            lax.fori_loop(0, jnp.where(need, MEM_LEN // KB, 0), step, 0)
    else:
        low, high = 0, GROUP
        low_row = jnp.zeros((1, QB), jnp.int32)
        high_row = jnp.full((1, QB), GROUP, jnp.int32)
        for j in range(SEQS - 1):
            low = jnp.where(q0 >= ends[j], ends[j], low)
            low_row = jnp.where(rows >= ends[j], ends[j], low_row)
        for j in reversed(range(SEQS - 1)):
            high = jnp.where(q0 + QB - 1 < ends[j], ends[j], high)
            high_row = jnp.where(rows < ends[j], ends[j], high_row)

        def step(j, carry):
            k0 = pl.multiple_of(j * KB, KB)
            keys = k0 + lax.broadcasted_iota(jnp.int32, (KB, QB), 0)
            bias = jnp.where((keys >= low_row) & (keys < high_row), 0.0, NEG)
            tile(k0, bias, None)
            return carry

        lax.fori_loop(low // KB, (high + KB - 1) // KB, step, 0)


def head_rows(h):
    return slice(h * HEAD_DIM, (h + 1) * HEAD_DIM)


def attend_kernel(cross, info, qt, k, v, ot, lse, vt, top, total, acc, bias_ref):
    i = pl.program_id(0)

    @pl.when(i == 0)
    def _():
        for c in range(GROUP // QB):
            vt[:, c * QB : (c + 1) * QB] = v[c * QB : (c + 1) * QB, :].T

    top[...] = jnp.full_like(top, NEG)
    total[...] = jnp.zeros_like(total)
    acc[...] = jnp.zeros_like(acc)

    def tile(k0, bias, allowed):
        keys = pl.ds(k0, KB)
        if bias is not None:
            bias_ref[...] = bias
        tops, totals = top[...], total[...]
        new_tops, new_totals = [], []
        group = 8
        for g in range(0, HEADS, group):
            heads = range(g, g + group)
            scores = [dot(k[keys, head_rows(h)], qt[head_rows(h), :]) for h in heads]
            parts = []
            for h, s in zip(heads, scores):
                old = tops[h : h + 1]
                if bias is not None:
                    s = s + bias_ref[...]
                    new = jnp.maximum(old, jnp.max(s, axis=0, keepdims=True))
                    base = new
                else:
                    peak = jnp.maximum(old, jnp.max(s, axis=0, keepdims=True))
                    new = jnp.where(allowed, peak, old)
                    base = jnp.where(allowed, peak, -NEG)
                decay = jnp.exp(old - new)
                p = jnp.exp(s - base)
                new_tops.append(new)
                new_totals.append(totals[h : h + 1] * decay + jnp.sum(p, axis=0, keepdims=True))
                parts.append((decay, p.astype(bf16)))
            for h, (decay, p) in zip(heads, parts):
                acc[head_rows(h), :] = acc[head_rows(h), :] * decay + dot(
                    vt[head_rows(h), keys], p
                )
        top[...] = jnp.concatenate(new_tops, axis=0)
        total[...] = jnp.concatenate(new_totals, axis=0)

    key_loop(info, cross, pl.multiple_of(i * QB, QB), tile)
    lse[...] = top[...] + jnp.log(total[...])
    inverse = 1.0 / total[...]
    for h in range(HEADS):
        ot[head_rows(h), :] = (acc[head_rows(h), :] * inverse[h : h + 1]).astype(bf16)


def attend_back_kernel(
    cross, info, qt, k, v, g, ot, lse, dqt, dk, dv, kt, dqt_acc, dk_acc, dv_acc, gt, gm, qm, bias_ref
):
    i = pl.program_id(0)

    @pl.when(i == 0)
    def _():
        dk_acc[...] = jnp.zeros_like(dk_acc)
        dv_acc[...] = jnp.zeros_like(dv_acc)
        for c in range(GROUP // QB):
            kt[:, c * QB : (c + 1) * QB] = k[c * QB : (c + 1) * QB, :].T

    gt[...] = g[...].T
    left = lax.broadcasted_iota(jnp.int32, (QB, 2 * HEAD_DIM), 1) < HEAD_DIM
    for pair in range(HEADS // 2):
        cols = slice(pair * 2 * HEAD_DIM, (pair + 1) * 2 * HEAD_DIM)
        gp = g[:, cols]
        qp = qt[cols, :].T
        zero = jnp.zeros_like(gp)
        gm[pair, :QB, :] = jnp.where(left, gp, zero)
        gm[pair, QB:, :] = jnp.where(left, zero, gp)
        qm[pair, :QB, :] = jnp.where(left, qp, zero)
        qm[pair, QB:, :] = jnp.where(left, zero, qp)
    weighted = [
        jnp.sum(
            gt[head_rows(h), :].astype(f32) * ot[head_rows(h), :].astype(f32),
            axis=0,
            keepdims=True,
        )
        for h in range(HEADS)
    ]
    dqt_acc[...] = jnp.zeros_like(dqt_acc)

    def tile(k0, bias, allowed):
        keys = pl.ds(k0, KB)
        if bias is not None:
            bias_ref[...] = bias
        lses = lse[...]
        if allowed is not None:
            lses = jnp.where(allowed, lses, -NEG)
        group = 4
        for first in range(0, HEADS, group):
            heads = range(first, first + group)
            scores = [dot(k[keys, head_rows(h)], qt[head_rows(h), :]) for h in heads]
            slopes = [dot(v[keys, head_rows(h)], gt[head_rows(h), :]) for h in heads]
            probs, grads = [], []
            for h, s, dp in zip(heads, scores, slopes):
                if bias is not None:
                    s = s + bias_ref[...]
                p = jnp.exp(s - lses[h : h + 1])
                probs.append(p.astype(bf16))
                grads.append((p * (dp - weighted[h])).astype(bf16))
            for n in range(0, group, 2):
                pair = (first + n) // 2
                cols = slice(pair * 2 * HEAD_DIM, (pair + 1) * 2 * HEAD_DIM)
                dv_acc[keys, cols] += dot(jnp.concatenate(probs[n : n + 2], axis=1), gm[pair])
                dk_acc[keys, cols] += dot(jnp.concatenate(grads[n : n + 2], axis=1), qm[pair])
            for h, ds in zip(heads, grads):
                dqt_acc[head_rows(h), :] += dot(kt[head_rows(h), keys], ds)

    key_loop(info, cross, pl.multiple_of(i * QB, QB), tile)
    dqt[...] = (dqt_acc[...] * HEAD_DIM**-0.5).astype(bf16)

    @pl.when(i == pl.num_programs(0) - 1)
    def _():
        dk[...] = dk_acc[...].astype(bf16)
        dv[...] = dv_acc[...].astype(bf16)


def norm(resid):
    center = resid - jnp.mean(resid, axis=-1, keepdims=True)
    inv = lax.rsqrt(jnp.mean(center * center, axis=-1, keepdims=True) + 1e-06)
    return center * inv, inv


def norm_back(grad, normed, inv, gain):
    scaled = grad * gain
    return inv * (
        scaled
        - jnp.mean(scaled, axis=-1, keepdims=True)
        - normed * jnp.mean(scaled * normed, axis=-1, keepdims=True)
    )


def column_sum(value):
    return jnp.sum(value, axis=0, keepdims=True)


def first_norm_kernel(ot, x, wa, wb, vecs, n1, inv1, qct):
    resid = x[...].astype(f32) + dot(ot[...], square(wa, 3), 0, 0)
    normed, inv = norm(resid)
    n1[...] = normed
    inv1[...] = inv
    hidden = (normed * vecs[0:1, :] + vecs[3:4, :]).astype(bf16)
    q = dot(hidden, square(wb, 0)).astype(bf16) * jnp.asarray(HEAD_DIM**-0.5, bf16)
    qct[...] = q.T


def ffn_kernel(
    info, oct_, n1, wb, vecs, b1, c0, c1, c2, c3,
    yg, d2, gc, g_ffn, g_co, g_b1, g_vec,
    cot, act, slope, dy, gw1, gw2, gco, yacc,
):
    i = pl.program_id(0)

    @pl.when(i == 0)
    def _():
        for k, piece in enumerate((c0, c1, c2, c3)):
            cot[pl.ds(piece_row(info, k), PIECE), :] = piece[...]
        for ref in (gw1, gw2, gco, g_b1, g_vec, yacc):
            ref[...] = jnp.zeros_like(ref)

    first_block = 2 * BROWS
    chunk = BROWS // 4

    def w1(c):
        return weight(wb, 0, BLOCKS, first_block + c * chunk, chunk)

    def w2(c):
        per = BLOCKS // 4
        return weight(wb, c * per, per, BROWS, BROWS)

    hidden_one = n1[...] * vecs[0:1, :] + vecs[3:4, :]
    n2, inv2 = norm(hidden_one + dot(oct_[...], square(wb, 3), 0, 0))
    hidden = n2 * vecs[1:2, :] + vecs[4:5, :]
    hidden_b = hidden.astype(bf16)

    factor = math.sqrt(2.0 / math.pi)
    cubic = 0.044715 * factor
    out = jnp.zeros((PIECE, D), f32)
    for c in range(4):
        cols = slice(c * D, (c + 1) * D)
        u = dot(hidden_b, w1(c)) + b1[0:1, cols]
        sq = u * u
        t = jnp.tanh(u * (factor + cubic * sq))
        half = 0.5 + 0.5 * t
        a = (u * half).astype(bf16)
        act[:, cols] = a
        slope[:, cols] = half + u * (1.0 - t * t) * (0.5 * factor + 1.5 * cubic * sq)
        out = out + dot(a, w2(c))
    n3, inv3 = norm(hidden + (out + vecs[6:7, :]))
    y = (n3 * vecs[2:3, :] + vecs[5:6, :]).astype(bf16)

    ends = place_ends(info)
    shifts = place_shifts(info, ends)
    p0 = i * PIECE
    rows = p0 + lax.broadcasted_iota(jnp.int32, (PIECE, 1), 0)
    given = rows + by_place(rows, ends, shifts)
    dy[...] = jnp.zeros_like(dy)

    def gather(c, carry):
        r0 = pl.multiple_of(c * QB, QB)
        hit = jnp.bool_(False)
        for j in range(SEQS):
            begin = jnp.maximum(ends[j - 1] if j else 0, p0)
            end = jnp.minimum(ends[j], p0 + PIECE)
            hit = hit | (
                (begin < end) & (begin + shifts[j] < r0 + QB) & (end + shifts[j] > r0)
            )

        @pl.when(hit)
        def _():
            cols = r0 + lax.broadcasted_iota(jnp.int32, (PIECE, QB), 1)
            select = jnp.where(cols == given, 1.0, 0.0).astype(bf16)
            dy[...] += dot(select, cot[pl.ds(r0, QB), :])
            yacc[pl.ds(r0, QB), :] += dot(select, y, 0, 0)

        return carry

    lax.fori_loop(0, GROUP // QB, gather, 0)

    grad = dy[...]
    g_vec[2:3, :] += column_sum(grad * n3)
    g_vec[5:6, :] += column_sum(grad)
    d3 = norm_back(grad, n3, inv3, vecs[2:3, :])
    df = d3.astype(bf16)
    g_vec[6:7, :] += column_sum(df.astype(f32))
    back = d3
    for c in range(4):
        cols = slice(c * D, (c + 1) * D)
        a = act[:, cols]
        gw2[cols, :] += dot(a, df, 0, 0)
        du = (dot(df, w2(c), 1, 1) * slope[:, cols]).astype(bf16)
        gw1[c] += dot(hidden_b, du, 0, 0)
        g_b1[0:1, cols] += column_sum(du.astype(f32))
        back = back + dot(du, w1(c), 1, 1)
    g_vec[1:2, :] += column_sum(back * n2)
    g_vec[4:5, :] += column_sum(back)
    second = norm_back(back, n2, inv2, vecs[1:2, :])
    d2[...] = second
    dco = second.astype(bf16)
    gco[...] += dot(oct_[...], dco)
    gc[...] = dot(dco, square(wb, 3), 1, 1).astype(bf16)

    @pl.when(i == pl.num_programs(0) - 1)
    def _():
        keep = info[3 * SEQS + 1] > 0
        yg[...] = yacc[...].astype(bf16)
        g_co[...] = jnp.where(keep, gco[...], 0.0).astype(bf16)
        for c in range(4):
            part = jnp.where(keep, gw1[c], 0.0).astype(bf16)
            g_ffn[:, c * chunk : (c + 1) * chunk, :] = part.reshape(BLOCKS, chunk, D)
            part = jnp.where(keep, gw2[c * D : (c + 1) * D, :], 0.0).astype(bf16)
            per = BLOCKS // 4
            g_ffn[c * per : (c + 1) * per, BROWS:, :] = part.reshape(per, BROWS, D)
        g_b1[...] = jnp.where(keep, g_b1[...], 0.0)
        g_vec[...] = jnp.where(keep, g_vec[...], 0.0)


def cross_post_kernel(
    info, dqct, dkc, dvc, mem, d2, n1, inv1, ot, wa, wb, vecs, g_co,
    dmem, d1, go, g_cross, g_wo, g_vec,
    gcq, gck, gcv, gwo,
):
    i = pl.program_id(0)

    @pl.when(i == 0)
    def _():
        for ref in (gcq, gck, gcv, gwo, g_vec):
            ref[...] = jnp.zeros_like(ref)

    m, dk, dv = mem[...], dkc[...], dvc[...]
    dmem[...] = (dot(dk, square(wb, 1), 1, 1) + dot(dv, square(wb, 2), 1, 1)).astype(bf16)
    gck[...] += dot(m, dk, 0, 0)
    gcv[...] += dot(m, dv, 0, 0)
    normed = n1[...]
    hidden = (normed * vecs[0:1, :] + vecs[3:4, :]).astype(bf16)
    dq = dqct[...].T
    gcq[...] += dot(hidden, dq, 0, 0)
    back = d2[...] + dot(dq, square(wb, 0), 1, 1)
    g_vec[0:1, :] += column_sum(back * normed)
    g_vec[3:4, :] += column_sum(back)
    first = norm_back(back, normed, inv1[...], vecs[0:1, :])
    d1[...] = first
    dao = first.astype(bf16)
    gwo[...] += dot(ot[...], dao)
    go[...] = dot(dao, square(wa, 3), 1, 1).astype(bf16)

    @pl.when(i == pl.num_programs(0) - 1)
    def _():
        keep = info[3 * SEQS + 1] > 0
        for n, ref in enumerate((gcq, gck, gcv)):
            g_cross[n * D : (n + 1) * D, :] = jnp.where(keep, ref[...], 0.0).astype(bf16)
        g_cross[3 * D :, :] = g_co[...]
        g_wo[...] = jnp.where(keep, gwo[...], 0.0).astype(bf16)
        g_vec[...] = jnp.where(keep, g_vec[...], 0.0)


def self_post_kernel(
    info, dqt, dk_ref, dv_ref, x_ref, d1, wa, g_wo, dtok, g_self, gq, gk, gv
):
    i = pl.program_id(0)

    @pl.when(i == 0)
    def _():
        for ref in (gq, gk, gv):
            ref[...] = jnp.zeros_like(ref)

    x, dk, dv = x_ref[...], dk_ref[...], dv_ref[...]
    dq = dqt[...].T
    dtok[...] = (
        d1[...]
        + dot(dq, square(wa, 0), 1, 1)
        + dot(dk, square(wa, 1), 1, 1)
        + dot(dv, square(wa, 2), 1, 1)
    ).astype(bf16)
    gq[...] += dot(x, dq, 0, 0)
    gk[...] += dot(x, dk, 0, 0)
    gv[...] += dot(x, dv, 0, 0)

    @pl.when(i == pl.num_programs(0) - 1)
    def _():
        keep = info[3 * SEQS + 1] > 0
        for n, ref in enumerate((gq, gk, gv)):
            g_self[n * D : (n + 1) * D, :] = jnp.where(keep, ref[...], 0.0).astype(bf16)
        g_self[3 * D :, :] = g_wo[...]


SMEM = pl.BlockSpec(memory_space=pltpu.SMEM)
WHOLE = pl.BlockSpec(memory_space=pltpu.VMEM)
ROWS = pl.BlockSpec((PIECE, D), lambda i: (i, 0))
COLS = pl.BlockSpec((D, PIECE), lambda i: (0, i))
ROWS_Q = pl.BlockSpec((QB, D), lambda i: (i, 0))
COLS_Q = pl.BlockSpec((D, QB), lambda i: (0, i))
HEADS_Q = pl.BlockSpec((HEADS, QB), lambda i: (0, i))
ONES = pl.BlockSpec((PIECE, 1), lambda i: (i, 0))


def fixed(*shape):
    return pl.BlockSpec(shape, lambda i: (0,) * len(shape))


def shape(dims, dtype=bf16):
    return jax.ShapeDtypeStruct(dims, dtype)


def call(kernel, name, grid, in_specs, out_specs, out_shape, scratch, flops, *args):
    return pl.pallas_call(
        kernel,
        grid=grid,
        in_specs=in_specs,
        out_specs=out_specs,
        out_shape=out_shape,
        scratch_shapes=scratch,
        name=name,
        compiler_params=pltpu.CompilerParams(vmem_limit_bytes=VMEM_LIMIT),
        cost_estimate=pl.CostEstimate(flops=flops, bytes_accessed=8 << 20, transcendentals=0),
    )(*args)


ROWMAJOR = shape((GROUP, D))
COLMAJOR = shape((D, GROUP))


def project_rows(info, pieces, w, with_query):
    outs = [ROWMAJOR] + ([COLMAJOR] if with_query else []) + [ROWMAJOR, ROWMAJOR]
    return call(
        functools.partial(project_kernel, with_query),
        "project",
        (),
        [SMEM] + [WHOLE] * 5,
        [WHOLE] * len(outs),
        outs,
        [],
        4 << 30,
        info,
        *pieces,
        w,
    )


def attend(info, qt, k, v, cross):
    return call(
        functools.partial(attend_kernel, cross),
        "attend",
        (GROUP // QB,),
        [SMEM, COLS_Q, fixed(GROUP, D), fixed(GROUP, D)],
        [COLS_Q, HEADS_Q],
        [COLMAJOR, shape((HEADS, GROUP), f32)],
        [
            pltpu.VMEM((D, GROUP), bf16),
            pltpu.VMEM((HEADS, QB), f32),
            pltpu.VMEM((HEADS, QB), f32),
            pltpu.VMEM((D, QB), f32),
            pltpu.VMEM((KB, QB), f32),
        ],
        30 << 30,
        info,
        qt,
        k,
        v,
    )


def attend_back(info, qt, k, v, g, ot, lse, cross):
    return call(
        functools.partial(attend_back_kernel, cross),
        "attend_back",
        (GROUP // QB,),
        [SMEM, COLS_Q, fixed(GROUP, D), fixed(GROUP, D), ROWS_Q, COLS_Q, HEADS_Q],
        [COLS_Q, fixed(GROUP, D), fixed(GROUP, D)],
        [COLMAJOR, ROWMAJOR, ROWMAJOR],
        [
            pltpu.VMEM((D, GROUP), bf16),
            pltpu.VMEM((D, QB), f32),
            pltpu.VMEM((GROUP, D), f32),
            pltpu.VMEM((GROUP, D), f32),
            pltpu.VMEM((D, QB), bf16),
            pltpu.VMEM((HEADS // 2, 2 * QB, 2 * HEAD_DIM), bf16),
            pltpu.VMEM((HEADS // 2, 2 * QB, 2 * HEAD_DIM), bf16),
            pltpu.VMEM((KB, QB), f32),
        ],
        60 << 30,
        info,
        qt,
        k,
        v,
        g,
        ot,
        lse,
    )


def local(
    tokens, memory, cotangent, lengths, seq_order, memory_pick,
    self_attn, cross_attn, ffn_in, ffn_in_bias, ffn_out, ffn_out_bias, norm_gain, norm_bias,
):
    axes = ("dp", "fsdp")
    n_dp, members = lax.axis_size("dp"), lax.axis_size("fsdp")
    micro = tokens.shape[0]
    owners = n_dp * members
    dp, z = lax.axis_index("dp"), lax.axis_index("fsdp")

    def offset(d):
        return d % 2 if micro < members else 0

    def unit_at(d, member):
        return member - offset(d)

    mine = unit_at(dp, z)
    valid = (mine >= 0) & (mine < micro)
    unit = jnp.clip(mine, 0, micro - 1)

    def pairs(k, into):
        out = []
        for d in range(n_dp):
            for source in range(members):
                target = (source + k) % members
                if 0 <= unit_at(d, target if into else source) < micro:
                    out.append((d * members + source, d * members + target))
        return out

    def to_unit(array):
        pieces = [lax.dynamic_index_in_dim(array, unit, 0, False)]
        for k in range(1, members):
            target = jnp.clip(unit_at(dp, lax.rem(z + k, members)), 0, micro - 1)
            part = lax.dynamic_index_in_dim(array, target, 0, False)
            pieces.append(lax.ppermute(part, axes, pairs(k, True)))
        return pieces

    def from_unit(array):
        blocks = array.reshape(members, PIECE, D)
        pieces = [lax.dynamic_index_in_dim(blocks, z, 0, False)]
        for k in range(1, members):
            part = lax.dynamic_index_in_dim(blocks, lax.rem(z + k, members), 0, False)
            pieces.append(lax.ppermute(part, axes, pairs(k, False)))
        out = []
        for b in range(micro):
            shift = lax.rem(z - offset(dp) - b + 2 * members, members)
            value = pieces[0]
            for k in range(1, members):
                value = jnp.where(shift == k, pieces[k], value)
            out.append(value.astype(f32))
        return jnp.stack(out)

    def row_of(array):
        return lax.dynamic_index_in_dim(array, unit, 0, False)[0]

    info = jnp.concatenate(
        [
            row_of(lengths),
            row_of(seq_order),
            row_of(memory_pick),
            jnp.stack([z, valid.astype(jnp.int32)]),
        ]
    ).astype(jnp.int32)

    smalls = jnp.concatenate(
        [ffn_in_bias, ffn_out_bias, norm_gain.T.reshape(-1), norm_bias.T.reshape(-1)]
    )
    rows = self_attn.shape[0]
    in_rows = ffn_in.shape[0]
    n_smalls = smalls.shape[0]
    small_row = jnp.pad(smalls, (0, 16 * D - n_smalls)).reshape(16, D)
    bundle_a = jnp.concatenate([self_attn, small_row], axis=0)
    in_blocks = ffn_in.reshape(in_rows, 4, D).transpose(1, 0, 2).reshape(4 * in_rows, D)
    bundle_b = jnp.concatenate([cross_attn, ffn_out, in_blocks], axis=0)
    all_a = lax.all_gather(bundle_a, axes, axis=0, tiled=False)
    token_pieces = to_unit(tokens)
    all_b = lax.all_gather(bundle_b, axes, axis=0, tiled=False)
    memory_pieces = to_unit(memory)
    cotangent_pieces = to_unit(cotangent)

    def blocked(array, count):
        return array.reshape(BLOCKS, count, D)

    small = all_a[:, rows, :n_smalls].astype(f32)
    wa = blocked(all_a[:, :rows], BROWS)
    if owners == BLOCKS:
        wb = all_b
    else:
        first = all_b[:, 2 * rows :].reshape(owners, 4, in_rows, D).transpose(1, 0, 2, 3)
        first = first.reshape(4, BLOCKS, BROWS // 4, D).transpose(1, 0, 2, 3)
        wb = jnp.concatenate(
            [
                blocked(all_b[:, :rows], BROWS),
                blocked(all_b[:, rows : 2 * rows], BROWS),
                blocked(first, BROWS),
            ],
            axis=1,
        )
    out_rows = D // owners
    b1 = small[:, :rows].reshape(1, FF)
    at = rows + out_rows
    vec_rows = [small[:, at + n * out_rows : at + (n + 1) * out_rows].reshape(1, D) for n in range(6)]
    vecs = jnp.concatenate(
        vec_rows + [small[:, rows:at].reshape(1, D), jnp.zeros((1, D), f32)], axis=0
    )

    x, qt, k, v = project_rows(info, token_pieces, wa, True)
    ot, lse = attend(info, qt, k, v, False)
    n1, inv1, qct = call(
        first_norm_kernel,
        "first_norm",
        (PIECES,),
        [COLS, ROWS, fixed(BLOCKS, BROWS, D), fixed(BLOCKS, 3 * BROWS, D), fixed(8, D)],
        [ROWS, ONES, COLS],
        [shape((GROUP, D), f32), shape((GROUP, 1), f32), COLMAJOR],
        [],
        2 << 30,
        ot,
        x,
        wa,
        wb,
        vecs,
    )
    mem, kc, vc = project_rows(info, memory_pieces, wb, False)
    oct_, lse_c = attend(info, qct, kc, vc, True)
    yg, d2, gc, g_ffn, g_co, g_b1, g_vec = call(
        ffn_kernel,
        "ffn",
        (PIECES,),
        [SMEM, COLS, ROWS, fixed(BLOCKS, 3 * BROWS, D), fixed(8, D), fixed(1, FF)]
        + [fixed(PIECE, D)] * 4,
        [
            fixed(GROUP, D),
            ROWS,
            ROWS,
            fixed(BLOCKS, 2 * BROWS, D),
            fixed(D, D),
            fixed(1, FF),
            fixed(8, D),
        ],
        [
            ROWMAJOR,
            shape((GROUP, D), f32),
            ROWMAJOR,
            shape((BLOCKS, 2 * BROWS, D)),
            shape((D, D)),
            shape((1, FF), f32),
            shape((8, D), f32),
        ],
        [
            pltpu.VMEM((GROUP, D), bf16),
            pltpu.VMEM((PIECE, FF), bf16),
            pltpu.VMEM((PIECE, FF), f32),
            pltpu.VMEM((PIECE, D), f32),
            pltpu.VMEM((4, D, D), f32),
            pltpu.VMEM((FF, D), f32),
            pltpu.VMEM((D, D), f32),
            pltpu.VMEM((GROUP, D), f32),
        ],
        32 << 30,
        info,
        oct_,
        n1,
        wb,
        vecs,
        b1,
        *cotangent_pieces,
    )
    layer_output = from_unit(yg)

    def owned(array, count):
        return lax.psum_scatter(array, axes, scatter_dimension=0, tiled=True).astype(f32)

    if owners == BLOCKS:
        ffn_part = owned(g_ffn, 0)[0]
    else:
        second = g_ffn[:, BROWS:].reshape(owners, rows, D)
        first = g_ffn[:, :BROWS].reshape(BLOCKS, 4, BROWS // 4, D).transpose(1, 0, 2, 3)
        first = first.reshape(4, owners, in_rows, D).transpose(1, 0, 2, 3)
        both = jnp.concatenate([first.reshape(owners, rows, D), second], axis=1)
        ffn_part = owned(both, 0)[0]
    ffn_in_grad = ffn_part[:rows].reshape(4, in_rows, D).transpose(1, 0, 2).reshape(in_rows, FF)
    ffn_out_grad = ffn_part[rows:]

    dqct, dkc, dvc = attend_back(info, qct, kc, vc, gc, oct_, lse_c, True)
    dmem, d1, go, g_cross, g_wo, g_vec_one = call(
        cross_post_kernel,
        "cross_post",
        (PIECES,),
        [SMEM, COLS, ROWS, ROWS, ROWS, ROWS, ROWS, ONES, COLS]
        + [fixed(BLOCKS, BROWS, D), fixed(BLOCKS, 3 * BROWS, D), fixed(8, D), fixed(D, D)],
        [ROWS, ROWS, ROWS, fixed(4 * D, D), fixed(D, D), fixed(8, D)],
        [
            ROWMAJOR,
            shape((GROUP, D), f32),
            ROWMAJOR,
            shape((4 * D, D)),
            shape((D, D)),
            shape((8, D), f32),
        ],
        [pltpu.VMEM((D, D), f32)] * 4,
        9 << 30,
        info,
        dqct,
        dkc,
        dvc,
        mem,
        d2,
        n1,
        inv1,
        ot,
        wa,
        wb,
        vecs,
        g_co,
    )
    memory_grad = from_unit(dmem)
    cross_attn_grad = owned(g_cross, 0)
    dqt, dk, dv = attend_back(info, qt, k, v, go, ot, lse, False)
    dtok, g_self = call(
        self_post_kernel,
        "self_post",
        (PIECES,),
        [SMEM, COLS, ROWS, ROWS, ROWS, ROWS, fixed(BLOCKS, BROWS, D), fixed(D, D)],
        [ROWS, fixed(4 * D, D)],
        [ROWMAJOR, shape((4 * D, D))],
        [pltpu.VMEM((D, D), f32)] * 3,
        7 << 30,
        info,
        dqt,
        dk,
        dv,
        x,
        d1,
        wa,
        g_wo,
    )
    input_grad = from_unit(dtok)
    g_vec = g_vec + g_vec_one
    small_grads = jnp.concatenate(
        [g_b1.reshape(owners, rows), g_vec[6].reshape(owners, out_rows)]
        + [g_vec[n].reshape(owners, out_rows) for n in range(6)],
        axis=1,
    )
    small_grads = jnp.pad(small_grads, ((0, 0), (0, 16 * D - n_smalls))).reshape(owners, 16, D)
    last = jnp.concatenate(
        [g_self.reshape(owners, rows, D), small_grads.astype(bf16)], axis=1
    )
    last = owned(last, 0)[0]
    small_out = last[rows]
    norm_part = small_out[at : at + 6 * out_rows].reshape(6, out_rows)
    return (
        layer_output,
        input_grad,
        memory_grad,
        last[:rows],
        cross_attn_grad,
        ffn_in_grad,
        small_out[:rows],
        ffn_out_grad,
        small_out[rows:at],
        norm_part[:3].T,
        norm_part[3:].T,
    )


def solution(mesh):
    rows = P(None, ("dp", "fsdp"), None)
    group = P(None, "dp", None)
    shard = P(("dp", "fsdp"), None)
    flat = P(("dp", "fsdp"))
    in_specs = (rows,) * 3 + (group,) * 3 + (shard, shard, shard, flat, shard, flat, shard, shard)
    out_specs = (rows,) * 3 + (shard, shard, shard, flat, shard, flat, shard, shard)
    return jax.shard_map(local, mesh=mesh, in_specs=in_specs, out_specs=out_specs, check_vma=False)
```

```python
import functools
import math

import jax
import jax.numpy as jnp
from jax import lax
from jax.experimental import pallas as pl
from jax.experimental.pallas import tpu as pltpu
from jax.sharding import PartitionSpec as P

D = 512
HEADS = 8
HEAD_DIM = 64
FF = 2048
MEM_LEN = 1024
SEQS = 4
NMEM = 2
GROUP = 2048
PIECE = 512
PIECES = GROUP // PIECE
QB = 256
KB = 512
FR = 512
LANES = 128
NEG = -1e30
BLOCKS = 32
BROWS = D * 4 // BLOCKS
bf16 = jnp.bfloat16
f32 = jnp.float32
VMEM_LIMIT = 58 << 20
CORE = 3 * SEQS + 2
HALF = BLOCKS // 2
SMALL = 16


def dot(left, right, cl=1, cr=0):
    return lax.dot_general(
        left, right, (((cl,), (cr,)), ((), ())), preferred_element_type=f32
    )


def place_ends(info):
    ends, total = [], 0
    for j in range(SEQS):
        total = total + info[info[SEQS + j]]
        ends.append(total)
    return ends


def place_picks(info):
    return [info[2 * SEQS + info[SEQS + j]] for j in range(SEQS)]


def place_shifts(info, ends):
    shifts = []
    for j in range(SEQS):
        seq = info[SEQS + j]
        start = 0
        for s in range(SEQS):
            start = start + jnp.where(s < seq, info[s], 0)
        shifts.append(start - (ends[j - 1] if j else 0))
    return shifts


def by_place(rows, ends, values):
    out = jnp.full(rows.shape, values[0], jnp.int32)
    for j in range(SEQS - 1):
        out = jnp.where(rows >= ends[j], values[j + 1], out)
    return out


def piece_row(info, k):
    return pl.multiple_of(lax.rem(info[3 * SEQS] - k + PIECES, PIECES) * PIECE, PIECE)


def shift_row(info, k):
    return pl.multiple_of(lax.rem(info[3 * SEQS] + k, PIECES) * PIECE, PIECE)


def weight(ref, first, count, offset, rows):
    return ref[first : first + count, offset : offset + rows, :].reshape(count * rows, D)


def square(ref, index, offset=0):
    per = BLOCKS // 4
    return weight(ref, index * per, per, offset, BROWS)


def project_kernel(with_query, info, x0, x1, x2, x3, w, x_out, *outs):
    base = 0
    if with_query:
        qt_out, k_out, v_out = outs
        wq = square(w, 0, base)
    else:
        k_out, v_out = outs
    wk, wv = square(w, 1, base), square(w, 2, base)
    for k, piece in enumerate((x0, x1, x2, x3)):
        r0 = piece_row(info, k)
        rows = pl.ds(r0, PIECE)
        x = piece[...]
        x_out[rows, :] = x
        if with_query:
            q = dot(x, wq).astype(bf16) * jnp.asarray(HEAD_DIM**-0.5, bf16)
            qt_out[:, rows] = q.T
        k_out[rows, :] = dot(x, wk).astype(bf16)
        v_out[rows, :] = dot(x, wv).astype(bf16)


def key_loop(info, cross, q0, tile):
    ends = place_ends(info)
    rows = q0 + lax.broadcasted_iota(jnp.int32, (1, QB), 1)
    if cross:
        picks = place_picks(info)
        picked = by_place(rows, ends, picks)
        for mem in range(NMEM):
            need = jnp.bool_(False)
            for j in range(SEQS):
                start = ends[j - 1] if j else 0
                need = need | ((start < q0 + QB) & (ends[j] > q0) & (picks[j] == mem))

            @pl.when(need)
            def _():
                tile(mem * MEM_LEN, MEM_LEN, None, picked == mem)
    else:
        low, high = 0, GROUP
        low_row = jnp.zeros((1, QB), jnp.int32)
        high_row = jnp.full((1, QB), GROUP, jnp.int32)
        for j in range(SEQS - 1):
            low = jnp.where(q0 >= ends[j], ends[j], low)
            low_row = jnp.where(rows >= ends[j], ends[j], low_row)
        for j in reversed(range(SEQS - 1)):
            high = jnp.where(q0 + QB - 1 < ends[j], ends[j], high)
            high_row = jnp.where(rows < ends[j], ends[j], high_row)
        low = low // LANES * LANES
        many = (high - low) // KB
        rest = high - low - many * KB
        many = jnp.where(rest > KB // 2, many + 1, many)

        def part(first, size):
            k0 = pl.multiple_of(jnp.minimum(first, GROUP - size), LANES)
            keys = k0 + lax.broadcasted_iota(jnp.int32, (size, QB), 0)
            inside = (keys >= jnp.maximum(low_row, first)) & (keys < high_row)
            tile(k0, size, jnp.where(inside, 0.0, NEG), None)

        def step(j, carry):
            part(low + j * KB, KB)
            return carry

        lax.fori_loop(0, many, step, 0)

        @pl.when((rest > 0) & (rest <= KB // 2))
        def _():
            part(low + many * KB, KB // 2)


def head_rows(h):
    return slice(h * HEAD_DIM, (h + 1) * HEAD_DIM)


def pipelined(groups, *stages):
    for step in range(groups + len(stages) - 1):
        for lag, stage in enumerate(stages):
            if 0 <= step - lag < groups:
                stage(step - lag)


def attend_kernel(cross, info, qt, k, v, ot, lse, vt, top, total, acc, bias_ref):
    i = pl.program_id(0)
    q0 = pl.multiple_of(i * QB, QB)
    group = 2

    @pl.when(i == 0)
    def _():
        for c in range(GROUP // QB):
            vt[:, c * QB : (c + 1) * QB] = v[c * QB : (c + 1) * QB, :].T

    def sweep(safe):
        if safe:
            top[...] = jnp.full_like(top, NEG)
        total[...] = jnp.zeros_like(total)
        acc[...] = jnp.zeros_like(acc)

        def tile(k0, size, bias, allowed):
            keys = pl.ds(k0, size)
            if bias is not None:
                bias_ref[:size, :] = bias
            totals = total[...]
            tops = top[...] if safe else None
            new_tops, new_totals = [], []
            scores, parts = {}, {}

            def score(g):
                heads = range(g * group, (g + 1) * group)
                scores[g] = [dot(k[keys, head_rows(h)], qt[head_rows(h), :]) for h in heads]

            def soften(g):
                parts[g] = []
                for n, s in enumerate(scores.pop(g)):
                    h = g * group + n
                    decay = None
                    if bias is not None:
                        s = s + bias_ref[:size, :]
                    if safe:
                        old = tops[h : h + 1]
                        new = jnp.maximum(old, jnp.max(s, axis=0, keepdims=True))
                        if allowed is not None:
                            new = jnp.where(allowed, new, old)
                        decay = jnp.exp(old - new)
                        new_tops.append(new)
                        s = s - new
                    p = jnp.exp(s)
                    if safe and allowed is not None:
                        p = jnp.where(allowed, p, 0.0)
                    part = jnp.sum(p, axis=0, keepdims=True)
                    if allowed is not None:
                        part = jnp.where(allowed, part, 0.0)
                    before = totals[h : h + 1]
                    new_totals.append((before * decay if safe else before) + part)
                    parts[g].append((decay, p.astype(bf16)))

            def mix(g):
                for n, (decay, p) in enumerate(parts.pop(g)):
                    rows = head_rows(g * group + n)
                    part = dot(vt[rows, keys], p)
                    if allowed is not None:
                        part = jnp.where(allowed, part, 0.0)
                    before = acc[rows, :]
                    acc[rows, :] = (before * decay if safe else before) + part

            pipelined(HEADS // group, score, soften, mix)
            if safe:
                top[...] = jnp.concatenate(new_tops, axis=0)
            total[...] = jnp.concatenate(new_totals, axis=0)

        key_loop(info, cross, q0, tile)
        sums = total[...]
        inverse = 1.0 / sums
        lse[...] = jnp.log(sums) + (top[...] if safe else 0.0)
        for h in range(HEADS):
            ot[head_rows(h), :] = (acc[head_rows(h), :] * inverse[h : h + 1]).astype(bf16)

    sweep(False)
    sums = total[...]
    safe_range = (jnp.min(sums) > 1e-18) & (jnp.max(sums) < 1e18)

    @pl.when(jnp.logical_not(safe_range))
    def _():
        sweep(True)


def attend_back_kernel(
    cross, info, qt, k, v, g, ot, lse, dqt, dk, dv, kt, dqt_acc, dk_acc, dv_acc, gt, gm, qm, bias_ref
):
    i = pl.program_id(0)

    @pl.when(i == 0)
    def _():
        dk_acc[...] = jnp.zeros_like(dk_acc)
        dv_acc[...] = jnp.zeros_like(dv_acc)
        for c in range(GROUP // QB):
            kt[:, c * QB : (c + 1) * QB] = k[c * QB : (c + 1) * QB, :].T

    gt[...] = g[...].T
    left = lax.broadcasted_iota(jnp.int32, (QB, 2 * HEAD_DIM), 1) < HEAD_DIM
    for pair in range(HEADS // 2):
        cols = slice(pair * 2 * HEAD_DIM, (pair + 1) * 2 * HEAD_DIM)
        gp = g[:, cols]
        qp = qt[cols, :].T
        zero = jnp.zeros_like(gp)
        gm[pair, :QB, :] = jnp.where(left, gp, zero)
        gm[pair, QB:, :] = jnp.where(left, zero, gp)
        qm[pair, :QB, :] = jnp.where(left, qp, zero)
        qm[pair, QB:, :] = jnp.where(left, zero, qp)
    weighted = [
        jnp.sum(
            gt[head_rows(h), :].astype(f32) * ot[head_rows(h), :].astype(f32),
            axis=0,
            keepdims=True,
        )
        for h in range(HEADS)
    ]
    dqt_acc[...] = jnp.zeros_like(dqt_acc)

    def tile(k0, size, bias, allowed):
        keys = pl.ds(k0, size)
        if bias is not None:
            bias_ref[:size, :] = bias
        lses = lse[...]
        if allowed is not None:
            lses = jnp.where(allowed, lses, -NEG)
        group = 2
        scores, slopes, probs, grads = {}, {}, {}, {}

        def score(g):
            heads = range(g * group, (g + 1) * group)
            scores[g] = [dot(k[keys, head_rows(h)], qt[head_rows(h), :]) for h in heads]
            slopes[g] = [dot(v[keys, head_rows(h)], gt[head_rows(h), :]) for h in heads]

        def soften(g):
            probs[g], grads[g] = [], []
            for n, (s, dp) in enumerate(zip(scores.pop(g), slopes.pop(g))):
                h = g * group + n
                if bias is not None:
                    s = s + bias_ref[:size, :]
                p = jnp.exp(s - lses[h : h + 1])
                probs[g].append(p.astype(bf16))
                grads[g].append((p * (dp - weighted[h])).astype(bf16))

        def mix(g):
            for n in range(0, group, 2):
                pair = (g * group + n) // 2
                cols = slice(pair * 2 * HEAD_DIM, (pair + 1) * 2 * HEAD_DIM)
                dv_acc[keys, cols] += dot(jnp.concatenate(probs[g][n : n + 2], axis=1), gm[pair])
                dk_acc[keys, cols] += dot(jnp.concatenate(grads[g][n : n + 2], axis=1), qm[pair])
            for n, ds in enumerate(grads[g]):
                rows = head_rows(g * group + n)
                dqt_acc[rows, :] += dot(kt[rows, keys], ds)

        pipelined(HEADS // group, score, soften, mix)

    key_loop(info, cross, pl.multiple_of(i * QB, QB), tile)
    dqt[...] = (dqt_acc[...] * HEAD_DIM**-0.5).astype(bf16)

    @pl.when(i == pl.num_programs(0) - 1)
    def _():
        dk[...] = dk_acc[...].astype(bf16)
        dv[...] = dv_acc[...].astype(bf16)


def norm(resid):
    center = resid - jnp.mean(resid, axis=-1, keepdims=True)
    inv = lax.rsqrt(jnp.mean(center * center, axis=-1, keepdims=True) + 1e-06)
    return center * inv, inv


def norm_back(grad, normed, inv, gain):
    scaled = grad * gain
    return inv * (
        scaled
        - jnp.mean(scaled, axis=-1, keepdims=True)
        - normed * jnp.mean(scaled * normed, axis=-1, keepdims=True)
    )


def column_sum(value):
    return jnp.sum(value, axis=0, keepdims=True)


def first_norm_kernel(ot, x, wa, wb, vecs, n1, inv1, qct):
    resid = x[...].astype(f32) + dot(ot[...], square(wa, 3), 0, 0)
    normed, inv = norm(resid)
    n1[...] = normed
    inv1[...] = inv
    hidden = (normed * vecs[0:1, :] + vecs[3:4, :]).astype(bf16)
    q = dot(hidden, square(wb, 0)).astype(bf16) * jnp.asarray(HEAD_DIM**-0.5, bf16)
    qct[...] = q.T


def ffn_kernel(
    info, oct_, n1, wb, vecs, b1, c0, c1, c2, c3,
    y0, y1, y2, y3, d2, gc, keep_ffn, send_ffn, g_co, g_b1, g_vec,
    cot, act, slope, dy, gw1, gw2, gco, yacc,
):
    i = pl.program_id(0)

    @pl.when(i == 0)
    def _():
        for k, piece in enumerate((c0, c1, c2, c3)):
            cot[pl.ds(piece_row(info, k), PIECE), :] = piece[...]
        for ref in (gw1, gw2, gco, g_b1, g_vec, yacc):
            ref[...] = jnp.zeros_like(ref)

    first_block = 2 * BROWS
    chunk = BROWS // 4

    def w1(c):
        return weight(wb, 0, BLOCKS, first_block + c * chunk, chunk)

    def w2(c):
        per = BLOCKS // 4
        return weight(wb, c * per, per, BROWS, BROWS)

    hidden_one = n1[...] * vecs[0:1, :] + vecs[3:4, :]
    n2, inv2 = norm(hidden_one + dot(oct_[...], square(wb, 3), 0, 0))
    hidden = n2 * vecs[1:2, :] + vecs[4:5, :]
    hidden_b = hidden.astype(bf16)

    factor = math.sqrt(2.0 / math.pi)
    cubic = 0.044715 * factor
    ups, acts, outs = {}, {}, []

    def cols(c):
        return slice(c * D, (c + 1) * D)

    def up(c):
        ups[c] = dot(hidden_b, w1(c))

    def bend(c):
        u = ups.pop(c) + b1[0:1, cols(c)]
        sq = u * u
        t = jnp.tanh(u * (factor + cubic * sq))
        half = 0.5 + 0.5 * t
        acts[c] = (u * half).astype(bf16)
        act[:, cols(c)] = acts[c]
        slope[:, cols(c)] = half + u * (1.0 - t * t) * (0.5 * factor + 1.5 * cubic * sq)

    def down(c):
        outs.append(dot(acts.pop(c), w2(c)))

    pipelined(4, up, bend, down)
    out = (outs[0] + outs[1]) + (outs[2] + outs[3])
    n3, inv3 = norm(hidden + (out + vecs[6:7, :]))
    y = (n3 * vecs[2:3, :] + vecs[5:6, :]).astype(bf16)

    ends = place_ends(info)
    shifts = place_shifts(info, ends)
    p0 = i * FR
    rows = p0 + lax.broadcasted_iota(jnp.int32, (FR, 1), 0)
    given = rows + by_place(rows, ends, shifts)
    dy[...] = jnp.zeros_like(dy)

    def gather(c, carry):
        r0 = pl.multiple_of(c * QB, QB)
        hit = jnp.bool_(False)
        for j in range(SEQS):
            begin = jnp.maximum(ends[j - 1] if j else 0, p0)
            end = jnp.minimum(ends[j], p0 + FR)
            hit = hit | (
                (begin < end) & (begin + shifts[j] < r0 + QB) & (end + shifts[j] > r0)
            )

        @pl.when(hit)
        def _():
            cols = r0 + lax.broadcasted_iota(jnp.int32, (FR, QB), 1)
            select = jnp.where(cols == given, 1.0, 0.0).astype(bf16)
            dy[...] += dot(select, cot[pl.ds(r0, QB), :])
            yacc[pl.ds(r0, QB), :] += dot(select, y, 0, 0)

        return carry

    lax.fori_loop(0, GROUP // QB, gather, 0)

    grad = dy[...]
    g_vec[2:3, :] += column_sum(grad * n3)
    g_vec[5:6, :] += column_sum(grad)
    d3 = norm_back(grad, n3, inv3, vecs[2:3, :])
    df = d3.astype(bf16)
    g_vec[6:7, :] += column_sum(df.astype(f32))
    downs, dus, backs = {}, {}, [d3]

    def down_back(c):
        downs[c] = dot(df, w2(c), 1, 1)
        gw2[cols(c), :] += dot(act[:, cols(c)], df, 0, 0)

    def bend_back(c):
        dus[c] = (downs.pop(c) * slope[:, cols(c)]).astype(bf16)
        g_b1[0:1, cols(c)] += column_sum(dus[c].astype(f32))

    def up_back(c):
        du = dus.pop(c)
        gw1[c] += dot(hidden_b, du, 0, 0)
        backs.append(dot(du, w1(c), 1, 1))

    pipelined(4, down_back, bend_back, up_back)
    back = ((backs[0] + backs[1]) + (backs[2] + backs[3])) + backs[4]
    g_vec[1:2, :] += column_sum(back * n2)
    g_vec[4:5, :] += column_sum(back)
    second = norm_back(back, n2, inv2, vecs[1:2, :])
    d2[...] = second
    dco = second.astype(bf16)
    gco[...] += dot(oct_[...], dco)
    gc[...] = dot(dco, square(wb, 3), 1, 1).astype(bf16)

    @pl.when(i == pl.num_programs(0) - 1)
    def _():
        keep = info[3 * SEQS + 1] > 0
        for k, ref in enumerate((y0, y1, y2, y3)):
            ref[...] = yacc[pl.ds(shift_row(info, k), PIECE), :].astype(bf16)
        g_co[...] = jnp.where(keep, gco[...], 0.0).astype(bf16)
        for ref, core in ((keep_ffn, info[CORE]), (send_ffn, 1 - info[CORE])):
            for n in range(4):
                blocks = slice(4 * n, 4 * n + 4)
                for c in range(4):
                    r0 = pl.multiple_of((2 * n + core) * 4 * chunk, 4 * chunk)
                    part = jnp.where(keep, gw1[c, pl.ds(r0, 4 * chunk), :], 0.0).astype(bf16)
                    ref[blocks, c * chunk : (c + 1) * chunk, :] = part.reshape(4, chunk, D)
                r0 = pl.multiple_of((2 * n + core) * 4 * BROWS, 4 * BROWS)
                part = jnp.where(keep, gw2[pl.ds(r0, 4 * BROWS), :], 0.0).astype(bf16)
                ref[blocks, BROWS:, :] = part.reshape(4, BROWS, D)
        g_b1[...] = jnp.where(keep, g_b1[...], 0.0)
        g_vec[...] = jnp.where(keep, g_vec[...], 0.0)


def store_shifted(info, i, refs, value):
    shift = lax.rem(i - info[3 * SEQS] + PIECES, PIECES)
    for k, ref in enumerate(refs):

        @pl.when(shift == k)
        def _():
            ref[...] = value


def cross_post_kernel(
    info, dqct, dkc, dvc, mem, d2, n1, inv1, ot, wa, wb, vecs, g_co,
    m0, m1, m2, m3, d1, go, g_cross, g_wo, g_vec,
    gcq, gck, gcv, gwo,
):
    i = pl.program_id(0)

    @pl.when(i == 0)
    def _():
        for ref in (gcq, gck, gcv, gwo, g_vec):
            ref[...] = jnp.zeros_like(ref)

    m, dk, dv = mem[...], dkc[...], dvc[...]
    dmem = (dot(dk, square(wb, 1), 1, 1) + dot(dv, square(wb, 2), 1, 1)).astype(bf16)
    store_shifted(info, i, (m0, m1, m2, m3), dmem)
    gck[...] += dot(m, dk, 0, 0)
    gcv[...] += dot(m, dv, 0, 0)
    normed = n1[...]
    hidden = (normed * vecs[0:1, :] + vecs[3:4, :]).astype(bf16)
    dq = dqct[...].T
    gcq[...] += dot(hidden, dq, 0, 0)
    back = d2[...] + dot(dq, square(wb, 0), 1, 1)
    g_vec[0:1, :] += column_sum(back * normed)
    g_vec[3:4, :] += column_sum(back)
    first = norm_back(back, normed, inv1[...], vecs[0:1, :])
    d1[...] = first
    dao = first.astype(bf16)
    gwo[...] += dot(ot[...], dao)
    go[...] = dot(dao, square(wa, 3), 1, 1).astype(bf16)

    @pl.when(i == pl.num_programs(0) - 1)
    def _():
        keep = info[3 * SEQS + 1] > 0
        for n, ref in enumerate((gcq, gck, gcv)):
            g_cross[n * D : (n + 1) * D, :] = jnp.where(keep, ref[...], 0.0).astype(bf16)
        g_cross[3 * D :, :] = g_co[...]
        g_wo[...] = jnp.where(keep, gwo[...], 0.0).astype(bf16)
        g_vec[...] = jnp.where(keep, g_vec[...], 0.0)


def self_grad_kernel(
    info, dqt, dk_ref, dv_ref, x_ref, g_wo, g_cross, g_small, keep_out, send_out, gq, gk, gv
):
    i = pl.program_id(0)

    @pl.when(i == 0)
    def _():
        for ref in (gq, gk, gv):
            ref[...] = jnp.zeros_like(ref)

    x = x_ref[...]
    gq[...] += dot(x, dqt[...], 0, 1)
    gk[...] += dot(x, dk_ref[...], 0, 0)
    gv[...] += dot(x, dv_ref[...], 0, 0)

    @pl.when(i == pl.num_programs(0) - 1)
    def _():
        keep = info[3 * SEQS + 1] > 0
        rows = 4 * BROWS
        for ref, core in ((keep_out, info[CORE]), (send_out, 1 - info[CORE])):
            for n in range(4):
                blocks = slice(4 * n, 4 * n + 4)
                r0 = pl.multiple_of(core * rows, rows)
                if n < 3:
                    part = jnp.where(keep, (gq, gk, gv)[n][pl.ds(r0, rows), :], 0.0).astype(bf16)
                else:
                    part = g_wo[pl.ds(r0, rows), :]
                ref[blocks, :BROWS, :] = part.reshape(4, BROWS, D)
                part = g_cross[pl.ds(pl.multiple_of(r0 + n * D, rows), rows), :]
                ref[blocks, BROWS : 2 * BROWS, :] = part.reshape(4, BROWS, D)
                ref[blocks, 2 * BROWS :, :] = g_small[pl.ds((2 * n + core) * 4, 4), :, :]


def self_input_kernel(info, dqt, dk, dv, d1, wa, t0, t1, t2, t3):
    value = (
        d1[...]
        + dot(dqt[...], square(wa, 0), 0, 1)
        + dot(dk[...], square(wa, 1), 1, 1)
        + dot(dv[...], square(wa, 2), 1, 1)
    ).astype(bf16)
    store_shifted(info, pl.program_id(0), (t0, t1, t2, t3), value)


def pick_kernel(count, places, *refs):
    arrays, outs, sems = refs[:count], refs[count : 5 * count], refs[5 * count]
    copies = []
    for n, array in enumerate(arrays):
        for k in range(PIECES):
            copies.append(
                pltpu.make_async_copy(array.at[places[k]], outs[n * PIECES + k], sems.at[n, k])
            )
    for copy in copies:
        copy.start()
    for copy in copies:
        copy.wait()


def place_kernel(places, near, far, out):
    for n in range(HALF):
        out[pl.ds(places[n], 1)] = near[n : n + 1]
        out[pl.ds(places[HALF + n], 1)] = far[n : n + 1]


def unpack_kernel(places, r0, r1, r2, r3, out):
    b = pl.program_id(0)
    for k, ref in enumerate((r0, r1, r2, r3)):

        @pl.when(places[b] == k)
        def _():
            out[0] = ref[...].astype(f32)


def plus(*parts):
    total = parts[0].astype(f32)
    for part in parts[1:]:
        total = total + part.astype(f32)
    return total


def route_one_kernel(info, keep, recv, a_keep, a_send, b_keep, b_send):
    x, y = info[CORE + 1], info[CORE + 2]
    for n in range(2):
        for ref, own in ((a_keep, x), (a_send, 1 - x)):
            at = (2 * n + own) * 4
            ref[n] = plus(keep[pl.ds(at, 2)], recv[pl.ds(at, 2)]).astype(bf16)
        for ref, own in ((b_keep, y), (b_send, 1 - y)):
            at = (2 * own + n) * 4 + 2
            ref[n] = plus(keep[pl.ds(at, 2)], recv[pl.ds(at, 2)]).astype(bf16)


def route_two_kernel(info, a, ra, b, rb, a_keep, a_send, b_keep, b_send):
    x, y = info[CORE + 1], info[CORE + 2]
    for ref, own in ((a_keep, y), (a_send, 1 - y)):
        ref[...] = plus(a[own], ra[own]).astype(bf16)
    for ref, own in ((b_keep, x), (b_send, 1 - x)):
        ref[...] = plus(b[own], rb[own]).astype(bf16)


def route_three_kernel(info, a, ra, b, rb, o0, o1, o2, o3, total):
    total[0:2] = plus(a[...], ra[...]).astype(bf16)
    total[2:4] = plus(b[...], rb[...]).astype(bf16)
    for k, ref in enumerate((o0, o1, o2, o3)):
        ref[...] = total[lax.rem(info[3 * SEQS] + k, PIECES)]


def route_four_kernel(r0, r1, r2, r3, out):
    out[...] = plus(r0[...], r1[...], r2[...], r3[...])


SMEM = pl.BlockSpec(memory_space=pltpu.SMEM)
WHOLE = pl.BlockSpec(memory_space=pltpu.VMEM)
ROWS = pl.BlockSpec((PIECE, D), lambda i: (i, 0))
COLS = pl.BlockSpec((D, PIECE), lambda i: (0, i))
ROWS_Q = pl.BlockSpec((QB, D), lambda i: (i, 0))
COLS_Q = pl.BlockSpec((D, QB), lambda i: (0, i))
HEADS_Q = pl.BlockSpec((HEADS, QB), lambda i: (0, i))
ROWS_F = pl.BlockSpec((FR, D), lambda i: (i, 0))
COLS_F = pl.BlockSpec((D, FR), lambda i: (0, i))
ONES = pl.BlockSpec((PIECE, 1), lambda i: (i, 0))


def fixed(*shape):
    return pl.BlockSpec(
        shape, lambda i: (0,) * len(shape), pipeline_mode=pl.Buffered(buffer_count=1)
    )


def shape(dims, dtype=bf16):
    return jax.ShapeDtypeStruct(dims, dtype)


def call(kernel, name, grid, in_specs, out_specs, out_shape, scratch, flops, *args):
    return pl.pallas_call(
        kernel,
        grid=grid,
        in_specs=in_specs,
        out_specs=out_specs,
        out_shape=out_shape,
        scratch_shapes=scratch,
        name=name,
        compiler_params=pltpu.CompilerParams(vmem_limit_bytes=VMEM_LIMIT),
        cost_estimate=pl.CostEstimate(flops=flops, bytes_accessed=8 << 20, transcendentals=0),
    )(*args)


ROWMAJOR = shape((GROUP, D))
COLMAJOR = shape((D, GROUP))


def project_rows(info, pieces, w, with_query):
    outs = [ROWMAJOR] + ([COLMAJOR] if with_query else []) + [ROWMAJOR, ROWMAJOR]
    return call(
        functools.partial(project_kernel, with_query),
        "project",
        (),
        [SMEM] + [WHOLE] * 5,
        [WHOLE] * len(outs),
        outs,
        [],
        4 << 30,
        info,
        *pieces,
        w,
    )


def attend(info, qt, k, v, cross):
    return call(
        functools.partial(attend_kernel, cross),
        "attend",
        (GROUP // QB,),
        [SMEM, COLS_Q, fixed(GROUP, D), fixed(GROUP, D)],
        [COLS_Q, HEADS_Q],
        [COLMAJOR, shape((HEADS, GROUP), f32)],
        [
            pltpu.VMEM((D, GROUP), bf16),
            pltpu.VMEM((HEADS, QB), f32),
            pltpu.VMEM((HEADS, QB), f32),
            pltpu.VMEM((D, QB), f32),
            pltpu.VMEM((KB, QB), f32),
        ],
        30 << 30,
        info,
        qt,
        k,
        v,
    )


def attend_back(info, qt, k, v, g, ot, lse, cross):
    return call(
        functools.partial(attend_back_kernel, cross),
        "attend_back",
        (GROUP // QB,),
        [SMEM, COLS_Q, fixed(GROUP, D), fixed(GROUP, D), ROWS_Q, COLS_Q, HEADS_Q],
        [COLS_Q, fixed(GROUP, D), fixed(GROUP, D)],
        [COLMAJOR, ROWMAJOR, ROWMAJOR],
        [
            pltpu.VMEM((D, GROUP), bf16),
            pltpu.VMEM((D, QB), f32),
            pltpu.VMEM((GROUP, D), f32),
            pltpu.VMEM((GROUP, D), f32),
            pltpu.VMEM((D, QB), bf16),
            pltpu.VMEM((HEADS // 2, 2 * QB, 2 * HEAD_DIM), bf16),
            pltpu.VMEM((HEADS // 2, 2 * QB, 2 * HEAD_DIM), bf16),
            pltpu.VMEM((KB, QB), f32),
        ],
        60 << 30,
        info,
        qt,
        k,
        v,
        g,
        ot,
        lse,
    )


ANY = pl.BlockSpec(memory_space=pl.ANY)


def pick_four(arrays, places):
    n = len(arrays)
    outs = call(
        functools.partial(pick_kernel_args, n),
        "pick",
        (),
        [SMEM] + [ANY] * n,
        [WHOLE] * (PIECES * n),
        [shape(a.shape[1:], a.dtype) for a in arrays for _ in range(PIECES)],
        [pltpu.SemaphoreType.DMA((n, PIECES))],
        1 << 20,
        places,
        *arrays,
    )
    return [list(outs[PIECES * m : PIECES * (m + 1)]) for m in range(n)]


def pick_kernel_args(count, places, *refs):
    pick_kernel(count, places, *refs)


def place_blocks(places, near, far):
    return call(
        place_kernel,
        "place",
        (),
        [SMEM, WHOLE, WHOLE],
        WHOLE,
        shape((BLOCKS,) + near.shape[1:]),
        [],
        1 << 20,
        places,
        near,
        far,
    )


def unpack(places, pieces, micro):
    return call(
        unpack_kernel,
        "unpack",
        (micro,),
        [SMEM] + [fixed(PIECE, D)] * PIECES,
        pl.BlockSpec((1, PIECE, D), lambda b: (b, 0, 0)),
        shape((micro, PIECE, D), f32),
        [],
        1 << 20,
        places,
        *pieces,
    )


def route_one(info, keep, recv):
    half = shape((2, 2) + keep.shape[1:])
    return call(
        route_one_kernel, "route_one", (), [SMEM, WHOLE, WHOLE], [WHOLE] * 4, [half] * 4, [], 1 << 20,
        info, keep, recv,
    )


def route_two(info, a, ra, b, rb):
    half = shape(a.shape[1:])
    return call(
        route_two_kernel, "route_two", (), [SMEM] + [WHOLE] * 4, [WHOLE] * 4, [half] * 4, [], 1 << 20,
        info, a, ra, b, rb,
    )


def route_three(info, a, ra, b, rb):
    block = a.shape[1:]
    return call(
        route_three_kernel, "route_three", (), [SMEM] + [WHOLE] * 4, [WHOLE] * 4,
        [shape(block)] * 4, [pltpu.VMEM((4,) + block, bf16)], 1 << 20,
        info, a, ra, b, rb,
    )


def route_four(pieces):
    return call(
        route_four_kernel, "route_four", (), [WHOLE] * 4, WHOLE, shape(pieces[0].shape, f32), [], 1 << 20,
        *pieces,
    )


def tie(value, *deps):
    return lax.optimization_barrier((value, deps))[0]


def dp_swap(array, bit):
    n = lax.axis_size("dp")
    return lax.ppermute(array, "dp", [(d, d ^ bit) for d in range(n)])


def turns(arrays):
    n = lax.axis_size("fsdp")
    return [arrays[0]] + [
        lax.ppermute(arrays[k], "fsdp", [(m, (m + k) % n) for m in range(n)])
        for k in range(1, len(arrays))
    ]


def local(
    tokens, memory, cotangent, lengths, seq_order, memory_pick,
    self_attn, cross_attn, ffn_in, ffn_in_bias, ffn_out, ffn_out_bias, norm_gain, norm_bias,
):
    axes = ("dp", "fsdp")
    n_dp, members = lax.axis_size("dp"), lax.axis_size("fsdp")
    micro = tokens.shape[0]
    owners = n_dp * members
    dp, z = lax.axis_index("dp"), lax.axis_index("fsdp")

    def offset(d):
        return d % 2 if micro < members else 0

    def unit_at(d, member):
        return member - offset(d)

    mine = unit_at(dp, z)
    valid = (mine >= 0) & (mine < micro)
    unit = jnp.clip(mine, 0, micro - 1)

    def pairs(k, into):
        out = []
        for d in range(n_dp):
            for source in range(members):
                target = (source + k) % members
                if 0 <= unit_at(d, target if into else source) < micro:
                    out.append((d * members + source, d * members + target))
        return out

    boxed = n_dp == 8 and members == 4
    shifts = jnp.arange(members, dtype=jnp.int32)

    targets = jnp.clip(lax.rem(z + shifts, members) - offset(dp), 0, micro - 1)
    sources = lax.rem(z - offset(dp) - jnp.arange(micro, dtype=jnp.int32) + 2 * members, members)
    targets = targets.at[0].set(unit).astype(jnp.int32)

    def to_unit(pieces):
        return [pieces[0]] + [
            lax.ppermute(pieces[k], axes, pairs(k, True)) for k in range(1, members)
        ]

    def from_unit(pieces):
        return [pieces[0]] + [
            lax.ppermute(pieces[k], axes, pairs(k, False)) for k in range(1, members)
        ]

    def row_of(array):
        return lax.dynamic_index_in_dim(array, unit, 0, False)[0]

    bits = [dp & 1, (dp >> 1) & 1, (dp >> 2) & 1] if boxed else [jnp.zeros_like(dp)] * 3
    info = jnp.concatenate(
        [
            row_of(lengths),
            row_of(seq_order),
            row_of(memory_pick),
            jnp.stack([z, valid.astype(jnp.int32), *bits]),
        ]
    ).astype(jnp.int32)

    smalls = jnp.concatenate(
        [ffn_in_bias, ffn_out_bias, norm_gain.T.reshape(-1), norm_bias.T.reshape(-1)]
    )
    rows = self_attn.shape[0]
    in_rows = ffn_in.shape[0]
    n_smalls = smalls.shape[0]
    small_row = jnp.pad(smalls, (0, 16 * D - n_smalls)).reshape(16, D)
    bundle_a = jnp.concatenate([self_attn, small_row], axis=0)
    in_blocks = ffn_in.reshape(in_rows, 4, D).transpose(1, 0, 2).reshape(4 * in_rows, D)
    bundle_b = jnp.concatenate([cross_attn, ffn_out, in_blocks], axis=0)
    token_slices = pick_four([tokens], targets)[0]
    bundle_a = tie(bundle_a, *token_slices)
    token_pieces = to_unit(token_slices)
    if boxed:
        turned = turns([bundle_a] * members)
        a0, b0 = jnp.stack(turned[:2]), jnp.stack(turned[2:])
        a1, b1 = dp_swap(a0, 2), dp_swap(b0, 4)
        a2 = dp_swap(jnp.stack([a0, a1]), 4)
        b2 = dp_swap(jnp.stack([b0, b1]), 2)
        near = jnp.concatenate([a0, a1, a2[0], a2[1], b0, b1, b2[0], b2[1]])
        near = tie(near, *token_pieces[1:])
        far = dp_swap(near, 1)
        masks = jnp.array([0, 0, 2, 2, 4, 4, 6, 6, 0, 0, 4, 4, 2, 2, 6, 6], jnp.int32)
        steps = jnp.array([0, 1] * 4 + [2, 3] * 4, jnp.int32)
        owner = (dp ^ masks) * members + lax.rem(z - steps + members, members)
        places = jnp.concatenate([owner, owner ^ members]).astype(jnp.int32)
        all_a = place_blocks(places, near, far)
    else:
        all_a = lax.all_gather(bundle_a, axes, axis=0, tiled=False)
    all_b = lax.all_gather(bundle_b, axes, axis=0, tiled=False)
    def blocked(array, count):
        return array.reshape(BLOCKS, count, D)

    small = all_a[:, rows, :n_smalls].astype(f32)
    if owners == BLOCKS:
        wa, wb = all_a, all_b
    else:
        wa = jnp.pad(blocked(all_a[:, :rows], BROWS), ((0, 0), (0, SMALL), (0, 0)))
        first = all_b[:, 2 * rows :].reshape(owners, 4, in_rows, D).transpose(1, 0, 2, 3)
        first = first.reshape(4, BLOCKS, BROWS // 4, D).transpose(1, 0, 2, 3)
        wb = jnp.concatenate(
            [
                blocked(all_b[:, :rows], BROWS),
                blocked(all_b[:, rows : 2 * rows], BROWS),
                blocked(first, BROWS),
            ],
            axis=1,
        )
    out_rows = D // owners
    b1 = small[:, :rows].reshape(1, FF)
    at = rows + out_rows
    vec_rows = [small[:, at + n * out_rows : at + (n + 1) * out_rows].reshape(1, D) for n in range(6)]
    vecs = jnp.concatenate(
        vec_rows + [small[:, rows:at].reshape(1, D), jnp.zeros((1, D), f32)], axis=0
    )

    x, qt, k, v = project_rows(info, token_pieces, wa, True)
    memory_in = tie(memory, x)
    memory_pieces = to_unit(pick_four([memory_in], targets)[0])
    ot, lse = attend(info, qt, k, v, False)
    ot = tie(ot, *memory_pieces[1:])
    cotangent_in = tie(cotangent, *memory_pieces[1:])
    cotangent_pieces = to_unit(pick_four([cotangent_in], targets)[0])
    n1, inv1, qct = call(
        first_norm_kernel,
        "first_norm",
        (PIECES,),
        [COLS, ROWS, fixed(BLOCKS, BROWS + SMALL, D), fixed(BLOCKS, 3 * BROWS, D), fixed(8, D)],
        [ROWS, ONES, COLS],
        [shape((GROUP, D), f32), shape((GROUP, 1), f32), COLMAJOR],
        [],
        2 << 30,
        ot,
        x,
        wa,
        wb,
        vecs,
    )
    mem, kc, vc = project_rows(info, memory_pieces, wb, False)
    oct_, lse_c = attend(info, qct, kc, vc, True)
    *y_out, d2, gc, keep_ffn, send_ffn, g_co, g_b1, g_vec = call(
        ffn_kernel,
        "ffn",
        (GROUP // FR,),
        [SMEM, COLS_F, ROWS_F, fixed(BLOCKS, 3 * BROWS, D), fixed(8, D), fixed(1, FF)]
        + [fixed(PIECE, D)] * 4,
        [
            *[fixed(PIECE, D)] * PIECES,
            ROWS_F,
            ROWS_F,
            fixed(HALF, 2 * BROWS, D),
            fixed(HALF, 2 * BROWS, D),
            fixed(D, D),
            fixed(1, FF),
            fixed(8, D),
        ],
        [
            *[shape((PIECE, D))] * PIECES,
            shape((GROUP, D), f32),
            ROWMAJOR,
            shape((HALF, 2 * BROWS, D)),
            shape((HALF, 2 * BROWS, D)),
            shape((D, D)),
            shape((1, FF), f32),
            shape((8, D), f32),
        ],
        [
            pltpu.VMEM((GROUP, D), bf16),
            pltpu.VMEM((FR, FF), bf16),
            pltpu.VMEM((FR, FF), f32),
            pltpu.VMEM((FR, D), f32),
            pltpu.VMEM((4, D, D), f32),
            pltpu.VMEM((FF, D), f32),
            pltpu.VMEM((D, D), f32),
            pltpu.VMEM((GROUP, D), f32),
        ],
        32 << 30,
        info,
        oct_,
        n1,
        wb,
        vecs,
        b1,
        *cotangent_pieces,
    )
    y_pieces = from_unit(y_out)
    if boxed:
        recv_ffn = dp_swap(send_ffn, 1)

    dqct, dkc, dvc = attend_back(info, qct, kc, vc, gc, oct_, lse_c, True)
    if boxed:
        recv_ffn = tie(recv_ffn, dqct)
        ffn_a, send_a, ffn_b, send_b = route_one(info, keep_ffn, recv_ffn)
        recv_a, recv_b = dp_swap(send_a, 2), dp_swap(send_b, 4)
    layer_output = unpack(sources, y_pieces, micro)
    if boxed:
        g_co = tie(g_co, send_a, layer_output)
    m_and_rest = call(
        cross_post_kernel,
        "cross_post",
        (PIECES,),
        [SMEM, COLS, ROWS, ROWS, ROWS, ROWS, ROWS, ONES, COLS]
        + [fixed(BLOCKS, BROWS + SMALL, D), fixed(BLOCKS, 3 * BROWS, D), fixed(8, D), fixed(D, D)],
        [fixed(PIECE, D)] * PIECES + [ROWS, ROWS, fixed(4 * D, D), fixed(D, D), fixed(8, D)],
        [shape((PIECE, D))] * PIECES
        + [
            shape((GROUP, D), f32),
            ROWMAJOR,
            shape((4 * D, D)),
            shape((D, D)),
            shape((8, D), f32),
        ],
        [pltpu.VMEM((D, D), f32)] * 4,
        9 << 30,
        info,
        dqct,
        dkc,
        dvc,
        mem,
        d2,
        n1,
        inv1,
        ot,
        wa,
        wb,
        vecs,
        g_co,
    )
    *m_out, d1, go, g_cross, g_wo, g_vec_one = m_and_rest
    m_pieces = from_unit(m_out)
    if boxed:
        recv_a, recv_b, ffn_a, ffn_b = tie((recv_a, recv_b, ffn_a, ffn_b), d1)
        ffn_a, send_a, ffn_b, send_b = route_two(info, ffn_a, recv_a, ffn_b, recv_b)
        recv_a, recv_b = dp_swap(send_a, 4), dp_swap(send_b, 2)
        go = tie(go, send_a)
    g_vec = g_vec + g_vec_one
    small_grads = jnp.concatenate(
        [g_b1.reshape(owners, rows), g_vec[6].reshape(owners, out_rows)]
        + [g_vec[n].reshape(owners, out_rows) for n in range(6)],
        axis=1,
    )
    if boxed:
        g_small = jnp.pad(small_grads.astype(bf16), ((0, 0), (0, SMALL * D - n_smalls)))
        g_small = g_small.reshape(BLOCKS, SMALL, D)
    else:
        g_small = jnp.zeros((BLOCKS, SMALL, D), bf16)
    dqt, dk, dv = attend_back(info, qt, k, v, go, ot, lse, False)
    if boxed:
        recv_a, recv_b, ffn_a, ffn_b = tie((recv_a, recv_b, ffn_a, ffn_b), dqt)
        ffn_pieces = turns(route_three(info, ffn_a, recv_a, ffn_b, recv_b))
    memory_grad = unpack(sources, m_pieces, micro)
    if boxed:
        x_late = tie(x, ffn_pieces[0], memory_grad)
    else:
        x_late = x
    last_rows = 2 * BROWS + SMALL
    keep_last, send_last = call(
        self_grad_kernel,
        "self_grad",
        (PIECES,),
        [SMEM, COLS, ROWS, ROWS, ROWS, fixed(D, D), fixed(4 * D, D), fixed(BLOCKS, SMALL, D)],
        [fixed(HALF, last_rows, D)] * 2,
        [shape((HALF, last_rows, D))] * 2,
        [pltpu.VMEM((D, D), f32)] * 3,
        4 << 30,
        info,
        dqt,
        dk,
        dv,
        x_late,
        g_wo,
        g_cross,
        g_small,
    )
    if boxed:
        recv_last = dp_swap(send_last, 1)
        ffn_part = route_four(ffn_pieces)
        d1 = tie(d1, ffn_part)
    d1 = tie(d1, keep_last)
    t_out = call(
        self_input_kernel,
        "self_input",
        (PIECES,),
        [SMEM, COLS, ROWS, ROWS, ROWS, fixed(BLOCKS, BROWS + SMALL, D)],
        [fixed(PIECE, D)] * PIECES,
        [shape((PIECE, D))] * PIECES,
        [],
        4 << 30,
        info,
        dqt,
        dk,
        dv,
        d1,
        wa,
    )
    t_pieces = from_unit(t_out)

    def whole_blocks(keep, send):
        both = jnp.stack([keep, send]).reshape(2, 4, 4, -1, D)
        return both.transpose(1, 0, 2, 3, 4).reshape(BLOCKS, -1, D)

    def owned(array):
        return lax.psum_scatter(array, axes, scatter_dimension=0, tiled=True)[0].astype(f32)

    if boxed:
        recv_last = tie(recv_last, *t_out)
        near, send_a, far, send_b = route_one(info, keep_last, recv_last)
        recv_a, recv_b = dp_swap(send_a, 2), dp_swap(send_b, 4)
        near = tie(near, t_pieces[1])
        near, send_a, far, send_b = route_two(info, near, recv_a, far, recv_b)
        recv_a, recv_b = dp_swap(send_a, 4), dp_swap(send_b, 2)
        near = tie(near, *t_pieces)
        last = route_four(turns(route_three(info, near, recv_a, far, recv_b)))
        self_attn_grad, cross_attn_grad = last[:BROWS], last[BROWS : 2 * BROWS]
        small_out = last[2 * BROWS]
    else:
        ffn = whole_blocks(keep_ffn, send_ffn)
        second = ffn[:, BROWS:].reshape(owners, rows, D)
        first = ffn[:, :BROWS].reshape(BLOCKS, 4, BROWS // 4, D).transpose(1, 0, 2, 3)
        first = first.reshape(4, owners, in_rows, D).transpose(1, 0, 2, 3)
        ffn_part = owned(jnp.concatenate([first.reshape(owners, rows, D), second], axis=1))
        rest = whole_blocks(keep_last, send_last)
        self_attn_grad = owned(rest[:, :BROWS].reshape(owners, rows, D))
        cross_attn_grad = owned(rest[:, BROWS : 2 * BROWS].reshape(owners, rows, D))
        small_out = owned(small_grads)
    ffn_in_grad = ffn_part[:rows].reshape(4, in_rows, D).transpose(1, 0, 2).reshape(in_rows, FF)
    norm_part = small_out[at : at + 6 * out_rows].reshape(6, out_rows)
    return (
        layer_output,
        unpack(sources, t_pieces, micro),
        memory_grad,
        self_attn_grad,
        cross_attn_grad,
        ffn_in_grad,
        small_out[:rows],
        ffn_part[rows:],
        small_out[rows:at],
        norm_part[:3].T,
        norm_part[3:].T,
    )


def solution(mesh):
    rows = P(None, ("dp", "fsdp"), None)
    group = P(None, "dp", None)
    shard = P(("dp", "fsdp"), None)
    flat = P(("dp", "fsdp"))
    in_specs = (rows,) * 3 + (group,) * 3 + (shard, shard, shard, flat, shard, flat, shard, shard)
    out_specs = (rows,) * 3 + (shard, shard, shard, flat, shard, flat, shard, shard)
    return jax.shard_map(local, mesh=mesh, in_specs=in_specs, out_specs=out_specs, check_vma=False)
```

```python
import functools
import math

import jax
import jax.numpy as jnp
from jax import lax
from jax.experimental import pallas as pl
from jax.experimental.pallas import tpu as pltpu
from jax.sharding import PartitionSpec as P

D = 512
HEADS = 8
HEAD_DIM = 64
FF = 2048
MEM_LEN = 1024
SEQS = 4
NMEM = 2
GROUP = 2048
PIECE = 512
PIECES = GROUP // PIECE
QB = 256
KB = 512
FR = 512
LANES = 128
KEPT = 1024
NEG = -1e30
BLOCKS = 32
BROWS = D * 4 // BLOCKS
bf16 = jnp.bfloat16
f32 = jnp.float32
VMEM_LIMIT = 58 << 20
CORE = 3 * SEQS + 2
HALF = BLOCKS // 2
SMALL = 16
MICRO = 3
SOURCES = 3 * SEQS + 5


def dot(left, right, cl=1, cr=0):
    return lax.dot_general(
        left, right, (((cl,), (cr,)), ((), ())), preferred_element_type=f32
    )


def place_ends(info):
    ends, total = [], 0
    for j in range(SEQS):
        total = total + info[info[SEQS + j]]
        ends.append(total)
    return ends


def place_picks(info):
    return [info[2 * SEQS + info[SEQS + j]] for j in range(SEQS)]


def place_shifts(info, ends):
    shifts = []
    for j in range(SEQS):
        seq = info[SEQS + j]
        start = 0
        for s in range(SEQS):
            start = start + jnp.where(s < seq, info[s], 0)
        shifts.append(start - (ends[j - 1] if j else 0))
    return shifts


def by_place(rows, ends, values):
    out = jnp.full(rows.shape, values[0], jnp.int32)
    for j in range(SEQS - 1):
        out = jnp.where(rows >= ends[j], values[j + 1], out)
    return out


def piece_row(info, k):
    return pl.multiple_of(lax.rem(info[3 * SEQS] - k + PIECES, PIECES) * PIECE, PIECE)


def weight(ref, first, count, offset, rows):
    return ref[first : first + count, offset : offset + rows, :].reshape(count * rows, D)


def square(ref, index, offset=0):
    per = BLOCKS // 4
    return weight(ref, index * per, per, offset, BROWS)


def project_kernel(kind, info, x0, x1, x2, x3, *refs):
    with_query = kind > 0
    if kind == 2:
        places, near, far, x_out, qt_out, k_out, v_out, w = refs
        for n in range(HALF):
            w[pl.ds(places[n], 1)] = near[n : n + 1]
            w[pl.ds(places[HALF + n], 1)] = far[n : n + 1]
    elif kind == 1:
        w, x_out, qt_out, k_out, v_out = refs
    else:
        w, x_out, k_out, v_out = refs
    if with_query:
        wq = square(w, 0)
    wk, wv = square(w, 1), square(w, 2)
    for k, piece in enumerate((x0, x1, x2, x3)):
        r0 = piece_row(info, k)
        rows = pl.ds(r0, PIECE)
        x = piece[...]
        x_out[rows, :] = x
        if with_query:
            q = dot(x, wq).astype(bf16) * jnp.asarray(HEAD_DIM**-0.5, bf16)
            qt_out[:, rows] = q.T
        k_out[rows, :] = dot(x, wk).astype(bf16)
        v_out[rows, :] = dot(x, wv).astype(bf16)


def memories_read(info, q0):
    ends, picks = place_ends(info), place_picks(info)
    rows = q0 + lax.broadcasted_iota(jnp.int32, (1, QB), 1)
    picked = by_place(rows, ends, picks)
    needs = []
    for mem in range(NMEM):
        need = jnp.bool_(False)
        for j in range(SEQS):
            start = ends[j - 1] if j else 0
            need = need | ((start < q0 + QB) & (ends[j] > q0) & (picks[j] == mem))
        needs.append(need)
    return needs, [picked == mem for mem in range(NMEM)]


def window(info, q0):
    ends = place_ends(info)
    rows = q0 + lax.broadcasted_iota(jnp.int32, (1, QB), 1)
    low, high = 0, GROUP
    low_row = jnp.zeros((1, QB), jnp.int32)
    high_row = jnp.full((1, QB), GROUP, jnp.int32)
    for j in range(SEQS - 1):
        low = jnp.where(q0 >= ends[j], ends[j], low)
        low_row = jnp.where(rows >= ends[j], ends[j], low_row)
    for j in reversed(range(SEQS - 1)):
        high = jnp.where(q0 + QB - 1 < ends[j], ends[j], high)
        high_row = jnp.where(rows < ends[j], ends[j], high_row)
    low = low // LANES * LANES
    many = (high - low) // KB
    rest = high - low - many * KB
    many = jnp.where(rest > KB // 2, many + 1, many)
    narrow = (rest > 0) & (rest <= KB // 2)

    def place(first, size):
        k0 = pl.multiple_of(jnp.minimum(first, GROUP - size), LANES)
        keys = k0 + lax.broadcasted_iota(jnp.int32, (size, QB), 0)
        inside = (keys >= jnp.maximum(low_row, first)) & (keys < high_row)
        return k0, jnp.where(inside, 0.0, NEG)

    return low, many, narrow, place


def loop(first, last, body):
    def step(j, carry):
        body(j)
        return carry

    lax.fori_loop(first, last, step, 0)


def head_rows(h):
    return slice(h * HEAD_DIM, (h + 1) * HEAD_DIM)


def pipelined(groups, *stages):
    for step in range(groups + len(stages) - 1):
        for lag, stage in enumerate(stages):
            if 0 <= step - lag < groups:
                stage(step - lag)


def attend_kernel(
    cross, info, qt, k, v, ot, lse, flags, saved, vt, top, total, peak, acc, bias_ref
):
    i = pl.program_id(0)
    q0 = pl.multiple_of(i * QB, QB)
    group = 2

    @pl.when(i == 0)
    def _():
        for c in range(GROUP // QB):
            vt[:, c * QB : (c + 1) * QB] = v[c * QB : (c + 1) * QB, :].T

    def tile(safe, k0, size, bias, allowed, slot):
        keys = pl.ds(k0, size)
        if bias is not None:
            bias_ref[:size, :] = bias
        totals = total[...]
        tops = top[...] if safe else None
        new_tops, new_totals, peaks = [], [], []
        scores, parts = {}, {}

        def score(g):
            heads = range(g * group, (g + 1) * group)
            scores[g] = [dot(k[keys, head_rows(h)], qt[head_rows(h), :]) for h in heads]

        def soften(g):
            parts[g] = []
            for n, s in enumerate(scores.pop(g)):
                h = g * group + n
                decay = None
                if bias is not None:
                    s = s + bias_ref[:size, :]
                if safe:
                    old = tops[h : h + 1]
                    new = jnp.maximum(old, jnp.max(s, axis=0, keepdims=True))
                    if allowed is not None:
                        new = jnp.where(allowed, new, old)
                    decay = jnp.exp(old - new)
                    new_tops.append(new)
                    s = s - new
                p = jnp.exp(s)
                part = jnp.sum(p, axis=0, keepdims=True)
                if allowed is not None:
                    peaks.append(part)
                    p = jnp.where(allowed, p, 0.0)
                    part = jnp.where(allowed, part, 0.0)
                before = totals[h : h + 1]
                new_totals.append((before * decay if safe else before) + part)
                low = p.astype(bf16)
                if slot is not None:
                    saved[0, h, pl.ds(slot, size), :] = low
                parts[g].append((decay, low))

        def mix(g):
            for n, (decay, p) in enumerate(parts.pop(g)):
                rows = head_rows(g * group + n)
                before = acc[rows, :]
                acc[rows, :] = (before * decay if safe else before) + dot(vt[rows, keys], p)

        pipelined(HEADS // group, score, soften, mix)
        if safe:
            top[...] = jnp.concatenate(new_tops, axis=0)
        elif peaks:
            peak[...] = jnp.maximum(peak[...], jnp.concatenate(peaks, axis=0))
        total[...] = jnp.concatenate(new_totals, axis=0)

    def sweep(safe):
        if safe:
            top[...] = jnp.full_like(top, NEG)
        else:
            peak[...] = jnp.zeros_like(peak)
        total[...] = jnp.zeros_like(total)
        acc[...] = jnp.zeros_like(acc)
        if cross:
            needs, allowed = memories_read(info, q0)
            both = needs[0] & needs[1]
            if safe:
                for mem in range(NMEM):

                    @pl.when(needs[mem])
                    def _():
                        tile(True, mem * MEM_LEN, MEM_LEN, None, allowed[mem], None)
            else:

                @pl.when(jnp.logical_not(both))
                def _():
                    first = pl.multiple_of(jnp.where(needs[0], 0, MEM_LEN), MEM_LEN)
                    tile(False, first, MEM_LEN, None, None, 0)

                @pl.when(both)
                def _():
                    tile(False, 0, MEM_LEN, None, allowed[0], 0)
                    tile(False, MEM_LEN, MEM_LEN, None, allowed[1], None)
        else:
            low, many, narrow, place = window(info, q0)

            def part(j, size, slot):
                k0, bias = place(low + j * KB, size)
                tile(safe, k0, size, bias, None, slot)

            kept = 0 if safe else jnp.minimum(many, KEPT // KB)
            if not safe:
                loop(0, kept, lambda j: part(j, KB, pl.multiple_of(j * KB, KB)))
            loop(kept, many, lambda j: part(j, KB, None))

            @pl.when(narrow)
            def _():
                part(many, KB // 2, None if safe else pl.multiple_of(kept * KB, KB))

        sums = total[...]
        inverse = 1.0 / sums
        lse[...] = jnp.log(sums) + (top[...] if safe else 0.0)
        for h in range(HEADS):
            ot[head_rows(h), :] = (acc[head_rows(h), :] * inverse[h : h + 1]).astype(bf16)

    sweep(False)
    sums = total[...]
    safe_range = (jnp.min(sums) > 1e-18) & (jnp.max(sums) < 1e18) & (jnp.max(peak[...]) < 1e18)
    flags[i] = safe_range.astype(jnp.int32)

    @pl.when(jnp.logical_not(safe_range))
    def _():
        sweep(True)


def attend_back_kernel(
    cross, info, flags, qt, k, v, g, ot, lse, saved, dqt, dk, dv,
    kt, dqt_acc, dk_acc, dv_acc, gt, gm, qm, bias_ref,
):
    i = pl.program_id(0)
    q0 = pl.multiple_of(i * QB, QB)
    group = 2
    shiftless = flags[i] > 0

    @pl.when(i == 0)
    def _():
        dk_acc[...] = jnp.zeros_like(dk_acc)
        dv_acc[...] = jnp.zeros_like(dv_acc)
        for c in range(GROUP // QB):
            kt[:, c * QB : (c + 1) * QB] = k[c * QB : (c + 1) * QB, :].T

    lses = lse[...]
    factor = jnp.where(shiftless, jnp.exp(-lses), 1.0)
    shifts = jnp.where(shiftless, 0.0, lses)
    weighted = []
    turned = g[...].T
    for h in range(HEADS):
        scaled = turned[head_rows(h), :].astype(f32) * factor[h : h + 1]
        weighted.append(
            jnp.sum(scaled * ot[head_rows(h), :].astype(f32), axis=0, keepdims=True)
        )
        gt[head_rows(h), :] = scaled.astype(bf16)
    left = lax.broadcasted_iota(jnp.int32, (QB, 2 * HEAD_DIM), 1) < HEAD_DIM
    for pair in range(HEADS // 2):
        cols = slice(pair * 2 * HEAD_DIM, (pair + 1) * 2 * HEAD_DIM)
        gp = gt[cols, :].T
        qp = qt[cols, :].T
        zero = jnp.zeros_like(gp)
        gm[pair, :QB, :] = jnp.where(left, gp, zero)
        gm[pair, QB:, :] = jnp.where(left, zero, gp)
        qm[pair, :QB, :] = jnp.where(left, qp, zero)
        qm[pair, QB:, :] = jnp.where(left, zero, qp)
    dqt_acc[...] = jnp.zeros_like(dqt_acc)

    def tile(k0, size, bias, allowed, slot):
        keys = pl.ds(k0, size)
        if bias is not None:
            bias_ref[:size, :] = bias
        bases = shifts if allowed is None else jnp.where(allowed, shifts, -NEG)
        scores, slopes, probs, grads = {}, {}, {}, {}

        def score(g):
            heads = range(g * group, (g + 1) * group)
            if slot is None:
                scores[g] = [dot(k[keys, head_rows(h)], qt[head_rows(h), :]) for h in heads]
            slopes[g] = [dot(v[keys, head_rows(h)], gt[head_rows(h), :]) for h in heads]

        def soften(g):
            probs[g], grads[g] = [], []
            for n, dp in enumerate(slopes.pop(g)):
                h = g * group + n
                if slot is None:
                    s = scores[g][n]
                    if bias is not None:
                        s = s + bias_ref[:size, :]
                    p = jnp.exp(s - bases[h : h + 1])
                    probs[g].append(p.astype(bf16))
                else:
                    probs[g].append(saved[0, h, pl.ds(slot, size), :])
                    p = probs[g][n].astype(f32)
                grads[g].append((p * (dp - weighted[h])).astype(bf16))

        def mix(g):
            for n in range(0, group, 2):
                pair = (g * group + n) // 2
                cols = slice(pair * 2 * HEAD_DIM, (pair + 1) * 2 * HEAD_DIM)
                dv_acc[keys, cols] += dot(jnp.concatenate(probs[g][n : n + 2], axis=1), gm[pair])
                dk_acc[keys, cols] += dot(jnp.concatenate(grads[g][n : n + 2], axis=1), qm[pair])
            for n, ds in enumerate(grads[g]):
                rows = head_rows(g * group + n)
                dqt_acc[rows, :] += dot(kt[rows, keys], ds)

        pipelined(HEADS // group, score, soften, mix)

    if cross:
        needs, allowed = memories_read(info, q0)

        @pl.when(shiftless)
        def _():
            first = pl.multiple_of(jnp.where(needs[0], 0, MEM_LEN), MEM_LEN)
            tile(first, MEM_LEN, None, None, 0)

        for mem in range(NMEM):
            done = shiftless & (jnp.logical_not(needs[0]) if mem else True)

            @pl.when(needs[mem] & jnp.logical_not(done))
            def _():
                tile(mem * MEM_LEN, MEM_LEN, None, allowed[mem], None)
    else:
        low, many, narrow, place = window(info, q0)

        def part(j, size, slot):
            k0, bias = place(low + j * KB, size)
            tile(k0, size, bias if slot is None else None, None, slot)

        kept = jnp.where(shiftless, jnp.minimum(many, KEPT // KB), 0)
        loop(0, kept, lambda j: part(j, KB, pl.multiple_of(j * KB, KB)))
        loop(kept, many, lambda j: part(j, KB, None))

        @pl.when(narrow & shiftless)
        def _():
            part(many, KB // 2, pl.multiple_of(kept * KB, KB))

        @pl.when(narrow & jnp.logical_not(shiftless))
        def _():
            part(many, KB // 2, None)

    dqt[...] = (dqt_acc[...] * HEAD_DIM**-0.5).astype(bf16)

    @pl.when(i == pl.num_programs(0) - 1)
    def _():
        dk[...] = dk_acc[...].astype(bf16)
        dv[...] = dv_acc[...].astype(bf16)


def norm(resid):
    center = resid - jnp.mean(resid, axis=-1, keepdims=True)
    inv = lax.rsqrt(jnp.mean(center * center, axis=-1, keepdims=True) + 1e-06)
    return center * inv, inv


def norm_back(grad, normed, inv, gain):
    scaled = grad * gain
    return inv * (
        scaled
        - jnp.mean(scaled, axis=-1, keepdims=True)
        - normed * jnp.mean(scaled * normed, axis=-1, keepdims=True)
    )


def column_sum(value):
    return jnp.sum(value, axis=0, keepdims=True)


def first_norm_kernel(ot, x, wa, wb, vecs, n1, inv1, qct):
    resid = x[...].astype(f32) + dot(ot[...], square(wa, 0), 0, 0)
    normed, inv = norm(resid)
    n1[...] = normed
    inv1[...] = inv
    hidden = (normed * vecs[0:1, :] + vecs[3:4, :]).astype(bf16)
    q = dot(hidden, square(wb, 0)).astype(bf16) * jnp.asarray(HEAD_DIM**-0.5, bf16)
    qct[...] = q.T


def ffn_kernel(
    info, oct_, n1, wb, vecs, b1, c0, c1, c2, c3,
    yg, d2, gc, keep_ffn, send_ffn, g_co, g_b1, g_vec,
    cot, act, slope, dy, gw1, gw2, gco, yacc,
):
    i = pl.program_id(0)

    @pl.when(i == 0)
    def _():
        for k, piece in enumerate((c0, c1, c2, c3)):
            cot[pl.ds(piece_row(info, k), PIECE), :] = piece[...]
        for ref in (gw1, gw2, gco, g_b1, g_vec, yacc):
            ref[...] = jnp.zeros_like(ref)

    first_block = 2 * BROWS
    chunk = BROWS // 4

    def w1(c):
        return weight(wb, 0, BLOCKS, first_block + c * chunk, chunk)

    def w2(c):
        per = BLOCKS // 4
        return weight(wb, c * per, per, BROWS, BROWS)

    hidden_one = n1[...] * vecs[0:1, :] + vecs[3:4, :]
    n2, inv2 = norm(hidden_one + dot(oct_[...], square(wb, 3), 0, 0))
    hidden = n2 * vecs[1:2, :] + vecs[4:5, :]
    hidden_b = hidden.astype(bf16)

    factor = math.sqrt(2.0 / math.pi)
    cubic = 0.044715 * factor
    ups, acts, outs = {}, {}, []

    def cols(c):
        return slice(c * D, (c + 1) * D)

    def up(c):
        ups[c] = dot(hidden_b, w1(c))

    def bend(c):
        u = ups.pop(c) + b1[0:1, cols(c)]
        sq = u * u
        t = jnp.tanh(u * (factor + cubic * sq))
        half = 0.5 + 0.5 * t
        acts[c] = (u * half).astype(bf16)
        act[:, cols(c)] = acts[c]
        slope[:, cols(c)] = half + u * (1.0 - t * t) * (0.5 * factor + 1.5 * cubic * sq)

    def down(c):
        outs.append(dot(acts.pop(c), w2(c)))

    pipelined(4, up, bend, down)
    out = (outs[0] + outs[1]) + (outs[2] + outs[3])
    n3, inv3 = norm(hidden + (out + vecs[6:7, :]))
    y = (n3 * vecs[2:3, :] + vecs[5:6, :]).astype(bf16)

    ends = place_ends(info)
    shifts = place_shifts(info, ends)
    p0 = i * FR
    rows = p0 + lax.broadcasted_iota(jnp.int32, (FR, 1), 0)
    given = rows + by_place(rows, ends, shifts)
    dy[...] = jnp.zeros_like(dy)

    def gather(c, carry):
        r0 = pl.multiple_of(c * QB, QB)
        hit = jnp.bool_(False)
        for j in range(SEQS):
            begin = jnp.maximum(ends[j - 1] if j else 0, p0)
            end = jnp.minimum(ends[j], p0 + FR)
            hit = hit | (
                (begin < end) & (begin + shifts[j] < r0 + QB) & (end + shifts[j] > r0)
            )

        @pl.when(hit)
        def _():
            cols = r0 + lax.broadcasted_iota(jnp.int32, (FR, QB), 1)
            select = jnp.where(cols == given, 1.0, 0.0).astype(bf16)
            dy[...] += dot(select, cot[pl.ds(r0, QB), :])
            yacc[pl.ds(r0, QB), :] += dot(select, y, 0, 0)

        return carry

    lax.fori_loop(0, GROUP // QB, gather, 0)

    grad = dy[...]
    g_vec[2:3, :] += column_sum(grad * n3)
    g_vec[5:6, :] += column_sum(grad)
    d3 = norm_back(grad, n3, inv3, vecs[2:3, :])
    df = d3.astype(bf16)
    g_vec[6:7, :] += column_sum(df.astype(f32))
    downs, dus, backs = {}, {}, [d3]

    def down_back(c):
        downs[c] = dot(df, w2(c), 1, 1)
        gw2[cols(c), :] += dot(act[:, cols(c)], df, 0, 0)

    def bend_back(c):
        dus[c] = (downs.pop(c) * slope[:, cols(c)]).astype(bf16)
        g_b1[0:1, cols(c)] += column_sum(dus[c].astype(f32))

    def up_back(c):
        du = dus.pop(c)
        gw1[c] += dot(hidden_b, du, 0, 0)
        backs.append(dot(du, w1(c), 1, 1))

    pipelined(4, down_back, bend_back, up_back)
    back = ((backs[0] + backs[1]) + (backs[2] + backs[3])) + backs[4]
    g_vec[1:2, :] += column_sum(back * n2)
    g_vec[4:5, :] += column_sum(back)
    second = norm_back(back, n2, inv2, vecs[1:2, :])
    d2[...] = second
    dco = second.astype(bf16)
    gco[...] += dot(oct_[...], dco)
    gc[...] = dot(dco, square(wb, 3), 1, 1).astype(bf16)

    @pl.when(i == pl.num_programs(0) - 1)
    def _():
        keep = info[3 * SEQS + 1] > 0
        yg[...] = yacc[...].astype(bf16)
        g_co[...] = jnp.where(keep, gco[...], 0.0).astype(bf16)
        for ref, core in ((keep_ffn, info[CORE]), (send_ffn, 1 - info[CORE])):
            for n in range(4):
                blocks = slice(4 * n, 4 * n + 4)
                for c in range(4):
                    r0 = pl.multiple_of((2 * n + core) * 4 * chunk, 4 * chunk)
                    part = jnp.where(keep, gw1[c, pl.ds(r0, 4 * chunk), :], 0.0).astype(bf16)
                    ref[blocks, c * chunk : (c + 1) * chunk, :] = part.reshape(4, chunk, D)
                r0 = pl.multiple_of((2 * n + core) * 4 * BROWS, 4 * BROWS)
                part = jnp.where(keep, gw2[pl.ds(r0, 4 * BROWS), :], 0.0).astype(bf16)
                ref[blocks, BROWS:, :] = part.reshape(4, BROWS, D)
        g_b1[...] = jnp.where(keep, g_b1[...], 0.0)
        g_vec[...] = jnp.where(keep, g_vec[...], 0.0)


def unpack_into(info, i, blocks, out):
    @pl.when(i < MICRO)
    def _():
        out[0] = blocks[info[SOURCES + jnp.minimum(i, MICRO - 1)]].astype(f32)


def cross_post_kernel(
    info, blocks, dqct, dkc, dvc, mem, d2, n1, inv1, ot, wa, wb, vecs, g_co,
    out, dmem, d1, go, g_cross, g_wo, g_vec,
    gcq, gck, gcv, gwo,
):
    i = pl.program_id(0)
    unpack_into(info, i, blocks, out)

    @pl.when(i == 0)
    def _():
        for ref in (gcq, gck, gcv, gwo, g_vec):
            ref[...] = jnp.zeros_like(ref)

    m, dk, dv = mem[...], dkc[...], dvc[...]
    dmem[...] = (dot(dk, square(wb, 1), 1, 1) + dot(dv, square(wb, 2), 1, 1)).astype(bf16)
    gck[...] += dot(m, dk, 0, 0)
    gcv[...] += dot(m, dv, 0, 0)
    normed = n1[...]
    hidden = (normed * vecs[0:1, :] + vecs[3:4, :]).astype(bf16)
    dq = dqct[...].T
    gcq[...] += dot(hidden, dq, 0, 0)
    back = d2[...] + dot(dq, square(wb, 0), 1, 1)
    g_vec[0:1, :] += column_sum(back * normed)
    g_vec[3:4, :] += column_sum(back)
    first = norm_back(back, normed, inv1[...], vecs[0:1, :])
    d1[...] = first
    dao = first.astype(bf16)
    gwo[...] += dot(ot[...], dao)
    go[...] = dot(dao, square(wa, 0), 1, 1).astype(bf16)

    @pl.when(i == pl.num_programs(0) - 1)
    def _():
        keep = info[3 * SEQS + 1] > 0
        for n, ref in enumerate((gcq, gck, gcv)):
            g_cross[n * D : (n + 1) * D, :] = jnp.where(keep, ref[...], 0.0).astype(bf16)
        g_cross[3 * D :, :] = g_co[...]
        g_wo[...] = jnp.where(keep, gwo[...], 0.0).astype(bf16)
        g_vec[...] = jnp.where(keep, g_vec[...], 0.0)


def self_grad_kernel(
    info, blocks, dqt, dk_ref, dv_ref, x_ref, g_wo, g_cross, g_small,
    out, keep_out, send_out,
    gq, gk, gv,
):
    i = pl.program_id(0)
    unpack_into(info, i, blocks, out)

    @pl.when(i == 0)
    def _():
        for ref in (gq, gk, gv):
            ref[...] = jnp.zeros_like(ref)

    x = x_ref[...]
    gq[...] += dot(x, dqt[...], 0, 1)
    gk[...] += dot(x, dk_ref[...], 0, 0)
    gv[...] += dot(x, dv_ref[...], 0, 0)

    @pl.when(i == pl.num_programs(0) - 1)
    def _():
        keep = info[3 * SEQS + 1] > 0
        rows = 4 * BROWS
        for ref, core in ((keep_out, info[CORE]), (send_out, 1 - info[CORE])):
            for n in range(4):
                blocks = slice(4 * n, 4 * n + 4)
                r0 = pl.multiple_of(core * rows, rows)
                if n < 3:
                    part = jnp.where(keep, (gq, gk, gv)[n][pl.ds(r0, rows), :], 0.0).astype(bf16)
                else:
                    part = g_wo[pl.ds(r0, rows), :]
                ref[blocks, :BROWS, :] = part.reshape(4, BROWS, D)
                part = g_cross[pl.ds(pl.multiple_of(r0 + n * D, rows), rows), :]
                ref[blocks, BROWS : 2 * BROWS, :] = part.reshape(4, BROWS, D)
                ref[blocks, 2 * BROWS :, : 2 * LANES] = g_small[pl.ds((2 * n + core) * 4, 4), :, :]
                ref[blocks, 2 * BROWS :, 2 * LANES :] = jnp.zeros((4, SMALL, D - 2 * LANES), bf16)


def self_input_kernel(dqt, dk, dv, d1, wa, dtok):
    dtok[...] = (
        d1[...]
        + dot(dqt[...], square(wa, 0), 0, 1)
        + dot(dk[...], square(wa, 1), 1, 1)
        + dot(dv[...], square(wa, 2), 1, 1)
    ).astype(bf16)


def pick_kernel(count, places, *refs):
    arrays, outs, sems = refs[:count], refs[count : 5 * count], refs[5 * count]
    copies = []
    for n, array in enumerate(arrays):
        for k in range(PIECES):
            copies.append(
                pltpu.make_async_copy(array.at[places[k]], outs[n * PIECES + k], sems.at[n, k])
            )
    for copy in copies:
        copy.start()
    for copy in copies:
        copy.wait()


def unpack_kernel(info, blocks, out):
    unpack_into(info, pl.program_id(0), blocks, out)


def plus(*parts):
    total = parts[0].astype(f32)
    for part in parts[1:]:
        total = total + part.astype(f32)
    return total


def route_one_kernel(info, keep, recv, a_keep, a_send, b_keep, b_send):
    x, y = info[CORE + 1], info[CORE + 2]
    for n in range(2):
        for ref, own in ((a_keep, x), (a_send, 1 - x)):
            at = (2 * n + own) * 4
            ref[n] = plus(keep[pl.ds(at, 2)], recv[pl.ds(at, 2)]).astype(bf16)
        for ref, own in ((b_keep, y), (b_send, 1 - y)):
            at = (2 * own + n) * 4 + 2
            ref[n] = plus(keep[pl.ds(at, 2)], recv[pl.ds(at, 2)]).astype(bf16)


def route_two_kernel(info, a, ra, b, rb, a_keep, a_send, b_keep, b_send):
    x, y = info[CORE + 1], info[CORE + 2]
    for ref, own in ((a_keep, y), (a_send, 1 - y)):
        ref[...] = plus(a[own], ra[own]).astype(bf16)
    for ref, own in ((b_keep, x), (b_send, 1 - x)):
        ref[...] = plus(b[own], rb[own]).astype(bf16)


def route_three_kernel(info, a, ra, b, rb, o0, o1, o2, o3, total):
    total[0:2] = plus(a[...], ra[...]).astype(bf16)
    total[2:4] = plus(b[...], rb[...]).astype(bf16)
    for k, ref in enumerate((o0, o1, o2, o3)):
        ref[...] = total[lax.rem(info[3 * SEQS] + k, PIECES)]


def route_four_kernel(r0, r1, r2, r3, out):
    out[...] = plus(r0[...], r1[...], r2[...], r3[...])


SMEM = pl.BlockSpec(memory_space=pltpu.SMEM)
WHOLE = pl.BlockSpec(memory_space=pltpu.VMEM)
ROWS = pl.BlockSpec((PIECE, D), lambda i: (i, 0))
COLS = pl.BlockSpec((D, PIECE), lambda i: (0, i))
BLOCKS_IN = pl.BlockSpec(
    (PIECES, PIECE, D), lambda i: (0, 0, 0), pipeline_mode=pl.Buffered(buffer_count=1)
)
BATCH = pl.BlockSpec((1, PIECE, D), lambda i: (jnp.minimum(i, MICRO - 1), 0, 0))
ROWS_Q = pl.BlockSpec((QB, D), lambda i: (i, 0))
COLS_Q = pl.BlockSpec((D, QB), lambda i: (0, i))
HEADS_Q = pl.BlockSpec((HEADS, QB), lambda i: (0, i))
OUT_W = pl.BlockSpec(
    (BLOCKS // 4, BROWS, D), lambda i: (3, 0, 0), pipeline_mode=pl.Buffered(buffer_count=1)
)
ROWS_F = pl.BlockSpec((FR, D), lambda i: (i, 0))
COLS_F = pl.BlockSpec((D, FR), lambda i: (0, i))
ONES = pl.BlockSpec((PIECE, 1), lambda i: (i, 0))


def fixed(*shape):
    return pl.BlockSpec(
        shape, lambda i: (0,) * len(shape), pipeline_mode=pl.Buffered(buffer_count=1)
    )


def shape(dims, dtype=bf16):
    return jax.ShapeDtypeStruct(dims, dtype)


def call(kernel, name, grid, in_specs, out_specs, out_shape, scratch, flops, *args):
    return pl.pallas_call(
        kernel,
        grid=grid,
        in_specs=in_specs,
        out_specs=out_specs,
        out_shape=out_shape,
        scratch_shapes=scratch,
        name=name,
        compiler_params=pltpu.CompilerParams(vmem_limit_bytes=VMEM_LIMIT),
        cost_estimate=pl.CostEstimate(flops=flops, bytes_accessed=8 << 20, transcendentals=0),
    )(*args)


ROWMAJOR = shape((GROUP, D))
COLMAJOR = shape((D, GROUP))


def project_rows(info, pieces, weights, kind):
    outs = [ROWMAJOR] + ([COLMAJOR] if kind else []) + [ROWMAJOR, ROWMAJOR]
    w_specs = [WHOLE]
    if kind == 2:
        outs = outs + [shape((BLOCKS,) + weights[1].shape[1:])]
        w_specs = [SMEM, WHOLE, WHOLE]
    elif kind == 0:
        w_specs = [fixed(BLOCKS, BROWS, D)]
    return call(
        functools.partial(project_kernel, kind),
        "project",
        (1,),
        [SMEM] + [WHOLE] * PIECES + w_specs,
        [WHOLE] * len(outs),
        outs,
        [],
        4 << 30,
        info,
        *pieces,
        *weights,
    )


def saved_rows(cross):
    return MEM_LEN if cross else KEPT + KB // 2


def attend(info, qt, k, v, cross):
    keep = (HEADS, saved_rows(cross), QB)
    return call(
        functools.partial(attend_kernel, cross),
        "attend",
        (GROUP // QB,),
        [SMEM, COLS_Q, fixed(GROUP, D), fixed(GROUP, D)],
        [COLS_Q, HEADS_Q, SMEM, pl.BlockSpec((1,) + keep, lambda i: (i, 0, 0, 0))],
        [
            COLMAJOR,
            shape((HEADS, GROUP), f32),
            shape((GROUP // QB,), jnp.int32),
            shape((GROUP // QB,) + keep),
        ],
        [
            pltpu.VMEM((D, GROUP), bf16),
            pltpu.VMEM((HEADS, QB), f32),
            pltpu.VMEM((HEADS, QB), f32),
            pltpu.VMEM((HEADS, QB), f32),
            pltpu.VMEM((D, QB), f32),
            pltpu.VMEM((KB, QB), f32),
        ],
        30 << 30,
        info,
        qt,
        k,
        v,
    )


def attend_back(info, qt, k, v, g, ot, lse, flags, saved, cross):
    keep = (HEADS, saved_rows(cross), QB)
    return call(
        functools.partial(attend_back_kernel, cross),
        "attend_back",
        (GROUP // QB,),
        [SMEM, SMEM, COLS_Q, fixed(GROUP, D), fixed(GROUP, D), ROWS_Q, COLS_Q, HEADS_Q]
        + [pl.BlockSpec((1,) + keep, lambda i: (i, 0, 0, 0))],
        [COLS_Q, fixed(GROUP, D), fixed(GROUP, D)],
        [COLMAJOR, ROWMAJOR, ROWMAJOR],
        [
            pltpu.VMEM((D, GROUP), bf16),
            pltpu.VMEM((D, QB), f32),
            pltpu.VMEM((GROUP, D), f32),
            pltpu.VMEM((GROUP, D), f32),
            pltpu.VMEM((D, QB), bf16),
            pltpu.VMEM((HEADS // 2, 2 * QB, 2 * HEAD_DIM), bf16),
            pltpu.VMEM((HEADS // 2, 2 * QB, 2 * HEAD_DIM), bf16),
            pltpu.VMEM((KB, QB), f32),
        ],
        60 << 30,
        info,
        flags,
        qt,
        k,
        v,
        g,
        ot,
        lse,
        saved,
    )


ANY = pl.BlockSpec(memory_space=pl.ANY)


def pick_four(arrays, places):
    n = len(arrays)
    outs = call(
        functools.partial(pick_kernel_args, n),
        "pick",
        (),
        [SMEM] + [ANY] * n,
        [WHOLE] * (PIECES * n),
        [shape(a.shape[1:], a.dtype) for a in arrays for _ in range(PIECES)],
        [pltpu.SemaphoreType.DMA((n, PIECES))],
        1 << 20,
        places,
        *arrays,
    )
    return [list(outs[PIECES * m : PIECES * (m + 1)]) for m in range(n)]


def pick_kernel_args(count, places, *refs):
    pick_kernel(count, places, *refs)


def unpack(info, blocks, micro):
    return call(
        unpack_kernel,
        "unpack",
        (micro,),
        [SMEM, BLOCKS_IN],
        BATCH,
        shape((micro, PIECE, D), f32),
        [],
        1 << 20,
        info,
        blocks,
    )


def route_one(info, keep, recv):
    half = shape((2, 2) + keep.shape[1:])
    return call(
        route_one_kernel, "route_one", (), [SMEM, WHOLE, WHOLE], [WHOLE] * 4, [half] * 4, [], 1 << 20,
        info, keep, recv,
    )


def route_two(info, a, ra, b, rb):
    half = shape(a.shape[1:])
    return call(
        route_two_kernel, "route_two", (), [SMEM] + [WHOLE] * 4, [WHOLE] * 4, [half] * 4, [], 1 << 20,
        info, a, ra, b, rb,
    )


def route_three(info, a, ra, b, rb):
    block = a.shape[1:]
    return call(
        route_three_kernel, "route_three", (), [SMEM] + [WHOLE] * 4, [WHOLE] * 4,
        [shape(block)] * 4, [pltpu.VMEM((4,) + block, bf16)], 1 << 20,
        info, a, ra, b, rb,
    )


def route_last_kernel(r0, r1, r2, r3, own, cross, gain, bias, out_bias, in_bias):
    def rows(first, count):
        part = slice(first, first + count)
        return plus(r0[part, :], r1[part, :], r2[part, :], r3[part, :])

    own[...] = rows(0, BROWS)
    cross[...] = rows(BROWS, BROWS)
    small = rows(2 * BROWS, SMALL)
    turned = small[:, :LANES].T
    gain[...] = turned[0:3]
    bias[...] = turned[3:6]
    out_bias[...] = turned[6:7]
    in_bias[...] = small[0:1, LANES : LANES + BROWS]


def route_last(pieces, rows, out_rows):
    outs = [(rows, D), (rows, D), (3, out_rows), (3, out_rows), (1, out_rows), (1, rows)]
    return call(
        route_last_kernel, "route_last", (), [WHOLE] * 4, [WHOLE] * 6, [shape(o, f32) for o in outs], [],
        1 << 20, *pieces,
    )


def route_four(pieces):
    return call(
        route_four_kernel, "route_four", (), [WHOLE] * 4, WHOLE, shape(pieces[0].shape, f32), [], 1 << 20,
        *pieces,
    )


def tie(value, *deps):
    return lax.optimization_barrier((value, deps))[0]


def dp_swap(array, bit):
    n = lax.axis_size("dp")
    return lax.ppermute(array, "dp", [(d, d ^ bit) for d in range(n)])


def turns(arrays):
    n = lax.axis_size("fsdp")
    return [arrays[0]] + [
        lax.ppermute(arrays[k], "fsdp", [(m, (m + k) % n) for m in range(n)])
        for k in range(1, len(arrays))
    ]


def local(
    tokens, memory, cotangent, lengths, seq_order, memory_pick,
    self_attn, cross_attn, ffn_in, ffn_in_bias, ffn_out, ffn_out_bias, norm_gain, norm_bias,
):
    axes = ("dp", "fsdp")
    n_dp, members = lax.axis_size("dp"), lax.axis_size("fsdp")
    micro = tokens.shape[0]
    owners = n_dp * members
    dp, z = lax.axis_index("dp"), lax.axis_index("fsdp")

    def offset(d):
        return d % 2 if micro < members else 0

    def unit_at(d, member):
        return member - offset(d)

    mine = unit_at(dp, z)
    valid = (mine >= 0) & (mine < micro)
    unit = jnp.clip(mine, 0, micro - 1)

    def pairs(k):
        out = []
        for d in range(n_dp):
            for source in range(members):
                target = (source + k) % members
                if 0 <= unit_at(d, target) < micro:
                    out.append((d * members + source, d * members + target))
        return out

    def to_unit(pieces):
        return [pieces[0]] + [
            lax.ppermute(pieces[k], axes, pairs(k)) for k in range(1, members)
        ]

    def from_unit(rows_of_unit):
        blocks = rows_of_unit.reshape(members, PIECE, D)
        return lax.all_to_all(blocks, "fsdp", split_axis=0, concat_axis=0)

    def row_of(array):
        return lax.dynamic_index_in_dim(array, unit, 0, False)[0]

    boxed = n_dp == 8 and members == 4
    shifts = jnp.arange(members, dtype=jnp.int32)

    targets = jnp.clip(lax.rem(z + shifts, members) - offset(dp), 0, micro - 1)
    sources = jnp.arange(micro, dtype=jnp.int32) + offset(dp)
    targets = targets.at[0].set(unit).astype(jnp.int32)

    bits = [dp & 1, (dp >> 1) & 1, (dp >> 2) & 1] if boxed else [jnp.zeros_like(dp)] * 3
    info = jnp.concatenate(
        [
            row_of(lengths),
            row_of(seq_order),
            row_of(memory_pick),
            jnp.stack([z, valid.astype(jnp.int32), *bits]),
            sources,
        ]
    ).astype(jnp.int32)

    smalls = jnp.concatenate(
        [ffn_in_bias, ffn_out_bias, norm_gain.T.reshape(-1), norm_bias.T.reshape(-1)]
    )
    rows = self_attn.shape[0]
    in_rows = ffn_in.shape[0]
    n_smalls = smalls.shape[0]
    token_slices = pick_four([tokens], targets)[0]
    smalls = tie(smalls, token_slices)
    small_row = jnp.pad(smalls, (0, 16 * D - n_smalls)).reshape(16, D)
    bundle_a = jnp.concatenate([self_attn, small_row], axis=0)
    in_blocks = ffn_in.reshape(in_rows, 4, D).transpose(1, 0, 2).reshape(4 * in_rows, D)
    bundle_b = jnp.concatenate([cross_attn, ffn_out, in_blocks], axis=0)
    if boxed:
        turned = turns([bundle_a] * members)
    token_pieces = to_unit(token_slices)
    late = tie([memory, cotangent], token_slices)
    memory_slices, cotangent_slices = pick_four(late, targets)
    if boxed:
        a0, b0 = jnp.stack(turned[:2]), jnp.stack(turned[2:])
        a1, b1 = dp_swap(a0, 2), dp_swap(b0, 4)
        a2 = dp_swap(jnp.stack([a0, a1]), 4)
        b2 = dp_swap(jnp.stack([b0, b1]), 2)
        near = jnp.concatenate([a0, a1, a2[0], a2[1], b0, b1, b2[0], b2[1]])
        masks = jnp.array([0, 0, 2, 2, 4, 4, 6, 6, 0, 0, 4, 4, 2, 2, 6, 6], jnp.int32)
        steps = jnp.array([0, 1] * 4 + [2, 3] * 4, jnp.int32)
        owner = (dp ^ masks) * members + lax.rem(z - steps + members, members)
        places = jnp.concatenate([owner, owner ^ members]).astype(jnp.int32)
        near = tie(near, token_pieces[1:], memory_slices, cotangent_slices, info, places)
        far = dp_swap(near, 1)
    else:
        all_a = lax.all_gather(bundle_a, axes, axis=0, tiled=False)
        wa = jnp.pad(all_a[:, :rows].reshape(BLOCKS, BROWS, D), ((0, 0), (0, SMALL), (0, 0)))
    all_b = lax.all_gather(tie(bundle_b, token_slices), axes, axis=0, tiled=False)
    def blocked(array, count):
        return array.reshape(BLOCKS, count, D)

    if owners == BLOCKS:
        wb = all_b
    else:
        first = all_b[:, 2 * rows :].reshape(owners, 4, in_rows, D).transpose(1, 0, 2, 3)
        first = first.reshape(4, BLOCKS, BROWS // 4, D).transpose(1, 0, 2, 3)
        wb = jnp.concatenate(
            [
                blocked(all_b[:, :rows], BROWS),
                blocked(all_b[:, rows : 2 * rows], BROWS),
                blocked(first, BROWS),
            ],
            axis=1,
        )
    if boxed:
        x, qt, k, v, wa = project_rows(info, token_pieces, (places, near, far), 2)
        all_a = wa
    else:
        x, qt, k, v = project_rows(info, token_pieces, (wa,), 1)
    small = all_a[:, rows, :n_smalls].astype(f32)
    out_rows = D // owners
    b1 = small[:, :rows].reshape(1, FF)
    at = rows + out_rows
    vec_rows = [small[:, at + n * out_rows : at + (n + 1) * out_rows].reshape(1, D) for n in range(6)]
    vecs = jnp.concatenate(
        vec_rows + [small[:, rows:at].reshape(1, D), jnp.zeros((1, D), f32)], axis=0
    )

    memory_pieces = to_unit(tie(memory_slices, x))
    ot, *self_saved = attend(info, qt, k, v, False)
    ot = tie(ot, *memory_pieces[1:])
    cotangent_pieces = to_unit(tie(cotangent_slices, memory_pieces[1:], ot))
    n1, inv1, qct = call(
        first_norm_kernel,
        "first_norm",
        (PIECES,),
        [COLS, ROWS, OUT_W, fixed(BLOCKS, BROWS, D), fixed(8, D)],
        [ROWS, ONES, COLS],
        [shape((GROUP, D), f32), shape((GROUP, 1), f32), COLMAJOR],
        [],
        2 << 30,
        ot,
        x,
        wa,
        wb,
        vecs,
    )
    mem, kc, vc = project_rows(info, memory_pieces, (wb,), 0)
    oct_, *cross_saved = attend(info, qct, kc, vc, True)
    y_out, d2, gc, keep_ffn, send_ffn, g_co, g_b1, g_vec = call(
        ffn_kernel,
        "ffn",
        (GROUP // FR,),
        [SMEM, COLS_F, ROWS_F, fixed(BLOCKS, 3 * BROWS, D), fixed(8, D), fixed(1, FF)]
        + [fixed(PIECE, D)] * 4,
        [
            fixed(GROUP, D),
            ROWS_F,
            ROWS_F,
            fixed(HALF, 2 * BROWS, D),
            fixed(HALF, 2 * BROWS, D),
            fixed(D, D),
            fixed(1, FF),
            fixed(8, D),
        ],
        [
            ROWMAJOR,
            shape((GROUP, D), f32),
            ROWMAJOR,
            shape((HALF, 2 * BROWS, D)),
            shape((HALF, 2 * BROWS, D)),
            shape((D, D)),
            shape((1, FF), f32),
            shape((8, D), f32),
        ],
        [
            pltpu.VMEM((GROUP, D), bf16),
            pltpu.VMEM((FR, FF), bf16),
            pltpu.VMEM((FR, FF), f32),
            pltpu.VMEM((FR, D), f32),
            pltpu.VMEM((4, D, D), f32),
            pltpu.VMEM((FF, D), f32),
            pltpu.VMEM((D, D), f32),
            pltpu.VMEM((GROUP, D), f32),
        ],
        32 << 30,
        info,
        oct_,
        n1,
        wb,
        vecs,
        b1,
        *cotangent_pieces,
    )
    y_pieces = from_unit(y_out)
    if boxed:
        ffn_a, send_a, ffn_b, send_b = route_one(info, keep_ffn, dp_swap(send_ffn, 1))
        recv_a, recv_b = dp_swap(send_a, 2), dp_swap(send_b, 4)
        gc = tie(gc, send_a)

    dqct, dkc, dvc = attend_back(info, qct, kc, vc, gc, oct_, *cross_saved, True)
    if boxed:
        recv_a, recv_b, ffn_a, ffn_b = tie((recv_a, recv_b, ffn_a, ffn_b), dqct)
        ffn_a, send_a, ffn_b, send_b = route_two(info, ffn_a, recv_a, ffn_b, recv_b)
        recv_a, recv_b = dp_swap(send_a, 4), dp_swap(send_b, 2)
        g_co = tie(g_co, send_a)
    layer_output, *m_and_rest = call(
        cross_post_kernel,
        "cross_post",
        (PIECES,),
        [SMEM, BLOCKS_IN, COLS, ROWS, ROWS, ROWS, ROWS, ROWS, ONES, COLS]
        + [OUT_W, fixed(BLOCKS, BROWS, D), fixed(8, D), fixed(D, D)],
        [BATCH, ROWS, ROWS, ROWS, fixed(4 * D, D), fixed(D, D), fixed(8, D)],
        [
            shape((micro, PIECE, D), f32),
            ROWMAJOR,
            shape((GROUP, D), f32),
            ROWMAJOR,
            shape((4 * D, D)),
            shape((D, D)),
            shape((8, D), f32),
        ],
        [pltpu.VMEM((D, D), f32)] * 4,
        9 << 30,
        info,
        y_pieces,
        dqct,
        dkc,
        dvc,
        mem,
        d2,
        n1,
        inv1,
        ot,
        wa,
        wb,
        vecs,
        g_co,
    )
    m_out, d1, go, g_cross, g_wo, g_vec_one = m_and_rest
    m_pieces = from_unit(m_out)
    if boxed:
        recv_a, recv_b, ffn_a, ffn_b = tie((recv_a, recv_b, ffn_a, ffn_b), d1)
        ffn_pieces = turns(route_three(info, ffn_a, recv_a, ffn_b, recv_b))
        go = tie(go, ffn_pieces[0])
    g_vec = g_vec + g_vec_one
    if boxed:
        columns = g_vec.reshape(8, BLOCKS, SMALL).transpose(1, 2, 0)
        columns = jnp.pad(columns, ((0, 0), (0, 0), (0, LANES - 8)))
        first = jnp.pad(g_b1.reshape(BLOCKS, 1, rows), ((0, 0), (0, SMALL - 1), (0, LANES - rows)))
        g_small = jnp.concatenate([columns, first], axis=2).astype(bf16)
    else:
        g_small = jnp.zeros((BLOCKS, SMALL, 2 * LANES), bf16)
        small_grads = jnp.concatenate(
            [g_b1.reshape(owners, rows), g_vec[6].reshape(owners, out_rows)]
            + [g_vec[n].reshape(owners, out_rows) for n in range(6)],
            axis=1,
        )
    dqt, dk, dv = attend_back(info, qt, k, v, go, ot, *self_saved, False)
    x_late = x
    if boxed:
        ffn_part = route_four(tie(ffn_pieces, dqt))
        d1 = tie(d1, ffn_part)
    last_rows = 2 * BROWS + SMALL
    t_out = call(
        self_input_kernel,
        "self_input",
        (PIECES,),
        [COLS, ROWS, ROWS, ROWS, fixed(3 * BLOCKS // 4, BROWS, D)],
        ROWS,
        ROWMAJOR,
        [],
        4 << 30,
        dqt,
        dk,
        dv,
        d1,
        wa,
    )
    t_pieces = from_unit(t_out)
    x_late = tie(x_late, t_out)
    memory_grad, keep_last, send_last = call(
        self_grad_kernel,
        "self_grad",
        (PIECES,),
        [SMEM, BLOCKS_IN, COLS, ROWS, ROWS, ROWS, fixed(D, D), fixed(4 * D, D), fixed(BLOCKS, SMALL, 2 * LANES)],
        [BATCH] + [fixed(HALF, last_rows, D)] * 2,
        [shape((micro, PIECE, D), f32)] + [shape((HALF, last_rows, D))] * 2,
        [pltpu.VMEM((D, D), f32)] * 3,
        4 << 30,
        info,
        m_pieces,
        dqt,
        dk,
        dv,
        x_late,
        g_wo,
        g_cross,
        g_small,
    )
    if boxed:
        recv_last = dp_swap(send_last, 1)
        near, send_a, far, send_b = route_one(info, keep_last, recv_last)
        recv_a, recv_b = dp_swap(send_a, 2), dp_swap(send_b, 4)

    def whole_blocks(keep, send):
        both = jnp.stack([keep, send]).reshape(2, 4, 4, -1, D)
        return both.transpose(1, 0, 2, 3, 4).reshape(BLOCKS, -1, D)

    def owned(array):
        return lax.psum_scatter(array, axes, scatter_dimension=0, tiled=True)[0].astype(f32)

    if boxed:
        recv_a = tie(recv_a, t_pieces)
        near, send_a, far, send_b = route_two(info, near, recv_a, far, recv_b)
        recv_a, recv_b = dp_swap(send_a, 4), dp_swap(send_b, 2)
        input_grad = unpack(info, t_pieces, micro)
        last_pieces = turns(route_three(info, near, recv_a, far, recv_b))
        self_attn_grad, cross_attn_grad, gain_grad, bias_grad, out_bias, in_bias = route_last(
            last_pieces, rows, out_rows
        )
    else:
        input_grad = unpack(info, t_pieces, micro)
        ffn = whole_blocks(keep_ffn, send_ffn)
        second = ffn[:, BROWS:].reshape(owners, rows, D)
        first = ffn[:, :BROWS].reshape(BLOCKS, 4, BROWS // 4, D).transpose(1, 0, 2, 3)
        first = first.reshape(4, owners, in_rows, D).transpose(1, 0, 2, 3)
        ffn_part = owned(jnp.concatenate([first.reshape(owners, rows, D), second], axis=1))
        rest = whole_blocks(keep_last, send_last)
        self_attn_grad = owned(rest[:, :BROWS].reshape(owners, rows, D))
        cross_attn_grad = owned(rest[:, BROWS : 2 * BROWS].reshape(owners, rows, D))
        small_out = owned(small_grads)
        at = rows + out_rows
        norm_part = small_out[at : at + 6 * out_rows].reshape(6, out_rows)
        gain_grad, bias_grad = norm_part[:3], norm_part[3:]
        in_bias, out_bias = small_out[:rows], small_out[rows:at]
    ffn_in_grad = ffn_part[:rows].reshape(4, in_rows, D).transpose(1, 0, 2).reshape(in_rows, FF)
    return (
        layer_output,
        input_grad,
        memory_grad,
        self_attn_grad,
        cross_attn_grad,
        ffn_in_grad,
        in_bias.reshape(rows),
        ffn_part[rows:],
        out_bias.reshape(out_rows),
        gain_grad.T,
        bias_grad.T,
    )


def solution(mesh):
    rows = P(None, ("dp", "fsdp"), None)
    group = P(None, "dp", None)
    shard = P(("dp", "fsdp"), None)
    flat = P(("dp", "fsdp"))
    in_specs = (rows,) * 3 + (group,) * 3 + (shard, shard, shard, flat, shard, flat, shard, shard)
    out_specs = (rows,) * 3 + (shard, shard, shard, flat, shard, flat, shard, shard)
    return jax.shard_map(local, mesh=mesh, in_specs=in_specs, out_specs=out_specs, check_vma=False)
```

```python
import functools
import math

import jax
import jax.numpy as jnp
from jax import lax
from jax.experimental import pallas as pl
from jax.experimental.pallas import tpu as pltpu
from jax.sharding import PartitionSpec as P

D = 512
HEADS = 8
HEAD_DIM = 64
FF = 2048
MEM_LEN = 1024
SEQS = 4
NMEM = 2
GROUP = 2048
PIECE = 512
PIECES = GROUP // PIECE
QB = 256
KB = 512
FR = 512
LANES = 128
KEPT = 1024
NEG = -1e30
BLOCKS = 32
BROWS = D * 4 // BLOCKS
bf16 = jnp.bfloat16
f32 = jnp.float32
VMEM_LIMIT = 58 << 20
CORE = 3 * SEQS + 2
HALF = BLOCKS // 2
SMALL = 16
MICRO = 3
SOURCES = 3 * SEQS + 5


def dot(left, right, cl=1, cr=0):
    return lax.dot_general(
        left, right, (((cl,), (cr,)), ((), ())), preferred_element_type=f32
    )


def place_ends(info):
    ends, total = [], 0
    for j in range(SEQS):
        total = total + info[info[SEQS + j]]
        ends.append(total)
    return ends


def place_picks(info):
    return [info[2 * SEQS + info[SEQS + j]] for j in range(SEQS)]


def place_shifts(info, ends):
    shifts = []
    for j in range(SEQS):
        seq = info[SEQS + j]
        start = 0
        for s in range(SEQS):
            start = start + jnp.where(s < seq, info[s], 0)
        shifts.append(start - (ends[j - 1] if j else 0))
    return shifts


def by_place(rows, ends, values):
    out = jnp.full(rows.shape, values[0], jnp.int32)
    for j in range(SEQS - 1):
        out = jnp.where(rows >= ends[j], values[j + 1], out)
    return out


def piece_row(info, k):
    return pl.multiple_of(lax.rem(info[3 * SEQS] - k + PIECES, PIECES) * PIECE, PIECE)


def weight(ref, first, count, offset, rows):
    return ref[first : first + count, offset : offset + rows, :].reshape(count * rows, D)


def square(ref, index, offset=0):
    per = BLOCKS // 4
    return weight(ref, index * per, per, offset, BROWS)


def project_kernel(kind, info, x0, x1, x2, x3, *refs):
    with_query = kind > 0
    if kind == 2:
        places, near, far, x_out, qt_out, k_out, v_out, w = refs
        for n in range(HALF):
            w[pl.ds(places[n], 1)] = near[n : n + 1]
            w[pl.ds(places[HALF + n], 1)] = far[n : n + 1]
    elif kind == 1:
        w, x_out, qt_out, k_out, v_out = refs
    else:
        w, x_out, k_out, v_out = refs
    if with_query:
        wq = square(w, 0)
    wk, wv = square(w, 1), square(w, 2)
    for k, piece in enumerate((x0, x1, x2, x3)):
        r0 = piece_row(info, k)
        rows = pl.ds(r0, PIECE)
        x = piece[...]
        x_out[rows, :] = x
        if with_query:
            q = dot(x, wq).astype(bf16) * jnp.asarray(HEAD_DIM**-0.5, bf16)
            qt_out[:, rows] = q.T
        k_out[rows, :] = dot(x, wk).astype(bf16)
        v_out[rows, :] = dot(x, wv).astype(bf16)


def memories_read(info, q0):
    ends, picks = place_ends(info), place_picks(info)
    rows = q0 + lax.broadcasted_iota(jnp.int32, (1, QB), 1)
    picked = by_place(rows, ends, picks)
    needs = []
    for mem in range(NMEM):
        need = jnp.bool_(False)
        for j in range(SEQS):
            start = ends[j - 1] if j else 0
            need = need | ((start < q0 + QB) & (ends[j] > q0) & (picks[j] == mem))
        needs.append(need)
    return needs, [picked == mem for mem in range(NMEM)]


def window(info, q0):
    ends = place_ends(info)
    rows = q0 + lax.broadcasted_iota(jnp.int32, (1, QB), 1)
    low, high = 0, GROUP
    low_row = jnp.zeros((1, QB), jnp.int32)
    high_row = jnp.full((1, QB), GROUP, jnp.int32)
    for j in range(SEQS - 1):
        low = jnp.where(q0 >= ends[j], ends[j], low)
        low_row = jnp.where(rows >= ends[j], ends[j], low_row)
    for j in reversed(range(SEQS - 1)):
        high = jnp.where(q0 + QB - 1 < ends[j], ends[j], high)
        high_row = jnp.where(rows < ends[j], ends[j], high_row)
    low = low // LANES * LANES
    many = (high - low) // KB
    rest = high - low - many * KB
    many = jnp.where(rest > KB // 2, many + 1, many)
    narrow = (rest > 0) & (rest <= KB // 2)

    def place(first, size):
        k0 = pl.multiple_of(jnp.minimum(first, GROUP - size), LANES)
        keys = k0 + lax.broadcasted_iota(jnp.int32, (size, QB), 0)
        inside = (keys >= jnp.maximum(low_row, first)) & (keys < high_row)
        return k0, jnp.where(inside, 0.0, NEG)

    return low, many, narrow, place


def loop(first, last, body):
    def step(j, carry):
        body(j)
        return carry

    lax.fori_loop(first, last, step, 0)


def head_rows(h):
    return slice(h * HEAD_DIM, (h + 1) * HEAD_DIM)


def pipelined(groups, *stages):
    for step in range(groups + len(stages) - 1):
        for lag, stage in enumerate(stages):
            if 0 <= step - lag < groups:
                stage(step - lag)


def attend_kernel(
    cross, info, qt, k, v, ot, lse, flags, saved, vt, top, total, peak, acc, bias_ref
):
    i = pl.program_id(0)
    q0 = pl.multiple_of(i * QB, QB)
    group = 2

    @pl.when(i == 0)
    def _():
        for c in range(GROUP // QB):
            vt[:, c * QB : (c + 1) * QB] = v[c * QB : (c + 1) * QB, :].T

    def tile(safe, k0, size, bias, allowed, slot):
        keys = pl.ds(k0, size)
        if bias is not None:
            bias_ref[:size, :] = bias
        totals = total[...]
        tops = top[...] if safe else None
        new_tops, new_totals, peaks = [], [], []
        scores, parts = {}, {}

        def score(g):
            heads = range(g * group, (g + 1) * group)
            scores[g] = [dot(k[keys, head_rows(h)], qt[head_rows(h), :]) for h in heads]

        def soften(g):
            parts[g] = []
            for n, s in enumerate(scores.pop(g)):
                h = g * group + n
                decay = None
                if bias is not None:
                    s = s + bias_ref[:size, :]
                if safe:
                    old = tops[h : h + 1]
                    new = jnp.maximum(old, jnp.max(s, axis=0, keepdims=True))
                    if allowed is not None:
                        new = jnp.where(allowed, new, old)
                    decay = jnp.exp(old - new)
                    new_tops.append(new)
                    s = s - new
                p = jnp.exp(s)
                part = jnp.sum(p, axis=0, keepdims=True)
                if allowed is not None:
                    peaks.append(part)
                    p = jnp.where(allowed, p, 0.0)
                    part = jnp.where(allowed, part, 0.0)
                before = totals[h : h + 1]
                new_totals.append((before * decay if safe else before) + part)
                low = p.astype(bf16)
                if slot is not None:
                    saved[0, h, pl.ds(slot, size), :] = low
                parts[g].append((decay, low))

        def mix(g):
            for n, (decay, p) in enumerate(parts.pop(g)):
                rows = head_rows(g * group + n)
                before = acc[rows, :]
                acc[rows, :] = (before * decay if safe else before) + dot(vt[rows, keys], p)

        pipelined(HEADS // group, score, soften, mix)
        if safe:
            top[...] = jnp.concatenate(new_tops, axis=0)
        elif peaks:
            peak[...] = jnp.maximum(peak[...], jnp.concatenate(peaks, axis=0))
        total[...] = jnp.concatenate(new_totals, axis=0)

    def sweep(safe):
        if safe:
            top[...] = jnp.full_like(top, NEG)
        else:
            peak[...] = jnp.zeros_like(peak)
        total[...] = jnp.zeros_like(total)
        acc[...] = jnp.zeros_like(acc)
        if cross:
            needs, allowed = memories_read(info, q0)
            both = needs[0] & needs[1]
            if safe:
                for mem in range(NMEM):

                    @pl.when(needs[mem])
                    def _():
                        tile(True, mem * MEM_LEN, MEM_LEN, None, allowed[mem], None)
            else:

                @pl.when(jnp.logical_not(both))
                def _():
                    first = pl.multiple_of(jnp.where(needs[0], 0, MEM_LEN), MEM_LEN)
                    tile(False, first, MEM_LEN, None, None, 0)

                @pl.when(both)
                def _():
                    tile(False, 0, MEM_LEN, None, allowed[0], 0)
                    tile(False, MEM_LEN, MEM_LEN, None, allowed[1], None)
        else:
            low, many, narrow, place = window(info, q0)

            def part(j, size, slot):
                k0, bias = place(low + j * KB, size)
                tile(safe, k0, size, bias, None, slot)

            kept = 0 if safe else jnp.minimum(many, KEPT // KB)
            if not safe:
                loop(0, kept, lambda j: part(j, KB, pl.multiple_of(j * KB, KB)))
            loop(kept, many, lambda j: part(j, KB, None))

            @pl.when(narrow)
            def _():
                part(many, KB // 2, None if safe else pl.multiple_of(kept * KB, KB))

        sums = total[...]
        inverse = 1.0 / sums
        lse[...] = jnp.log(sums) + (top[...] if safe else 0.0)
        for h in range(HEADS):
            ot[head_rows(h), :] = (acc[head_rows(h), :] * inverse[h : h + 1]).astype(bf16)

    sweep(False)
    sums = total[...]
    safe_range = (jnp.min(sums) > 1e-18) & (jnp.max(sums) < 1e18) & (jnp.max(peak[...]) < 1e18)
    flags[i] = safe_range.astype(jnp.int32)

    @pl.when(jnp.logical_not(safe_range))
    def _():
        sweep(True)


def attend_back_kernel(
    cross, info, flags, qt, k, v, g, ot, lse, saved, dqt, dk, dv,
    kt, dqt_acc, dk_acc, dv_acc, gt, gm, qm, bias_ref,
):
    i = pl.program_id(0)
    q0 = pl.multiple_of(i * QB, QB)
    group = 2
    shiftless = flags[i] > 0

    @pl.when(i == 0)
    def _():
        dk_acc[...] = jnp.zeros_like(dk_acc)
        dv_acc[...] = jnp.zeros_like(dv_acc)
        for c in range(GROUP // QB):
            kt[:, c * QB : (c + 1) * QB] = k[c * QB : (c + 1) * QB, :].T

    lses = lse[...]
    factor = jnp.where(shiftless, jnp.exp(-lses), 1.0)
    shifts = jnp.where(shiftless, 0.0, lses)
    weighted = []
    turned = g[...].T
    for h in range(HEADS):
        scaled = turned[head_rows(h), :].astype(f32) * factor[h : h + 1]
        weighted.append(
            jnp.sum(scaled * ot[head_rows(h), :].astype(f32), axis=0, keepdims=True)
        )
        gt[head_rows(h), :] = scaled.astype(bf16)
    left = lax.broadcasted_iota(jnp.int32, (QB, 2 * HEAD_DIM), 1) < HEAD_DIM
    for pair in range(HEADS // 2):
        cols = slice(pair * 2 * HEAD_DIM, (pair + 1) * 2 * HEAD_DIM)
        gp = gt[cols, :].T
        qp = qt[cols, :].T
        zero = jnp.zeros_like(gp)
        gm[pair, :QB, :] = jnp.where(left, gp, zero)
        gm[pair, QB:, :] = jnp.where(left, zero, gp)
        qm[pair, :QB, :] = jnp.where(left, qp, zero)
        qm[pair, QB:, :] = jnp.where(left, zero, qp)
    dqt_acc[...] = jnp.zeros_like(dqt_acc)

    def tile(k0, size, bias, allowed, slot):
        keys = pl.ds(k0, size)
        if bias is not None:
            bias_ref[:size, :] = bias
        bases = shifts if allowed is None else jnp.where(allowed, shifts, -NEG)
        scores, slopes, probs, grads = {}, {}, {}, {}

        def score(g):
            heads = range(g * group, (g + 1) * group)
            if slot is None:
                scores[g] = [dot(k[keys, head_rows(h)], qt[head_rows(h), :]) for h in heads]
            slopes[g] = [dot(v[keys, head_rows(h)], gt[head_rows(h), :]) for h in heads]

        def soften(g):
            probs[g], grads[g] = [], []
            for n, dp in enumerate(slopes.pop(g)):
                h = g * group + n
                if slot is None:
                    s = scores[g][n]
                    if bias is not None:
                        s = s + bias_ref[:size, :]
                    p = jnp.exp(s - bases[h : h + 1])
                    probs[g].append(p.astype(bf16))
                else:
                    probs[g].append(saved[0, h, pl.ds(slot, size), :])
                    p = probs[g][n].astype(f32)
                grads[g].append((p * (dp - weighted[h])).astype(bf16))

        def mix(g):
            for n in range(0, group, 2):
                pair = (g * group + n) // 2
                cols = slice(pair * 2 * HEAD_DIM, (pair + 1) * 2 * HEAD_DIM)
                dv_acc[keys, cols] += dot(jnp.concatenate(probs[g][n : n + 2], axis=1), gm[pair])
                dk_acc[keys, cols] += dot(jnp.concatenate(grads[g][n : n + 2], axis=1), qm[pair])
            for n, ds in enumerate(grads[g]):
                rows = head_rows(g * group + n)
                dqt_acc[rows, :] += dot(kt[rows, keys], ds)

        pipelined(HEADS // group, score, soften, mix)

    if cross:
        needs, allowed = memories_read(info, q0)

        @pl.when(shiftless)
        def _():
            first = pl.multiple_of(jnp.where(needs[0], 0, MEM_LEN), MEM_LEN)
            tile(first, MEM_LEN, None, None, 0)

        for mem in range(NMEM):
            done = shiftless & (jnp.logical_not(needs[0]) if mem else True)

            @pl.when(needs[mem] & jnp.logical_not(done))
            def _():
                tile(mem * MEM_LEN, MEM_LEN, None, allowed[mem], None)
    else:
        low, many, narrow, place = window(info, q0)

        def part(j, size, slot):
            k0, bias = place(low + j * KB, size)
            tile(k0, size, bias if slot is None else None, None, slot)

        kept = jnp.where(shiftless, jnp.minimum(many, KEPT // KB), 0)
        loop(0, kept, lambda j: part(j, KB, pl.multiple_of(j * KB, KB)))
        loop(kept, many, lambda j: part(j, KB, None))

        @pl.when(narrow & shiftless)
        def _():
            part(many, KB // 2, pl.multiple_of(kept * KB, KB))

        @pl.when(narrow & jnp.logical_not(shiftless))
        def _():
            part(many, KB // 2, None)

    dqt[...] = (dqt_acc[...] * HEAD_DIM**-0.5).astype(bf16)

    @pl.when(i == pl.num_programs(0) - 1)
    def _():
        dk[...] = dk_acc[...].astype(bf16)
        dv[...] = dv_acc[...].astype(bf16)


def norm(resid):
    center = resid - jnp.mean(resid, axis=-1, keepdims=True)
    inv = lax.rsqrt(jnp.mean(center * center, axis=-1, keepdims=True) + 1e-06)
    return center * inv, inv


def norm_back(grad, normed, inv, gain):
    scaled = grad * gain
    return inv * (
        scaled
        - jnp.mean(scaled, axis=-1, keepdims=True)
        - normed * jnp.mean(scaled * normed, axis=-1, keepdims=True)
    )


def column_sum(value):
    return jnp.sum(value, axis=0, keepdims=True)


def first_norm_kernel(ot, x, wa, wb, vecs, n1, inv1, qct):
    resid = x[...].astype(f32) + dot(ot[...], square(wa, 0), 0, 0)
    normed, inv = norm(resid)
    n1[...] = normed
    inv1[...] = inv
    hidden = (normed * vecs[0:1, :] + vecs[3:4, :]).astype(bf16)
    q = dot(hidden, square(wb, 0)).astype(bf16) * jnp.asarray(HEAD_DIM**-0.5, bf16)
    qct[...] = q.T


def ffn_kernel(
    info, oct_, n1, wo, wf, vecs, b1, c0, c1, c2, c3,
    yg, d2, gc, keep_ffn, send_ffn, g_co, g_b1, g_vec,
    act, pre, hid, third, slope, dy, gw, gco,
):
    i = pl.program_id(0)

    @pl.when(i == 0)
    def _():
        for ref in (gco, g_b1, g_vec, yg):
            ref[...] = jnp.zeros_like(ref)

    rows_here = pl.ds(pl.multiple_of(i * FR, FR), FR)
    chunk = BROWS // 4

    def w1(c):
        return weight(wf, 0, BLOCKS, BROWS + c * chunk, chunk)

    def w2(c):
        per = BLOCKS // 4
        return weight(wf, c * per, per, 0, BROWS)

    hidden_one = n1[...] * vecs[0:1, :] + vecs[3:4, :]
    n2, inv2 = norm(hidden_one + dot(oct_[...], square(wo, 0), 0, 0))
    hidden = n2 * vecs[1:2, :] + vecs[4:5, :]
    hidden_b = hidden.astype(bf16)

    factor = math.sqrt(2.0 / math.pi)
    cubic = 0.044715 * factor
    ups, acts, outs = {}, {}, []

    def cols(c):
        return slice(c * D, (c + 1) * D)

    def up(c):
        ups[c] = dot(hidden_b, w1(c))

    def bend(c):
        u = ups.pop(c) + b1[0:1, cols(c)]
        sq = u * u
        t = jnp.tanh(u * (factor + cubic * sq))
        half = 0.5 + 0.5 * t
        acts[c] = (u * half).astype(bf16)
        act[rows_here, cols(c)] = acts[c]
        slope[:, cols(c)] = half + u * (1.0 - t * t) * (0.5 * factor + 1.5 * cubic * sq)

    def down(c):
        outs.append(dot(acts.pop(c), w2(c)))

    pipelined(4, up, bend, down)
    out = (outs[0] + outs[1]) + (outs[2] + outs[3])
    n3, inv3 = norm(hidden + (out + vecs[6:7, :]))
    y = (n3 * vecs[2:3, :] + vecs[5:6, :]).astype(bf16)

    ends = place_ends(info)
    shifts = place_shifts(info, ends)
    p0 = i * FR
    rows = p0 + lax.broadcasted_iota(jnp.int32, (FR, 1), 0)
    given = rows + by_place(rows, ends, shifts)
    dy[...] = jnp.zeros_like(dy)

    for k, piece in enumerate((c0, c1, c2, c3)):
        r0 = piece_row(info, k)
        hit = jnp.bool_(False)
        for j in range(SEQS):
            begin = jnp.maximum(ends[j - 1] if j else 0, p0)
            end = jnp.minimum(ends[j], p0 + FR)
            hit = hit | (
                (begin < end) & (begin + shifts[j] < r0 + PIECE) & (end + shifts[j] > r0)
            )

        @pl.when(hit)
        def _():
            columns = r0 + lax.broadcasted_iota(jnp.int32, (FR, PIECE), 1)
            select = jnp.where(columns == given, 1.0, 0.0).astype(bf16)
            dy[...] += dot(select, piece[...])
            yg[pl.ds(r0, PIECE), :] += dot(select, y, 0, 0).astype(bf16)

    grad = dy[...]
    g_vec[2:3, :] += column_sum(grad * n3)
    g_vec[5:6, :] += column_sum(grad)
    d3 = norm_back(grad, n3, inv3, vecs[2:3, :])
    df = d3.astype(bf16)
    hid[rows_here, :] = hidden_b
    third[rows_here, :] = df
    g_vec[6:7, :] += column_sum(df.astype(f32))
    downs, dus, backs = {}, {}, [d3]

    def down_back(c):
        downs[c] = dot(df, w2(c), 1, 1)

    def bend_back(c):
        dus[c] = (downs.pop(c) * slope[:, cols(c)]).astype(bf16)
        g_b1[0:1, cols(c)] += column_sum(dus[c].astype(f32))

    def up_back(c):
        du = dus.pop(c)
        pre[rows_here, cols(c)] = du
        backs.append(dot(du, w1(c), 1, 1))

    pipelined(4, down_back, bend_back, up_back)
    back = ((backs[0] + backs[1]) + (backs[2] + backs[3])) + backs[4]
    g_vec[1:2, :] += column_sum(back * n2)
    g_vec[4:5, :] += column_sum(back)
    second = norm_back(back, n2, inv2, vecs[1:2, :])
    d2[...] = second
    dco = second.astype(bf16)
    gco[...] += dot(oct_[...], dco)
    gc[...] = dot(dco, square(wo, 0), 1, 1).astype(bf16)

    @pl.when(i == pl.num_programs(0) - 1)
    def _():
        keep = info[3 * SEQS + 1] > 0
        g_co[...] = jnp.where(keep, gco[...], 0.0).astype(bf16)
        targets = ((keep_ffn, info[CORE]), (send_ffn, 1 - info[CORE]))
        for c in range(4):
            gw[...] = jnp.where(keep, dot(hid[...], pre[:, cols(c)], 0, 0), 0.0)
            for ref, core in targets:
                for n in range(4):
                    r0 = pl.multiple_of((2 * n + core) * 4 * chunk, 4 * chunk)
                    part = gw[pl.ds(r0, 4 * chunk), :].astype(bf16).reshape(4, chunk, D)
                    ref[4 * n : 4 * n + 4, c * chunk : (c + 1) * chunk, :] = part
        for c in range(4):
            gw[...] = jnp.where(keep, dot(act[:, cols(c)], third[...], 0, 0), 0.0)
            for ref, core in targets:
                r0 = pl.multiple_of(core * 4 * BROWS, 4 * BROWS)
                part = gw[pl.ds(r0, 4 * BROWS), :].astype(bf16).reshape(4, BROWS, D)
                ref[4 * c : 4 * c + 4, BROWS:, :] = part
        g_b1[...] = jnp.where(keep, g_b1[...], 0.0)
        g_vec[...] = jnp.where(keep, g_vec[...], 0.0)


def unpack_into(info, i, blocks, out):
    @pl.when(i < MICRO)
    def _():
        out[0] = blocks[info[SOURCES + jnp.minimum(i, MICRO - 1)]].astype(f32)


def cross_post_kernel(
    info, blocks, dqct, dkc, dvc, mem, d2, n1, inv1, ot, wa, wb, vecs, g_co,
    out, dmem, d1, go, g_cross, g_wo, g_vec,
    gcq, gck, gcv, gwo,
):
    i = pl.program_id(0)
    unpack_into(info, i, blocks, out)

    @pl.when(i == 0)
    def _():
        for ref in (gcq, gck, gcv, gwo, g_vec):
            ref[...] = jnp.zeros_like(ref)

    m, dk, dv = mem[...], dkc[...], dvc[...]
    dmem[...] = (dot(dk, square(wb, 1), 1, 1) + dot(dv, square(wb, 2), 1, 1)).astype(bf16)
    gck[...] += dot(m, dk, 0, 0)
    gcv[...] += dot(m, dv, 0, 0)
    normed = n1[...]
    hidden = (normed * vecs[0:1, :] + vecs[3:4, :]).astype(bf16)
    dq = dqct[...].T
    gcq[...] += dot(hidden, dq, 0, 0)
    back = d2[...] + dot(dq, square(wb, 0), 1, 1)
    g_vec[0:1, :] += column_sum(back * normed)
    g_vec[3:4, :] += column_sum(back)
    first = norm_back(back, normed, inv1[...], vecs[0:1, :])
    d1[...] = first
    dao = first.astype(bf16)
    gwo[...] += dot(ot[...], dao)
    go[...] = dot(dao, square(wa, 0), 1, 1).astype(bf16)

    @pl.when(i == pl.num_programs(0) - 1)
    def _():
        keep = info[3 * SEQS + 1] > 0
        for n, ref in enumerate((gcq, gck, gcv)):
            g_cross[n * D : (n + 1) * D, :] = jnp.where(keep, ref[...], 0.0).astype(bf16)
        g_cross[3 * D :, :] = g_co[...]
        g_wo[...] = jnp.where(keep, gwo[...], 0.0).astype(bf16)
        g_vec[...] = jnp.where(keep, g_vec[...], 0.0)


def self_grad_kernel(
    info, dqt, dk_ref, dv_ref, x_ref, g_wo, g_cross, g_small,
    keep_out, send_out,
    gq, gk, gv,
):
    i = pl.program_id(0)

    @pl.when(i == 0)
    def _():
        for ref in (gq, gk, gv):
            ref[...] = jnp.zeros_like(ref)

    x = x_ref[...]
    gq[...] += dot(x, dqt[...], 0, 1)
    gk[...] += dot(x, dk_ref[...], 0, 0)
    gv[...] += dot(x, dv_ref[...], 0, 0)

    @pl.when(i == pl.num_programs(0) - 1)
    def _():
        keep = info[3 * SEQS + 1] > 0
        rows = 4 * BROWS
        for ref, core in ((keep_out, info[CORE]), (send_out, 1 - info[CORE])):
            for n in range(4):
                blocks = slice(4 * n, 4 * n + 4)
                r0 = pl.multiple_of(core * rows, rows)
                if n < 3:
                    part = jnp.where(keep, (gq, gk, gv)[n][pl.ds(r0, rows), :], 0.0).astype(bf16)
                else:
                    part = g_wo[pl.ds(r0, rows), :]
                ref[blocks, :BROWS, :] = part.reshape(4, BROWS, D)
                part = g_cross[pl.ds(pl.multiple_of(r0 + n * D, rows), rows), :]
                ref[blocks, BROWS : 2 * BROWS, :] = part.reshape(4, BROWS, D)
                ref[blocks, 2 * BROWS :, : 2 * LANES] = g_small[pl.ds((2 * n + core) * 4, 4), :, :]
                ref[blocks, 2 * BROWS :, 2 * LANES :] = jnp.zeros((4, SMALL, D - 2 * LANES), bf16)


def self_input_kernel(dqt, dk, dv, d1, wa, dtok):
    dtok[...] = (
        d1[...]
        + dot(dqt[...], square(wa, 0), 0, 1)
        + dot(dk[...], square(wa, 1), 1, 1)
        + dot(dv[...], square(wa, 2), 1, 1)
    ).astype(bf16)


def pick_kernel(count, places, *refs):
    arrays, outs, sems = refs[:count], refs[count : 5 * count], refs[5 * count]
    copies = []
    for n, array in enumerate(arrays):
        for k in range(PIECES):
            copies.append(
                pltpu.make_async_copy(array.at[places[k]], outs[n * PIECES + k], sems.at[n, k])
            )
    for copy in copies:
        copy.start()
    for copy in copies:
        copy.wait()


def unpack_kernel(info, blocks, out):
    unpack_into(info, pl.program_id(0), blocks, out)


def plus(*parts):
    total = parts[0].astype(f32)
    for part in parts[1:]:
        total = total + part.astype(f32)
    return total


def route_one_kernel(info, keep, recv, a_keep, a_send, b_keep, b_send):
    x, y = info[CORE + 1], info[CORE + 2]
    for n in range(2):
        for ref, own in ((a_keep, x), (a_send, 1 - x)):
            at = (2 * n + own) * 4
            ref[n] = plus(keep[pl.ds(at, 2)], recv[pl.ds(at, 2)]).astype(bf16)
        for ref, own in ((b_keep, y), (b_send, 1 - y)):
            at = (2 * own + n) * 4 + 2
            ref[n] = plus(keep[pl.ds(at, 2)], recv[pl.ds(at, 2)]).astype(bf16)


def route_two_kernel(info, a, ra, b, rb, a_keep, a_send, b_keep, b_send):
    x, y = info[CORE + 1], info[CORE + 2]
    for ref, own in ((a_keep, y), (a_send, 1 - y)):
        ref[...] = plus(a[own], ra[own]).astype(bf16)
    for ref, own in ((b_keep, x), (b_send, 1 - x)):
        ref[...] = plus(b[own], rb[own]).astype(bf16)


def route_three_kernel(info, a, ra, b, rb, o0, o1, o2, o3, total):
    total[0:2] = plus(a[...], ra[...]).astype(bf16)
    total[2:4] = plus(b[...], rb[...]).astype(bf16)
    for k, ref in enumerate((o0, o1, o2, o3)):
        ref[...] = total[lax.rem(info[3 * SEQS] + k, PIECES)]


def route_four_kernel(r0, r1, r2, r3, out):
    out[...] = plus(r0[...], r1[...], r2[...], r3[...])


SMEM = pl.BlockSpec(memory_space=pltpu.SMEM)
WHOLE = pl.BlockSpec(memory_space=pltpu.VMEM)
ROWS = pl.BlockSpec((PIECE, D), lambda i: (i, 0))
COLS = pl.BlockSpec((D, PIECE), lambda i: (0, i))
BLOCKS_IN = pl.BlockSpec(
    (PIECES, PIECE, D), lambda i: (0, 0, 0), pipeline_mode=pl.Buffered(buffer_count=1)
)
BATCH = pl.BlockSpec((1, PIECE, D), lambda i: (jnp.minimum(i, MICRO - 1), 0, 0))
ROWS_Q = pl.BlockSpec((QB, D), lambda i: (i, 0))
COLS_Q = pl.BlockSpec((D, QB), lambda i: (0, i))
HEADS_Q = pl.BlockSpec((HEADS, QB), lambda i: (0, i))
OUT_W = pl.BlockSpec(
    (BLOCKS // 4, BROWS, D), lambda i: (3, 0, 0), pipeline_mode=pl.Buffered(buffer_count=1)
)
ROWS_F = pl.BlockSpec((FR, D), lambda i: (i, 0))
COLS_F = pl.BlockSpec((D, FR), lambda i: (0, i))
ONES = pl.BlockSpec((PIECE, 1), lambda i: (i, 0))


def fixed(*shape):
    return pl.BlockSpec(
        shape, lambda i: (0,) * len(shape), pipeline_mode=pl.Buffered(buffer_count=1)
    )


def shape(dims, dtype=bf16):
    return jax.ShapeDtypeStruct(dims, dtype)


def call(kernel, name, grid, in_specs, out_specs, out_shape, scratch, flops, *args):
    return pl.pallas_call(
        kernel,
        grid=grid,
        in_specs=in_specs,
        out_specs=out_specs,
        out_shape=out_shape,
        scratch_shapes=scratch,
        name=name,
        compiler_params=pltpu.CompilerParams(vmem_limit_bytes=VMEM_LIMIT),
        cost_estimate=pl.CostEstimate(flops=flops, bytes_accessed=8 << 20, transcendentals=0),
    )(*args)


ROWMAJOR = shape((GROUP, D))
COLMAJOR = shape((D, GROUP))


def project_rows(info, pieces, weights, kind):
    outs = [ROWMAJOR] + ([COLMAJOR] if kind else []) + [ROWMAJOR, ROWMAJOR]
    w_specs = [WHOLE]
    if kind == 2:
        outs = outs + [shape((BLOCKS,) + weights[1].shape[1:])]
        w_specs = [SMEM, WHOLE, WHOLE]
    elif kind == 0:
        w_specs = [fixed(BLOCKS, BROWS, D)]
    return call(
        functools.partial(project_kernel, kind),
        "project",
        (1,),
        [SMEM] + [WHOLE] * PIECES + w_specs,
        [WHOLE] * len(outs),
        outs,
        [],
        4 << 30,
        info,
        *pieces,
        *weights,
    )


def saved_rows(cross):
    return MEM_LEN if cross else KEPT + KB // 2


def attend(info, qt, k, v, cross):
    keep = (HEADS, saved_rows(cross), QB)
    return call(
        functools.partial(attend_kernel, cross),
        "attend",
        (GROUP // QB,),
        [SMEM, COLS_Q, fixed(GROUP, D), fixed(GROUP, D)],
        [COLS_Q, HEADS_Q, SMEM, pl.BlockSpec((1,) + keep, lambda i: (i, 0, 0, 0))],
        [
            COLMAJOR,
            shape((HEADS, GROUP), f32),
            shape((GROUP // QB,), jnp.int32),
            shape((GROUP // QB,) + keep),
        ],
        [
            pltpu.VMEM((D, GROUP), bf16),
            pltpu.VMEM((HEADS, QB), f32),
            pltpu.VMEM((HEADS, QB), f32),
            pltpu.VMEM((HEADS, QB), f32),
            pltpu.VMEM((D, QB), f32),
            pltpu.VMEM((KB, QB), f32),
        ],
        30 << 30,
        info,
        qt,
        k,
        v,
    )


def attend_back(info, qt, k, v, g, ot, lse, flags, saved, cross):
    keep = (HEADS, saved_rows(cross), QB)
    return call(
        functools.partial(attend_back_kernel, cross),
        "attend_back",
        (GROUP // QB,),
        [SMEM, SMEM, COLS_Q, fixed(GROUP, D), fixed(GROUP, D), ROWS_Q, COLS_Q, HEADS_Q]
        + [pl.BlockSpec((1,) + keep, lambda i: (i, 0, 0, 0))],
        [COLS_Q, fixed(GROUP, D), fixed(GROUP, D)],
        [COLMAJOR, ROWMAJOR, ROWMAJOR],
        [
            pltpu.VMEM((D, GROUP), bf16),
            pltpu.VMEM((D, QB), f32),
            pltpu.VMEM((GROUP, D), f32),
            pltpu.VMEM((GROUP, D), f32),
            pltpu.VMEM((D, QB), bf16),
            pltpu.VMEM((HEADS // 2, 2 * QB, 2 * HEAD_DIM), bf16),
            pltpu.VMEM((HEADS // 2, 2 * QB, 2 * HEAD_DIM), bf16),
            pltpu.VMEM((KB, QB), f32),
        ],
        60 << 30,
        info,
        flags,
        qt,
        k,
        v,
        g,
        ot,
        lse,
        saved,
    )


ANY = pl.BlockSpec(memory_space=pl.ANY)


def pick_four(arrays, places):
    n = len(arrays)
    outs = call(
        functools.partial(pick_kernel_args, n),
        "pick",
        (),
        [SMEM] + [ANY] * n,
        [WHOLE] * (PIECES * n),
        [shape(a.shape[1:], a.dtype) for a in arrays for _ in range(PIECES)],
        [pltpu.SemaphoreType.DMA((n, PIECES))],
        1 << 20,
        places,
        *arrays,
    )
    return [list(outs[PIECES * m : PIECES * (m + 1)]) for m in range(n)]


def pick_kernel_args(count, places, *refs):
    pick_kernel(count, places, *refs)


def unpack(info, blocks, micro):
    return call(
        unpack_kernel,
        "unpack",
        (micro,),
        [SMEM, BLOCKS_IN],
        BATCH,
        shape((micro, PIECE, D), f32),
        [],
        1 << 20,
        info,
        blocks,
    )


def route_one(info, keep, recv):
    half = shape((2, 2) + keep.shape[1:])
    return call(
        route_one_kernel, "route_one", (), [SMEM, WHOLE, WHOLE], [WHOLE] * 4, [half] * 4, [], 1 << 20,
        info, keep, recv,
    )


def route_two(info, a, ra, b, rb):
    half = shape(a.shape[1:])
    return call(
        route_two_kernel, "route_two", (), [SMEM] + [WHOLE] * 4, [WHOLE] * 4, [half] * 4, [], 1 << 20,
        info, a, ra, b, rb,
    )


def route_three(info, a, ra, b, rb):
    block = a.shape[1:]
    return call(
        route_three_kernel, "route_three", (), [SMEM] + [WHOLE] * 4, [WHOLE] * 4,
        [shape(block)] * 4, [pltpu.VMEM((4,) + block, bf16)], 1 << 20,
        info, a, ra, b, rb,
    )


def route_last_kernel(r0, r1, r2, r3, own, cross, gain, bias, out_bias, in_bias):
    def rows(first, count):
        part = slice(first, first + count)
        return plus(r0[part, :], r1[part, :], r2[part, :], r3[part, :])

    own[...] = rows(0, BROWS)
    cross[...] = rows(BROWS, BROWS)
    small = rows(2 * BROWS, SMALL)
    turned = small[:, :LANES].T
    gain[...] = turned[0:3]
    bias[...] = turned[3:6]
    out_bias[...] = turned[6:7]
    in_bias[...] = small[0:1, LANES : LANES + BROWS]


def route_last(pieces, rows, out_rows):
    outs = [(rows, D), (rows, D), (3, out_rows), (3, out_rows), (1, out_rows), (1, rows)]
    return call(
        route_last_kernel, "route_last", (), [WHOLE] * 4, [WHOLE] * 6, [shape(o, f32) for o in outs], [],
        1 << 20, *pieces,
    )


def route_four(pieces):
    return call(
        route_four_kernel, "route_four", (), [WHOLE] * 4, WHOLE, shape(pieces[0].shape, f32), [], 1 << 20,
        *pieces,
    )


def tie(value, *deps):
    return lax.optimization_barrier((value, deps))[0]


def dp_swap(array, bit):
    n = lax.axis_size("dp")
    return lax.ppermute(array, "dp", [(d, d ^ bit) for d in range(n)])


def turns(arrays):
    n = lax.axis_size("fsdp")
    return [arrays[0]] + [
        lax.ppermute(arrays[k], "fsdp", [(m, (m + k) % n) for m in range(n)])
        for k in range(1, len(arrays))
    ]


def local(
    tokens, memory, cotangent, lengths, seq_order, memory_pick,
    self_attn, cross_attn, ffn_in, ffn_in_bias, ffn_out, ffn_out_bias, norm_gain, norm_bias,
):
    axes = ("dp", "fsdp")
    n_dp, members = lax.axis_size("dp"), lax.axis_size("fsdp")
    micro = tokens.shape[0]
    owners = n_dp * members
    dp, z = lax.axis_index("dp"), lax.axis_index("fsdp")

    def offset(d):
        return d % 2 if micro < members else 0

    def unit_at(d, member):
        return member - offset(d)

    mine = unit_at(dp, z)
    valid = (mine >= 0) & (mine < micro)
    unit = jnp.clip(mine, 0, micro - 1)

    def pairs(k):
        out = []
        for d in range(n_dp):
            for source in range(members):
                target = (source + k) % members
                if 0 <= unit_at(d, target) < micro:
                    out.append((d * members + source, d * members + target))
        return out

    def to_unit(pieces):
        return [pieces[0]] + [
            lax.ppermute(pieces[k], axes, pairs(k)) for k in range(1, members)
        ]

    def from_unit(rows_of_unit):
        blocks = rows_of_unit.reshape(members, PIECE, D)
        return lax.all_to_all(blocks, "fsdp", split_axis=0, concat_axis=0)

    def row_of(array):
        return lax.dynamic_index_in_dim(array, unit, 0, False)[0]

    boxed = n_dp == 8 and members == 4
    shifts = jnp.arange(members, dtype=jnp.int32)

    targets = jnp.clip(lax.rem(z + shifts, members) - offset(dp), 0, micro - 1)
    sources = jnp.arange(micro, dtype=jnp.int32) + offset(dp)
    targets = targets.at[0].set(unit).astype(jnp.int32)

    bits = [dp & 1, (dp >> 1) & 1, (dp >> 2) & 1] if boxed else [jnp.zeros_like(dp)] * 3
    info = jnp.concatenate(
        [
            row_of(lengths),
            row_of(seq_order),
            row_of(memory_pick),
            jnp.stack([z, valid.astype(jnp.int32), *bits]),
            sources,
        ]
    ).astype(jnp.int32)

    smalls = jnp.concatenate(
        [ffn_in_bias, ffn_out_bias, norm_gain.T.reshape(-1), norm_bias.T.reshape(-1)]
    )
    rows = self_attn.shape[0]
    in_rows = ffn_in.shape[0]
    n_smalls = smalls.shape[0]
    token_slices = pick_four([tokens], targets)[0]
    smalls = tie(smalls, token_slices)
    small_row = jnp.pad(smalls, (0, 16 * D - n_smalls)).reshape(16, D)
    bundle_a = jnp.concatenate([self_attn, small_row], axis=0)
    in_blocks = ffn_in.reshape(in_rows, 4, D).transpose(1, 0, 2).reshape(4 * in_rows, D)
    bundle_f = jnp.concatenate([ffn_out, in_blocks], axis=0)
    if boxed:
        turned = turns([bundle_a] * members)
    token_pieces = to_unit(token_slices)
    late = tie([memory, cotangent], token_slices)
    memory_slices, cotangent_slices = pick_four(late, targets)
    if boxed:
        a0, b0 = jnp.stack(turned[:2]), jnp.stack(turned[2:])
        a1, b1 = dp_swap(a0, 2), dp_swap(b0, 4)
        a2 = dp_swap(jnp.stack([a0, a1]), 4)
        b2 = dp_swap(jnp.stack([b0, b1]), 2)
        near = jnp.concatenate([a0, a1, a2[0], a2[1], b0, b1, b2[0], b2[1]])
        masks = jnp.array([0, 0, 2, 2, 4, 4, 6, 6, 0, 0, 4, 4, 2, 2, 6, 6], jnp.int32)
        steps = jnp.array([0, 1] * 4 + [2, 3] * 4, jnp.int32)
        owner = (dp ^ masks) * members + lax.rem(z - steps + members, members)
        places = jnp.concatenate([owner, owner ^ members]).astype(jnp.int32)
        near = tie(near, token_pieces[1:], memory_slices, cotangent_slices, info, places)
        far = dp_swap(near, 1)
    else:
        all_a = lax.all_gather(bundle_a, axes, axis=0, tiled=False)
        wa = jnp.pad(all_a[:, :rows].reshape(BLOCKS, BROWS, D), ((0, 0), (0, SMALL), (0, 0)))
    all_b = lax.all_gather(tie(cross_attn, token_slices), axes, axis=0, tiled=False)
    all_f = lax.all_gather(tie(bundle_f, token_slices), axes, axis=0, tiled=False)
    def blocked(array, count):
        return array.reshape(BLOCKS, count, D)

    if owners == BLOCKS:
        wb, wf = all_b, all_f
    else:
        first = all_f[:, rows:].reshape(owners, 4, in_rows, D).transpose(1, 0, 2, 3)
        first = first.reshape(4, BLOCKS, BROWS // 4, D).transpose(1, 0, 2, 3)
        wb = blocked(all_b, BROWS)
        wf = jnp.concatenate([blocked(all_f[:, :rows], BROWS), blocked(first, BROWS)], axis=1)
    if boxed:
        x, qt, k, v, wa = project_rows(info, token_pieces, (places, near, far), 2)
        all_a = wa
    else:
        x, qt, k, v = project_rows(info, token_pieces, (wa,), 1)
    small = all_a[:, rows, :n_smalls].astype(f32)
    out_rows = D // owners
    b1 = small[:, :rows].reshape(1, FF)
    at = rows + out_rows
    vec_rows = [small[:, at + n * out_rows : at + (n + 1) * out_rows].reshape(1, D) for n in range(6)]
    vecs = jnp.concatenate(
        vec_rows + [small[:, rows:at].reshape(1, D), jnp.zeros((1, D), f32)], axis=0
    )

    memory_pieces = to_unit(tie(memory_slices, x))
    ot, *self_saved = attend(info, qt, k, v, False)
    ot = tie(ot, *memory_pieces[1:])
    cotangent_pieces = to_unit(tie(cotangent_slices, memory_pieces[1:], ot))
    n1, inv1, qct = call(
        first_norm_kernel,
        "first_norm",
        (PIECES,),
        [COLS, ROWS, OUT_W, fixed(BLOCKS, BROWS, D), fixed(8, D)],
        [ROWS, ONES, COLS],
        [shape((GROUP, D), f32), shape((GROUP, 1), f32), COLMAJOR],
        [],
        2 << 30,
        ot,
        x,
        wa,
        wb,
        vecs,
    )
    mem, kc, vc = project_rows(info, memory_pieces, (wb,), 0)
    oct_, *cross_saved = attend(info, qct, kc, vc, True)
    y_out, d2, gc, keep_ffn, send_ffn, g_co, g_b1, g_vec = call(
        ffn_kernel,
        "ffn",
        (GROUP // FR,),
        [SMEM, COLS_F, ROWS_F, OUT_W, fixed(BLOCKS, 2 * BROWS, D), fixed(8, D), fixed(1, FF)]
        + [fixed(PIECE, D)] * 4,
        [
            fixed(GROUP, D),
            ROWS_F,
            ROWS_F,
            fixed(HALF, 2 * BROWS, D),
            fixed(HALF, 2 * BROWS, D),
            fixed(D, D),
            fixed(1, FF),
            fixed(8, D),
        ],
        [
            ROWMAJOR,
            shape((GROUP, D), f32),
            ROWMAJOR,
            shape((HALF, 2 * BROWS, D)),
            shape((HALF, 2 * BROWS, D)),
            shape((D, D)),
            shape((1, FF), f32),
            shape((8, D), f32),
        ],
        [
            pltpu.VMEM((GROUP, FF), bf16),
            pltpu.VMEM((GROUP, FF), bf16),
            pltpu.VMEM((GROUP, D), bf16),
            pltpu.VMEM((GROUP, D), bf16),
            pltpu.VMEM((FR, FF), f32),
            pltpu.VMEM((FR, D), f32),
            pltpu.VMEM((D, D), f32),
            pltpu.VMEM((D, D), f32),
        ],
        32 << 30,
        info,
        oct_,
        n1,
        wb,
        wf,
        vecs,
        b1,
        *cotangent_pieces,
    )
    y_pieces = from_unit(y_out)
    if boxed:
        ffn_a, send_a, ffn_b, send_b = route_one(info, keep_ffn, dp_swap(send_ffn, 1))
        recv_a, recv_b = dp_swap(send_a, 2), dp_swap(send_b, 4)
        gc = tie(gc, send_a)

    dqct, dkc, dvc = attend_back(info, qct, kc, vc, gc, oct_, *cross_saved, True)
    if boxed:
        recv_a, recv_b, ffn_a, ffn_b = tie((recv_a, recv_b, ffn_a, ffn_b), dqct)
        ffn_a, send_a, ffn_b, send_b = route_two(info, ffn_a, recv_a, ffn_b, recv_b)
        recv_a, recv_b = dp_swap(send_a, 4), dp_swap(send_b, 2)
        g_co = tie(g_co, send_a)
    layer_output, *m_and_rest = call(
        cross_post_kernel,
        "cross_post",
        (PIECES,),
        [SMEM, BLOCKS_IN, COLS, ROWS, ROWS, ROWS, ROWS, ROWS, ONES, COLS]
        + [OUT_W, fixed(BLOCKS, BROWS, D), fixed(8, D), fixed(D, D)],
        [BATCH, ROWS, ROWS, ROWS, fixed(4 * D, D), fixed(D, D), fixed(8, D)],
        [
            shape((micro, PIECE, D), f32),
            ROWMAJOR,
            shape((GROUP, D), f32),
            ROWMAJOR,
            shape((4 * D, D)),
            shape((D, D)),
            shape((8, D), f32),
        ],
        [pltpu.VMEM((D, D), f32)] * 4,
        9 << 30,
        info,
        y_pieces,
        dqct,
        dkc,
        dvc,
        mem,
        d2,
        n1,
        inv1,
        ot,
        wa,
        wb,
        vecs,
        g_co,
    )
    m_out, d1, go, g_cross, g_wo, g_vec_one = m_and_rest
    m_pieces = from_unit(m_out)
    if boxed:
        recv_a, recv_b, ffn_a, ffn_b = tie((recv_a, recv_b, ffn_a, ffn_b), d1)
        ffn_pieces = turns(route_three(info, ffn_a, recv_a, ffn_b, recv_b))
        go = tie(go, ffn_pieces[0])
    g_vec = g_vec + g_vec_one
    if boxed:
        columns = g_vec.reshape(8, BLOCKS, SMALL).transpose(1, 2, 0)
        columns = jnp.pad(columns, ((0, 0), (0, 0), (0, LANES - 8)))
        first = jnp.pad(g_b1.reshape(BLOCKS, 1, rows), ((0, 0), (0, SMALL - 1), (0, LANES - rows)))
        g_small = jnp.concatenate([columns, first], axis=2).astype(bf16)
    else:
        g_small = jnp.zeros((BLOCKS, SMALL, 2 * LANES), bf16)
        small_grads = jnp.concatenate(
            [g_b1.reshape(owners, rows), g_vec[6].reshape(owners, out_rows)]
            + [g_vec[n].reshape(owners, out_rows) for n in range(6)],
            axis=1,
        )
    dqt, dk, dv = attend_back(info, qt, k, v, go, ot, *self_saved, False)
    x_late = x
    if boxed:
        d1 = tie(d1, ffn_pieces, m_pieces)
    last_rows = 2 * BROWS + SMALL
    t_out = call(
        self_input_kernel,
        "self_input",
        (PIECES,),
        [COLS, ROWS, ROWS, ROWS, fixed(3 * BLOCKS // 4, BROWS, D)],
        ROWS,
        ROWMAJOR,
        [],
        4 << 30,
        dqt,
        dk,
        dv,
        d1,
        wa,
    )
    t_pieces = from_unit(t_out)
    x_late = tie(x_late, t_out)
    keep_last, send_last = call(
        self_grad_kernel,
        "self_grad",
        (PIECES,),
        [SMEM, COLS, ROWS, ROWS, ROWS, fixed(D, D), fixed(4 * D, D), fixed(BLOCKS, SMALL, 2 * LANES)],
        [fixed(HALF, last_rows, D)] * 2,
        [shape((HALF, last_rows, D))] * 2,
        [pltpu.VMEM((D, D), f32)] * 3,
        4 << 30,
        info,
        dqt,
        dk,
        dv,
        x_late,
        g_wo,
        g_cross,
        g_small,
    )
    if boxed:
        recv_last = dp_swap(send_last, 1)
        near, send_a, far, send_b = route_one(info, keep_last, recv_last)
        recv_a, recv_b = dp_swap(send_a, 2), dp_swap(send_b, 4)

    def whole_blocks(keep, send):
        both = jnp.stack([keep, send]).reshape(2, 4, 4, -1, D)
        return both.transpose(1, 0, 2, 3, 4).reshape(BLOCKS, -1, D)

    def owned(array):
        return lax.psum_scatter(array, axes, scatter_dimension=0, tiled=True)[0].astype(f32)

    if boxed:
        recv_a = tie(recv_a, t_pieces)
        ffn_part = route_four(tie(ffn_pieces, send_a))
        memory_grad = unpack(info, tie(m_pieces, send_a), micro)
        near = tie(near, ffn_part, memory_grad)
        near, send_a, far, send_b = route_two(info, near, recv_a, far, recv_b)
        recv_a, recv_b = dp_swap(send_a, 4), dp_swap(send_b, 2)
        input_grad = unpack(info, tie(t_pieces, send_a), micro)
        near = tie(near, input_grad)
        last_pieces = turns(route_three(info, near, recv_a, far, recv_b))
        self_attn_grad, cross_attn_grad, gain_grad, bias_grad, out_bias, in_bias = route_last(
            last_pieces, rows, out_rows
        )
    else:
        memory_grad = unpack(info, m_pieces, micro)
        input_grad = unpack(info, t_pieces, micro)
        ffn = whole_blocks(keep_ffn, send_ffn)
        second = ffn[:, BROWS:].reshape(owners, rows, D)
        first = ffn[:, :BROWS].reshape(BLOCKS, 4, BROWS // 4, D).transpose(1, 0, 2, 3)
        first = first.reshape(4, owners, in_rows, D).transpose(1, 0, 2, 3)
        ffn_part = owned(jnp.concatenate([first.reshape(owners, rows, D), second], axis=1))
        rest = whole_blocks(keep_last, send_last)
        self_attn_grad = owned(rest[:, :BROWS].reshape(owners, rows, D))
        cross_attn_grad = owned(rest[:, BROWS : 2 * BROWS].reshape(owners, rows, D))
        small_out = owned(small_grads)
        at = rows + out_rows
        norm_part = small_out[at : at + 6 * out_rows].reshape(6, out_rows)
        gain_grad, bias_grad = norm_part[:3], norm_part[3:]
        in_bias, out_bias = small_out[:rows], small_out[rows:at]
    ffn_in_grad = ffn_part[:rows].reshape(4, in_rows, D).transpose(1, 0, 2).reshape(in_rows, FF)
    return (
        layer_output,
        input_grad,
        memory_grad,
        self_attn_grad,
        cross_attn_grad,
        ffn_in_grad,
        in_bias.reshape(rows),
        ffn_part[rows:],
        out_bias.reshape(out_rows),
        gain_grad.T,
        bias_grad.T,
    )


def solution(mesh):
    rows = P(None, ("dp", "fsdp"), None)
    group = P(None, "dp", None)
    shard = P(("dp", "fsdp"), None)
    flat = P(("dp", "fsdp"))
    in_specs = (rows,) * 3 + (group,) * 3 + (shard, shard, shard, flat, shard, flat, shard, shard)
    out_specs = (rows,) * 3 + (shard, shard, shard, flat, shard, flat, shard, shard)
    return jax.shard_map(local, mesh=mesh, in_specs=in_specs, out_specs=out_specs, check_vma=False)
```

```python
import functools
import math

import jax
import jax.numpy as jnp
from jax import lax
from jax.experimental import pallas as pl
from jax.experimental.pallas import tpu as pltpu
from jax.sharding import PartitionSpec as P

D = 512
HEADS = 8
HEAD_DIM = 64
FF = 2048
MEM_LEN = 1024
SEQS = 4
NMEM = 2
GROUP = 2048
PIECE = 512
PIECES = GROUP // PIECE
QB = 256
KB = 512
FR = 512
LANES = 128
KEPT = 1024
NEG = -1e30
BLOCKS = 32
BROWS = D * 4 // BLOCKS
bf16 = jnp.bfloat16
f32 = jnp.float32
VMEM_LIMIT = 58 << 20
CORE = 3 * SEQS + 2
HALF = BLOCKS // 2
SMALL = 16
MICRO = 3
SOURCES = 3 * SEQS + 5


def dot(left, right, cl=1, cr=0):
    return lax.dot_general(
        left, right, (((cl,), (cr,)), ((), ())), preferred_element_type=f32
    )


def place_ends(info):
    ends, total = [], 0
    for j in range(SEQS):
        total = total + info[info[SEQS + j]]
        ends.append(total)
    return ends


def place_picks(info):
    return [info[2 * SEQS + info[SEQS + j]] for j in range(SEQS)]


def place_shifts(info, ends):
    shifts = []
    for j in range(SEQS):
        seq = info[SEQS + j]
        start = 0
        for s in range(SEQS):
            start = start + jnp.where(s < seq, info[s], 0)
        shifts.append(start - (ends[j - 1] if j else 0))
    return shifts


def by_place(rows, ends, values):
    out = jnp.full(rows.shape, values[0], jnp.int32)
    for j in range(SEQS - 1):
        out = jnp.where(rows >= ends[j], values[j + 1], out)
    return out


def piece_row(info, k):
    return pl.multiple_of(lax.rem(info[3 * SEQS] - k + PIECES, PIECES) * PIECE, PIECE)


def weight(ref, first, count, offset, rows):
    return ref[first : first + count, offset : offset + rows, :].reshape(count * rows, D)


def square(ref, index, offset=0):
    per = BLOCKS // 4
    return weight(ref, index * per, per, offset, BROWS)


def project_kernel(kind, info, x0, x1, x2, x3, *refs):
    with_query = kind > 0
    if kind == 2:
        places, near, far, x_out, qt_out, k_out, v_out, w = refs
        for n in range(HALF):
            w[pl.ds(places[n], 1)] = near[n : n + 1]
            w[pl.ds(places[HALF + n], 1)] = far[n : n + 1]
    elif kind == 1:
        w, x_out, qt_out, k_out, v_out = refs
    else:
        w, x_out, k_out, v_out = refs
    if with_query:
        wq = square(w, 0)
    wk, wv = square(w, 1), square(w, 2)
    for k, piece in enumerate((x0, x1, x2, x3)):
        r0 = piece_row(info, k)
        rows = pl.ds(r0, PIECE)
        x = piece[...]
        x_out[rows, :] = x
        if with_query:
            q = dot(x, wq).astype(bf16) * jnp.asarray(HEAD_DIM**-0.5, bf16)
            qt_out[:, rows] = q.T
        k_out[rows, :] = dot(x, wk).astype(bf16)
        v_out[rows, :] = dot(x, wv).astype(bf16)


def memories_read(info, q0):
    ends, picks = place_ends(info), place_picks(info)
    rows = q0 + lax.broadcasted_iota(jnp.int32, (1, QB), 1)
    picked = by_place(rows, ends, picks)
    needs = []
    for mem in range(NMEM):
        need = jnp.bool_(False)
        for j in range(SEQS):
            start = ends[j - 1] if j else 0
            need = need | ((start < q0 + QB) & (ends[j] > q0) & (picks[j] == mem))
        needs.append(need)
    return needs, [picked == mem for mem in range(NMEM)]


def window(info, q0):
    ends = place_ends(info)
    rows = q0 + lax.broadcasted_iota(jnp.int32, (1, QB), 1)
    low, high = 0, GROUP
    low_row = jnp.zeros((1, QB), jnp.int32)
    high_row = jnp.full((1, QB), GROUP, jnp.int32)
    for j in range(SEQS - 1):
        low = jnp.where(q0 >= ends[j], ends[j], low)
        low_row = jnp.where(rows >= ends[j], ends[j], low_row)
    for j in reversed(range(SEQS - 1)):
        high = jnp.where(q0 + QB - 1 < ends[j], ends[j], high)
        high_row = jnp.where(rows < ends[j], ends[j], high_row)
    low = low // LANES * LANES
    many = (high - low) // KB
    rest = high - low - many * KB
    many = jnp.where(rest > KB // 2, many + 1, many)
    narrow = (rest > 0) & (rest <= KB // 2)

    def place(first, size):
        k0 = pl.multiple_of(jnp.minimum(first, GROUP - size), LANES)
        keys = k0 + lax.broadcasted_iota(jnp.int32, (size, QB), 0)
        inside = (keys >= jnp.maximum(low_row, first)) & (keys < high_row)
        return k0, jnp.where(inside, 0.0, NEG)

    return low, many, narrow, place


def loop(first, last, body):
    def step(j, carry):
        body(j)
        return carry

    lax.fori_loop(first, last, step, 0)


def head_rows(h):
    return slice(h * HEAD_DIM, (h + 1) * HEAD_DIM)


def pipelined(groups, *stages):
    for step in range(groups + len(stages) - 1):
        for lag, stage in enumerate(stages):
            if 0 <= step - lag < groups:
                stage(step - lag)


def attend_kernel(
    cross, info, qt, k, v, ot, lse, flags, saved, vt, top, total, peak, acc, bias_ref
):
    i = pl.program_id(0)
    q0 = pl.multiple_of(i * QB, QB)
    group = 2

    @pl.when(i == 0)
    def _():
        for c in range(GROUP // QB):
            vt[:, c * QB : (c + 1) * QB] = v[c * QB : (c + 1) * QB, :].T

    def tile(safe, k0, size, bias, allowed, slot):
        keys = pl.ds(k0, size)
        if bias is not None:
            bias_ref[:size, :] = bias
        totals = total[...]
        tops = top[...] if safe else None
        new_tops, new_totals, peaks = [], [], []
        scores, parts = {}, {}

        def score(g):
            heads = range(g * group, (g + 1) * group)
            scores[g] = [dot(k[keys, head_rows(h)], qt[head_rows(h), :]) for h in heads]

        def soften(g):
            parts[g] = []
            for n, s in enumerate(scores.pop(g)):
                h = g * group + n
                decay = None
                if bias is not None:
                    s = s + bias_ref[:size, :]
                if safe:
                    old = tops[h : h + 1]
                    new = jnp.maximum(old, jnp.max(s, axis=0, keepdims=True))
                    if allowed is not None:
                        new = jnp.where(allowed, new, old)
                    decay = jnp.exp(old - new)
                    new_tops.append(new)
                    s = s - new
                p = jnp.exp(s)
                part = jnp.sum(p, axis=0, keepdims=True)
                if allowed is not None:
                    peaks.append(part)
                    p = jnp.where(allowed, p, 0.0)
                    part = jnp.where(allowed, part, 0.0)
                before = totals[h : h + 1]
                new_totals.append((before * decay if safe else before) + part)
                low = p.astype(bf16)
                if slot is not None:
                    saved[0, h, pl.ds(slot, size), :] = low
                parts[g].append((decay, low))

        def mix(g):
            for n, (decay, p) in enumerate(parts.pop(g)):
                rows = head_rows(g * group + n)
                before = acc[rows, :]
                acc[rows, :] = (before * decay if safe else before) + dot(vt[rows, keys], p)

        pipelined(HEADS // group, score, soften, mix)
        if safe:
            top[...] = jnp.concatenate(new_tops, axis=0)
        elif peaks:
            peak[...] = jnp.maximum(peak[...], jnp.concatenate(peaks, axis=0))
        total[...] = jnp.concatenate(new_totals, axis=0)

    def sweep(safe):
        if safe:
            top[...] = jnp.full_like(top, NEG)
        else:
            peak[...] = jnp.zeros_like(peak)
        total[...] = jnp.zeros_like(total)
        acc[...] = jnp.zeros_like(acc)
        if cross:
            needs, allowed = memories_read(info, q0)
            both = needs[0] & needs[1]
            if safe:
                for mem in range(NMEM):

                    @pl.when(needs[mem])
                    def _():
                        tile(True, mem * MEM_LEN, MEM_LEN, None, allowed[mem], None)
            else:

                @pl.when(jnp.logical_not(both))
                def _():
                    first = pl.multiple_of(jnp.where(needs[0], 0, MEM_LEN), MEM_LEN)
                    tile(False, first, MEM_LEN, None, None, 0)

                @pl.when(both)
                def _():
                    tile(False, 0, MEM_LEN, None, allowed[0], 0)
                    tile(False, MEM_LEN, MEM_LEN, None, allowed[1], None)
        else:
            low, many, narrow, place = window(info, q0)

            def part(j, size, slot):
                k0, bias = place(low + j * KB, size)
                tile(safe, k0, size, bias, None, slot)

            kept = 0 if safe else jnp.minimum(many, KEPT // KB)
            if not safe:
                loop(0, kept, lambda j: part(j, KB, pl.multiple_of(j * KB, KB)))
            loop(kept, many, lambda j: part(j, KB, None))

            @pl.when(narrow)
            def _():
                part(many, KB // 2, None if safe else pl.multiple_of(kept * KB, KB))

        sums = total[...]
        inverse = 1.0 / sums
        lse[...] = jnp.log(sums) + (top[...] if safe else 0.0)
        for h in range(HEADS):
            ot[head_rows(h), :] = (acc[head_rows(h), :] * inverse[h : h + 1]).astype(bf16)

    sweep(False)
    sums = total[...]
    safe_range = (jnp.min(sums) > 1e-18) & (jnp.max(sums) < 1e18) & (jnp.max(peak[...]) < 1e18)
    flags[i] = safe_range.astype(jnp.int32)

    @pl.when(jnp.logical_not(safe_range))
    def _():
        sweep(True)


def attend_back_kernel(
    cross, info, flags, qt, k, v, g, ot, lse, saved, dqt, dk, dv,
    kt, dqt_acc, dk_acc, dv_acc, gt, gm, qm, bias_ref,
):
    i = pl.program_id(0)
    q0 = pl.multiple_of(i * QB, QB)
    group = 2
    shiftless = flags[i] > 0

    @pl.when(i == 0)
    def _():
        dk_acc[...] = jnp.zeros_like(dk_acc)
        dv_acc[...] = jnp.zeros_like(dv_acc)
        for c in range(GROUP // QB):
            kt[:, c * QB : (c + 1) * QB] = k[c * QB : (c + 1) * QB, :].T

    lses = lse[...]
    factor = jnp.where(shiftless, jnp.exp(-lses), 1.0)
    shifts = jnp.where(shiftless, 0.0, lses)
    weighted = []
    turned = g[...].T
    for h in range(HEADS):
        scaled = turned[head_rows(h), :].astype(f32) * factor[h : h + 1]
        weighted.append(
            jnp.sum(scaled * ot[head_rows(h), :].astype(f32), axis=0, keepdims=True)
        )
        gt[head_rows(h), :] = scaled.astype(bf16)
    left = lax.broadcasted_iota(jnp.int32, (QB, 2 * HEAD_DIM), 1) < HEAD_DIM
    for pair in range(HEADS // 2):
        cols = slice(pair * 2 * HEAD_DIM, (pair + 1) * 2 * HEAD_DIM)
        gp = gt[cols, :].T
        qp = qt[cols, :].T
        zero = jnp.zeros_like(gp)
        gm[pair, :QB, :] = jnp.where(left, gp, zero)
        gm[pair, QB:, :] = jnp.where(left, zero, gp)
        qm[pair, :QB, :] = jnp.where(left, qp, zero)
        qm[pair, QB:, :] = jnp.where(left, zero, qp)
    dqt_acc[...] = jnp.zeros_like(dqt_acc)

    def tile(k0, size, bias, allowed, slot):
        keys = pl.ds(k0, size)
        if bias is not None:
            bias_ref[:size, :] = bias
        bases = shifts if allowed is None else jnp.where(allowed, shifts, -NEG)
        scores, slopes, probs, grads = {}, {}, {}, {}

        def score(g):
            heads = range(g * group, (g + 1) * group)
            if slot is None:
                scores[g] = [dot(k[keys, head_rows(h)], qt[head_rows(h), :]) for h in heads]
            slopes[g] = [dot(v[keys, head_rows(h)], gt[head_rows(h), :]) for h in heads]

        def soften(g):
            probs[g], grads[g] = [], []
            for n, dp in enumerate(slopes.pop(g)):
                h = g * group + n
                if slot is None:
                    s = scores[g][n]
                    if bias is not None:
                        s = s + bias_ref[:size, :]
                    p = jnp.exp(s - bases[h : h + 1])
                    probs[g].append(p.astype(bf16))
                else:
                    probs[g].append(saved[0, h, pl.ds(slot, size), :])
                    p = probs[g][n].astype(f32)
                grads[g].append((p * (dp - weighted[h])).astype(bf16))

        def mix(g):
            for n in range(0, group, 2):
                pair = (g * group + n) // 2
                cols = slice(pair * 2 * HEAD_DIM, (pair + 1) * 2 * HEAD_DIM)
                dv_acc[keys, cols] += dot(jnp.concatenate(probs[g][n : n + 2], axis=1), gm[pair])
                dk_acc[keys, cols] += dot(jnp.concatenate(grads[g][n : n + 2], axis=1), qm[pair])
            for n, ds in enumerate(grads[g]):
                rows = head_rows(g * group + n)
                dqt_acc[rows, :] += dot(kt[rows, keys], ds)

        pipelined(HEADS // group, score, soften, mix)

    if cross:
        needs, allowed = memories_read(info, q0)

        @pl.when(shiftless)
        def _():
            first = pl.multiple_of(jnp.where(needs[0], 0, MEM_LEN), MEM_LEN)
            tile(first, MEM_LEN, None, None, 0)

        for mem in range(NMEM):
            done = shiftless & (jnp.logical_not(needs[0]) if mem else True)

            @pl.when(needs[mem] & jnp.logical_not(done))
            def _():
                tile(mem * MEM_LEN, MEM_LEN, None, allowed[mem], None)
    else:
        low, many, narrow, place = window(info, q0)

        def part(j, size, slot):
            k0, bias = place(low + j * KB, size)
            tile(k0, size, bias if slot is None else None, None, slot)

        kept = jnp.where(shiftless, jnp.minimum(many, KEPT // KB), 0)
        loop(0, kept, lambda j: part(j, KB, pl.multiple_of(j * KB, KB)))
        loop(kept, many, lambda j: part(j, KB, None))

        @pl.when(narrow & shiftless)
        def _():
            part(many, KB // 2, pl.multiple_of(kept * KB, KB))

        @pl.when(narrow & jnp.logical_not(shiftless))
        def _():
            part(many, KB // 2, None)

    dqt[...] = (dqt_acc[...] * HEAD_DIM**-0.5).astype(bf16)

    @pl.when(i == pl.num_programs(0) - 1)
    def _():
        dk[...] = dk_acc[...].astype(bf16)
        dv[...] = dv_acc[...].astype(bf16)


def norm(resid):
    center = resid - jnp.mean(resid, axis=-1, keepdims=True)
    inv = lax.rsqrt(jnp.mean(center * center, axis=-1, keepdims=True) + 1e-06)
    return center * inv, inv


def norm_back(grad, normed, inv, gain):
    scaled = grad * gain
    return inv * (
        scaled
        - jnp.mean(scaled, axis=-1, keepdims=True)
        - normed * jnp.mean(scaled * normed, axis=-1, keepdims=True)
    )


def column_sum(value):
    return jnp.sum(value, axis=0, keepdims=True)


def first_norm_kernel(ot, x, wa, wb, vecs, n1, inv1, qct):
    resid = x[...].astype(f32) + dot(ot[...], square(wa, 0), 0, 0)
    normed, inv = norm(resid)
    n1[...] = normed
    inv1[...] = inv
    hidden = (normed * vecs[0:1, :] + vecs[3:4, :]).astype(bf16)
    q = dot(hidden, square(wb, 0)).astype(bf16) * jnp.asarray(HEAD_DIM**-0.5, bf16)
    qct[...] = q.T


def ffn_kernel(
    info, oct_, n1, wo, wf, vecs, b1, c0, c1, c2, c3,
    yg, d2, gc, keep_ffn, send_ffn, g_co, g_b1, g_vec,
    act, pre, hid, third, slope, dy, gw, gco,
):
    i = pl.program_id(0)

    @pl.when(i == 0)
    def _():
        for ref in (gco, g_b1, g_vec, yg):
            ref[...] = jnp.zeros_like(ref)

    rows_here = pl.ds(pl.multiple_of(i * FR, FR), FR)
    chunk = BROWS // 4

    def w1(c):
        return weight(wf, 0, BLOCKS, BROWS + c * chunk, chunk)

    def w2(c):
        per = BLOCKS // 4
        return weight(wf, c * per, per, 0, BROWS)

    hidden_one = n1[...] * vecs[0:1, :] + vecs[3:4, :]
    n2, inv2 = norm(hidden_one + dot(oct_[...], square(wo, 0), 0, 0))
    hidden = n2 * vecs[1:2, :] + vecs[4:5, :]
    hidden_b = hidden.astype(bf16)

    factor = math.sqrt(2.0 / math.pi)
    cubic = 0.044715 * factor
    ups, acts, outs = {}, {}, []

    def cols(c):
        return slice(c * D, (c + 1) * D)

    def up(c):
        ups[c] = dot(hidden_b, w1(c))

    def bend(c):
        u = ups.pop(c) + b1[0:1, cols(c)]
        sq = u * u
        t = jnp.tanh(u * (factor + cubic * sq))
        half = 0.5 + 0.5 * t
        acts[c] = (u * half).astype(bf16)
        act[rows_here, cols(c)] = acts[c]
        slope[:, cols(c)] = half + u * (1.0 - t * t) * (0.5 * factor + 1.5 * cubic * sq)

    def down(c):
        outs.append(dot(acts.pop(c), w2(c)))

    pipelined(4, up, bend, down)
    out = (outs[0] + outs[1]) + (outs[2] + outs[3])
    n3, inv3 = norm(hidden + (out + vecs[6:7, :]))
    y = (n3 * vecs[2:3, :] + vecs[5:6, :]).astype(bf16)

    ends = place_ends(info)
    shifts = place_shifts(info, ends)
    p0 = i * FR
    rows = p0 + lax.broadcasted_iota(jnp.int32, (FR, 1), 0)
    given = rows + by_place(rows, ends, shifts)
    dy[...] = jnp.zeros_like(dy)

    for k, piece in enumerate((c0, c1, c2, c3)):
        r0 = piece_row(info, k)
        hit = jnp.bool_(False)
        for j in range(SEQS):
            begin = jnp.maximum(ends[j - 1] if j else 0, p0)
            end = jnp.minimum(ends[j], p0 + FR)
            hit = hit | (
                (begin < end) & (begin + shifts[j] < r0 + PIECE) & (end + shifts[j] > r0)
            )

        @pl.when(hit)
        def _():
            columns = r0 + lax.broadcasted_iota(jnp.int32, (FR, PIECE), 1)
            select = jnp.where(columns == given, 1.0, 0.0).astype(bf16)
            dy[...] += dot(select, piece[...])
            yg[pl.ds(r0, PIECE), :] += dot(select, y, 0, 0).astype(bf16)

    grad = dy[...]
    g_vec[2:3, :] += column_sum(grad * n3)
    g_vec[5:6, :] += column_sum(grad)
    d3 = norm_back(grad, n3, inv3, vecs[2:3, :])
    df = d3.astype(bf16)
    hid[rows_here, :] = hidden_b
    third[rows_here, :] = df
    g_vec[6:7, :] += column_sum(df.astype(f32))
    downs, dus, backs = {}, {}, [d3]

    def down_back(c):
        downs[c] = dot(df, w2(c), 1, 1)

    def bend_back(c):
        dus[c] = (downs.pop(c) * slope[:, cols(c)]).astype(bf16)
        g_b1[0:1, cols(c)] += column_sum(dus[c].astype(f32))

    def up_back(c):
        du = dus.pop(c)
        pre[rows_here, cols(c)] = du
        backs.append(dot(du, w1(c), 1, 1))

    pipelined(4, down_back, bend_back, up_back)
    back = ((backs[0] + backs[1]) + (backs[2] + backs[3])) + backs[4]
    g_vec[1:2, :] += column_sum(back * n2)
    g_vec[4:5, :] += column_sum(back)
    second = norm_back(back, n2, inv2, vecs[1:2, :])
    d2[...] = second
    dco = second.astype(bf16)
    gco[...] += dot(oct_[...], dco)
    gc[...] = dot(dco, square(wo, 0), 1, 1).astype(bf16)

    @pl.when(i == pl.num_programs(0) - 1)
    def _():
        keep = info[3 * SEQS + 1] > 0
        g_co[...] = jnp.where(keep, gco[...], 0.0).astype(bf16)
        targets = ((keep_ffn, info[CORE]), (send_ffn, 1 - info[CORE]))
        for c in range(4):
            gw[...] = jnp.where(keep, dot(hid[...], pre[:, cols(c)], 0, 0), 0.0)
            for ref, core in targets:
                for n in range(4):
                    r0 = pl.multiple_of((2 * n + core) * 4 * chunk, 4 * chunk)
                    part = gw[pl.ds(r0, 4 * chunk), :].astype(bf16).reshape(4, chunk, D)
                    ref[4 * n : 4 * n + 4, c * chunk : (c + 1) * chunk, :] = part
        for c in range(4):
            gw[...] = jnp.where(keep, dot(act[:, cols(c)], third[...], 0, 0), 0.0)
            for ref, core in targets:
                r0 = pl.multiple_of(core * 4 * BROWS, 4 * BROWS)
                part = gw[pl.ds(r0, 4 * BROWS), :].astype(bf16).reshape(4, BROWS, D)
                ref[4 * c : 4 * c + 4, BROWS:, :] = part
        g_b1[...] = jnp.where(keep, g_b1[...], 0.0)
        g_vec[...] = jnp.where(keep, g_vec[...], 0.0)


def unpack_into(info, i, blocks, out):
    @pl.when(i < MICRO)
    def _():
        out[0] = blocks[info[SOURCES + jnp.minimum(i, MICRO - 1)]].astype(f32)


def cross_post_kernel(
    info, blocks, dqct, dkc, dvc, mem, d2, n1, inv1, ot, wa, wb, vecs, g_co,
    out, dmem, d1, go, g_cross, g_wo, g_vec,
    gcq, gck, gcv, gwo,
):
    i = pl.program_id(0)
    unpack_into(info, i, blocks, out)

    @pl.when(i == 0)
    def _():
        for ref in (gcq, gck, gcv, gwo, g_vec):
            ref[...] = jnp.zeros_like(ref)

    m, dk, dv = mem[...], dkc[...], dvc[...]
    dmem[...] = (dot(dk, square(wb, 1), 1, 1) + dot(dv, square(wb, 2), 1, 1)).astype(bf16)
    gck[...] += dot(m, dk, 0, 0)
    gcv[...] += dot(m, dv, 0, 0)
    normed = n1[...]
    hidden = (normed * vecs[0:1, :] + vecs[3:4, :]).astype(bf16)
    dq = dqct[...].T
    gcq[...] += dot(hidden, dq, 0, 0)
    back = d2[...] + dot(dq, square(wb, 0), 1, 1)
    g_vec[0:1, :] += column_sum(back * normed)
    g_vec[3:4, :] += column_sum(back)
    first = norm_back(back, normed, inv1[...], vecs[0:1, :])
    d1[...] = first
    dao = first.astype(bf16)
    gwo[...] += dot(ot[...], dao)
    go[...] = dot(dao, square(wa, 0), 1, 1).astype(bf16)

    @pl.when(i == pl.num_programs(0) - 1)
    def _():
        keep = info[3 * SEQS + 1] > 0
        for n, ref in enumerate((gcq, gck, gcv)):
            g_cross[n * D : (n + 1) * D, :] = jnp.where(keep, ref[...], 0.0).astype(bf16)
        g_cross[3 * D :, :] = g_co[...]
        g_wo[...] = jnp.where(keep, gwo[...], 0.0).astype(bf16)
        g_vec[...] = jnp.where(keep, g_vec[...], 0.0)


def self_post_kernel(
    info, dqt, dk_ref, dv_ref, x_ref, d1, wa, g_wo, g_cross, g_small,
    dtok, keep_out, send_out,
    gq, gk, gv,
):
    i = pl.program_id(0)

    @pl.when(i == 0)
    def _():
        for ref in (gq, gk, gv):
            ref[...] = jnp.zeros_like(ref)

    x, dk, dv, dq = x_ref[...], dk_ref[...], dv_ref[...], dqt[...].T
    dtok[...] = (
        d1[...]
        + dot(dq, square(wa, 0), 1, 1)
        + dot(dk, square(wa, 1), 1, 1)
        + dot(dv, square(wa, 2), 1, 1)
    ).astype(bf16)
    gq[...] += dot(x, dq, 0, 0)
    gk[...] += dot(x, dk, 0, 0)
    gv[...] += dot(x, dv, 0, 0)

    @pl.when(i == pl.num_programs(0) - 1)
    def _():
        keep = info[3 * SEQS + 1] > 0
        rows = 4 * BROWS
        for ref, core in ((keep_out, info[CORE]), (send_out, 1 - info[CORE])):
            for n in range(4):
                blocks = slice(4 * n, 4 * n + 4)
                r0 = pl.multiple_of(core * rows, rows)
                if n < 3:
                    part = jnp.where(keep, (gq, gk, gv)[n][pl.ds(r0, rows), :], 0.0).astype(bf16)
                else:
                    part = g_wo[pl.ds(r0, rows), :]
                ref[blocks, :BROWS, :] = part.reshape(4, BROWS, D)
                part = g_cross[pl.ds(pl.multiple_of(r0 + n * D, rows), rows), :]
                ref[blocks, BROWS : 2 * BROWS, :] = part.reshape(4, BROWS, D)
                ref[blocks, 2 * BROWS :, : 2 * LANES] = g_small[pl.ds((2 * n + core) * 4, 4), :, :]
                ref[blocks, 2 * BROWS :, 2 * LANES :] = jnp.zeros((4, SMALL, D - 2 * LANES), bf16)


def pick_kernel(count, places, *refs):
    arrays, outs, sems = refs[:count], refs[count : 5 * count], refs[5 * count]
    copies = []
    for n, array in enumerate(arrays):
        for k in range(PIECES):
            copies.append(
                pltpu.make_async_copy(array.at[places[k]], outs[n * PIECES + k], sems.at[n, k])
            )
    for copy in copies:
        copy.start()
    for copy in copies:
        copy.wait()


def unpack_kernel(info, blocks, out):
    unpack_into(info, pl.program_id(0), blocks, out)


def plus(*parts):
    total = parts[0].astype(f32)
    for part in parts[1:]:
        total = total + part.astype(f32)
    return total


def route_one_kernel(info, keep, recv, a_keep, a_send, b_keep, b_send):
    x, y = info[CORE + 1], info[CORE + 2]
    for n in range(2):
        for ref, own in ((a_keep, x), (a_send, 1 - x)):
            at = (2 * n + own) * 4
            ref[n] = plus(keep[pl.ds(at, 2)], recv[pl.ds(at, 2)]).astype(bf16)
        for ref, own in ((b_keep, y), (b_send, 1 - y)):
            at = (2 * own + n) * 4 + 2
            ref[n] = plus(keep[pl.ds(at, 2)], recv[pl.ds(at, 2)]).astype(bf16)


def route_two_kernel(info, a, ra, b, rb, a_keep, a_send, b_keep, b_send):
    x, y = info[CORE + 1], info[CORE + 2]
    for ref, own in ((a_keep, y), (a_send, 1 - y)):
        ref[...] = plus(a[own], ra[own]).astype(bf16)
    for ref, own in ((b_keep, x), (b_send, 1 - x)):
        ref[...] = plus(b[own], rb[own]).astype(bf16)


def route_three_kernel(info, a, ra, b, rb, o0, o1, o2, o3, total):
    total[0:2] = plus(a[...], ra[...]).astype(bf16)
    total[2:4] = plus(b[...], rb[...]).astype(bf16)
    for k, ref in enumerate((o0, o1, o2, o3)):
        ref[...] = total[lax.rem(info[3 * SEQS] + k, PIECES)]


def route_four_kernel(r0, r1, r2, r3, out):
    out[...] = plus(r0[...], r1[...], r2[...], r3[...])


SMEM = pl.BlockSpec(memory_space=pltpu.SMEM)
WHOLE = pl.BlockSpec(memory_space=pltpu.VMEM)
ROWS = pl.BlockSpec((PIECE, D), lambda i: (i, 0))
COLS = pl.BlockSpec((D, PIECE), lambda i: (0, i))
BLOCKS_IN = pl.BlockSpec(
    (PIECES, PIECE, D), lambda i: (0, 0, 0), pipeline_mode=pl.Buffered(buffer_count=1)
)
BATCH = pl.BlockSpec((1, PIECE, D), lambda i: (jnp.minimum(i, MICRO - 1), 0, 0))
ROWS_Q = pl.BlockSpec((QB, D), lambda i: (i, 0))
COLS_Q = pl.BlockSpec((D, QB), lambda i: (0, i))
HEADS_Q = pl.BlockSpec((HEADS, QB), lambda i: (0, i))
OUT_W = pl.BlockSpec(
    (BLOCKS // 4, BROWS, D), lambda i: (3, 0, 0), pipeline_mode=pl.Buffered(buffer_count=1)
)
ROWS_F = pl.BlockSpec((FR, D), lambda i: (i, 0))
COLS_F = pl.BlockSpec((D, FR), lambda i: (0, i))
ONES = pl.BlockSpec((PIECE, 1), lambda i: (i, 0))


def fixed(*shape):
    return pl.BlockSpec(
        shape, lambda i: (0,) * len(shape), pipeline_mode=pl.Buffered(buffer_count=1)
    )


def shape(dims, dtype=bf16):
    return jax.ShapeDtypeStruct(dims, dtype)


def call(kernel, name, grid, in_specs, out_specs, out_shape, scratch, flops, *args):
    return pl.pallas_call(
        kernel,
        grid=grid,
        in_specs=in_specs,
        out_specs=out_specs,
        out_shape=out_shape,
        scratch_shapes=scratch,
        name=name,
        compiler_params=pltpu.CompilerParams(vmem_limit_bytes=VMEM_LIMIT),
        cost_estimate=pl.CostEstimate(flops=flops, bytes_accessed=8 << 20, transcendentals=0),
    )(*args)


ROWMAJOR = shape((GROUP, D))
COLMAJOR = shape((D, GROUP))


def project_rows(info, pieces, weights, kind):
    outs = [ROWMAJOR] + ([COLMAJOR] if kind else []) + [ROWMAJOR, ROWMAJOR]
    w_specs = [WHOLE]
    if kind == 2:
        outs = outs + [shape((BLOCKS,) + weights[1].shape[1:])]
        w_specs = [SMEM, WHOLE, WHOLE]
    elif kind == 0:
        w_specs = [fixed(BLOCKS, BROWS, D)]
    return call(
        functools.partial(project_kernel, kind),
        "project",
        (1,),
        [SMEM] + [WHOLE] * PIECES + w_specs,
        [WHOLE] * len(outs),
        outs,
        [],
        4 << 30,
        info,
        *pieces,
        *weights,
    )


def saved_rows(cross):
    return MEM_LEN if cross else KEPT + KB // 2


def attend(info, qt, k, v, cross):
    keep = (HEADS, saved_rows(cross), QB)
    return call(
        functools.partial(attend_kernel, cross),
        "attend",
        (GROUP // QB,),
        [SMEM, COLS_Q, fixed(GROUP, D), fixed(GROUP, D)],
        [COLS_Q, HEADS_Q, SMEM, pl.BlockSpec((1,) + keep, lambda i: (i, 0, 0, 0))],
        [
            COLMAJOR,
            shape((HEADS, GROUP), f32),
            shape((GROUP // QB,), jnp.int32),
            shape((GROUP // QB,) + keep),
        ],
        [
            pltpu.VMEM((D, GROUP), bf16),
            pltpu.VMEM((HEADS, QB), f32),
            pltpu.VMEM((HEADS, QB), f32),
            pltpu.VMEM((HEADS, QB), f32),
            pltpu.VMEM((D, QB), f32),
            pltpu.VMEM((KB, QB), f32),
        ],
        30 << 30,
        info,
        qt,
        k,
        v,
    )


def attend_back(info, qt, k, v, g, ot, lse, flags, saved, cross):
    keep = (HEADS, saved_rows(cross), QB)
    return call(
        functools.partial(attend_back_kernel, cross),
        "attend_back",
        (GROUP // QB,),
        [SMEM, SMEM, COLS_Q, fixed(GROUP, D), fixed(GROUP, D), ROWS_Q, COLS_Q, HEADS_Q]
        + [pl.BlockSpec((1,) + keep, lambda i: (i, 0, 0, 0))],
        [COLS_Q, fixed(GROUP, D), fixed(GROUP, D)],
        [COLMAJOR, ROWMAJOR, ROWMAJOR],
        [
            pltpu.VMEM((D, GROUP), bf16),
            pltpu.VMEM((D, QB), f32),
            pltpu.VMEM((GROUP, D), f32),
            pltpu.VMEM((GROUP, D), f32),
            pltpu.VMEM((D, QB), bf16),
            pltpu.VMEM((HEADS // 2, 2 * QB, 2 * HEAD_DIM), bf16),
            pltpu.VMEM((HEADS // 2, 2 * QB, 2 * HEAD_DIM), bf16),
            pltpu.VMEM((KB, QB), f32),
        ],
        60 << 30,
        info,
        flags,
        qt,
        k,
        v,
        g,
        ot,
        lse,
        saved,
    )


ANY = pl.BlockSpec(memory_space=pl.ANY)


def pick_four(arrays, places):
    n = len(arrays)
    outs = call(
        functools.partial(pick_kernel_args, n),
        "pick",
        (),
        [SMEM] + [ANY] * n,
        [WHOLE] * (PIECES * n),
        [shape(a.shape[1:], a.dtype) for a in arrays for _ in range(PIECES)],
        [pltpu.SemaphoreType.DMA((n, PIECES))],
        1 << 20,
        places,
        *arrays,
    )
    return [list(outs[PIECES * m : PIECES * (m + 1)]) for m in range(n)]


def pick_kernel_args(count, places, *refs):
    pick_kernel(count, places, *refs)


def unpack(info, blocks, micro):
    return call(
        unpack_kernel,
        "unpack",
        (micro,),
        [SMEM, BLOCKS_IN],
        BATCH,
        shape((micro, PIECE, D), f32),
        [],
        1 << 20,
        info,
        blocks,
    )


def route_one(info, keep, recv):
    half = shape((2, 2) + keep.shape[1:])
    return call(
        route_one_kernel, "route_one", (), [SMEM, WHOLE, WHOLE], [WHOLE] * 4, [half] * 4, [], 1 << 20,
        info, keep, recv,
    )


def route_two(info, a, ra, b, rb):
    half = shape(a.shape[1:])
    return call(
        route_two_kernel, "route_two", (), [SMEM] + [WHOLE] * 4, [WHOLE] * 4, [half] * 4, [], 1 << 20,
        info, a, ra, b, rb,
    )


def route_three(info, a, ra, b, rb):
    block = a.shape[1:]
    return call(
        route_three_kernel, "route_three", (), [SMEM] + [WHOLE] * 4, [WHOLE] * 4,
        [shape(block)] * 4, [pltpu.VMEM((4,) + block, bf16)], 1 << 20,
        info, a, ra, b, rb,
    )


def route_last_kernel(r0, r1, r2, r3, own, cross, gain, bias, out_bias, in_bias):
    def rows(first, count):
        part = slice(first, first + count)
        return plus(r0[part, :], r1[part, :], r2[part, :], r3[part, :])

    own[...] = rows(0, BROWS)
    cross[...] = rows(BROWS, BROWS)
    small = rows(2 * BROWS, SMALL)
    turned = small[:, :LANES].T
    gain[...] = turned[0:3]
    bias[...] = turned[3:6]
    out_bias[...] = turned[6:7]
    in_bias[...] = small[0:1, LANES : LANES + BROWS]


def route_last(pieces, rows, out_rows):
    outs = [(rows, D), (rows, D), (3, out_rows), (3, out_rows), (1, out_rows), (1, rows)]
    return call(
        route_last_kernel, "route_last", (), [WHOLE] * 4, [WHOLE] * 6, [shape(o, f32) for o in outs], [],
        1 << 20, *pieces,
    )


def route_four(pieces):
    return call(
        route_four_kernel, "route_four", (), [WHOLE] * 4, WHOLE, shape(pieces[0].shape, f32), [], 1 << 20,
        *pieces,
    )


def tie(value, *deps):
    return lax.optimization_barrier((value, deps))[0]


def dp_swap(array, bit):
    n = lax.axis_size("dp")
    return lax.ppermute(array, "dp", [(d, d ^ bit) for d in range(n)])


def turns(arrays):
    n = lax.axis_size("fsdp")
    return [arrays[0]] + [
        lax.ppermute(arrays[k], "fsdp", [(m, (m + k) % n) for m in range(n)])
        for k in range(1, len(arrays))
    ]


def local(
    tokens, memory, cotangent, lengths, seq_order, memory_pick,
    self_attn, cross_attn, ffn_in, ffn_in_bias, ffn_out, ffn_out_bias, norm_gain, norm_bias,
):
    axes = ("dp", "fsdp")
    n_dp, members = lax.axis_size("dp"), lax.axis_size("fsdp")
    micro = tokens.shape[0]
    owners = n_dp * members
    dp, z = lax.axis_index("dp"), lax.axis_index("fsdp")

    def offset(d):
        return d % 2 if micro < members else 0

    def unit_at(d, member):
        return member - offset(d)

    mine = unit_at(dp, z)
    valid = (mine >= 0) & (mine < micro)
    unit = jnp.clip(mine, 0, micro - 1)

    def pairs(k):
        out = []
        for d in range(n_dp):
            for source in range(members):
                target = (source + k) % members
                if 0 <= unit_at(d, target) < micro:
                    out.append((d * members + source, d * members + target))
        return out

    def to_unit(pieces):
        return [pieces[0]] + [
            lax.ppermute(pieces[k], axes, pairs(k)) for k in range(1, members)
        ]

    def from_unit(rows_of_unit):
        blocks = rows_of_unit.reshape(members, PIECE, D)
        return lax.all_to_all(blocks, "fsdp", split_axis=0, concat_axis=0)

    def row_of(array):
        return lax.dynamic_index_in_dim(array, unit, 0, False)[0]

    boxed = n_dp == 8 and members == 4
    shifts = jnp.arange(members, dtype=jnp.int32)

    targets = jnp.clip(lax.rem(z + shifts, members) - offset(dp), 0, micro - 1)
    sources = jnp.arange(micro, dtype=jnp.int32) + offset(dp)
    targets = targets.at[0].set(unit).astype(jnp.int32)

    bits = [dp & 1, (dp >> 1) & 1, (dp >> 2) & 1] if boxed else [jnp.zeros_like(dp)] * 3
    info = jnp.concatenate(
        [
            row_of(lengths),
            row_of(seq_order),
            row_of(memory_pick),
            jnp.stack([z, valid.astype(jnp.int32), *bits]),
            sources,
        ]
    ).astype(jnp.int32)

    smalls = jnp.concatenate(
        [ffn_in_bias, ffn_out_bias, norm_gain.T.reshape(-1), norm_bias.T.reshape(-1)]
    )
    rows = self_attn.shape[0]
    in_rows = ffn_in.shape[0]
    n_smalls = smalls.shape[0]
    token_slices = pick_four([tokens], targets)[0]
    smalls = tie(smalls, token_slices)
    small_row = jnp.pad(smalls, (0, 16 * D - n_smalls)).reshape(16, D)
    bundle_a = jnp.concatenate([self_attn, small_row], axis=0)
    in_blocks = ffn_in.reshape(in_rows, 4, D).transpose(1, 0, 2).reshape(4 * in_rows, D)
    bundle_f = jnp.concatenate([ffn_out, in_blocks], axis=0)
    if boxed:
        turned = turns([bundle_a] * members)
    token_pieces = to_unit(token_slices)
    late = tie([memory, cotangent], token_slices)
    memory_slices, cotangent_slices = pick_four(late, targets)
    if boxed:
        a0, b0 = jnp.stack(turned[:2]), jnp.stack(turned[2:])
        a1, b1 = dp_swap(a0, 2), dp_swap(b0, 4)
        a2 = dp_swap(jnp.stack([a0, a1]), 4)
        b2 = dp_swap(jnp.stack([b0, b1]), 2)
        near = jnp.concatenate([a0, a1, a2[0], a2[1], b0, b1, b2[0], b2[1]])
        masks = jnp.array([0, 0, 2, 2, 4, 4, 6, 6, 0, 0, 4, 4, 2, 2, 6, 6], jnp.int32)
        steps = jnp.array([0, 1] * 4 + [2, 3] * 4, jnp.int32)
        owner = (dp ^ masks) * members + lax.rem(z - steps + members, members)
        places = jnp.concatenate([owner, owner ^ members]).astype(jnp.int32)
        near = tie(near, token_pieces[1:], memory_slices, cotangent_slices, info, places)
        far = dp_swap(near, 1)
    else:
        all_a = lax.all_gather(bundle_a, axes, axis=0, tiled=False)
        wa = jnp.pad(all_a[:, :rows].reshape(BLOCKS, BROWS, D), ((0, 0), (0, SMALL), (0, 0)))
    all_b = lax.all_gather(tie(cross_attn, token_slices), axes, axis=0, tiled=False)
    all_f = lax.all_gather(tie(bundle_f, token_slices), axes, axis=0, tiled=False)
    def blocked(array, count):
        return array.reshape(BLOCKS, count, D)

    if owners == BLOCKS:
        wb, wf = all_b, all_f
    else:
        first = all_f[:, rows:].reshape(owners, 4, in_rows, D).transpose(1, 0, 2, 3)
        first = first.reshape(4, BLOCKS, BROWS // 4, D).transpose(1, 0, 2, 3)
        wb = blocked(all_b, BROWS)
        wf = jnp.concatenate([blocked(all_f[:, :rows], BROWS), blocked(first, BROWS)], axis=1)
    if boxed:
        x, qt, k, v, wa = project_rows(info, token_pieces, (places, near, far), 2)
        all_a = wa
    else:
        x, qt, k, v = project_rows(info, token_pieces, (wa,), 1)
    small = all_a[:, rows, :n_smalls].astype(f32)
    out_rows = D // owners
    b1 = small[:, :rows].reshape(1, FF)
    at = rows + out_rows
    vec_rows = [small[:, at + n * out_rows : at + (n + 1) * out_rows].reshape(1, D) for n in range(6)]
    vecs = jnp.concatenate(
        vec_rows + [small[:, rows:at].reshape(1, D), jnp.zeros((1, D), f32)], axis=0
    )

    memory_pieces = to_unit(tie(memory_slices, x))
    ot, *self_saved = attend(info, qt, k, v, False)
    ot = tie(ot, *memory_pieces[1:])
    cotangent_pieces = to_unit(tie(cotangent_slices, memory_pieces[1:], ot))
    n1, inv1, qct = call(
        first_norm_kernel,
        "first_norm",
        (PIECES,),
        [COLS, ROWS, OUT_W, fixed(BLOCKS, BROWS, D), fixed(8, D)],
        [ROWS, ONES, COLS],
        [shape((GROUP, D), f32), shape((GROUP, 1), f32), COLMAJOR],
        [],
        2 << 30,
        ot,
        x,
        wa,
        wb,
        vecs,
    )
    mem, kc, vc = project_rows(info, memory_pieces, (wb,), 0)
    oct_, *cross_saved = attend(info, qct, kc, vc, True)
    y_out, d2, gc, keep_ffn, send_ffn, g_co, g_b1, g_vec = call(
        ffn_kernel,
        "ffn",
        (GROUP // FR,),
        [SMEM, COLS_F, ROWS_F, OUT_W, fixed(BLOCKS, 2 * BROWS, D), fixed(8, D), fixed(1, FF)]
        + [fixed(PIECE, D)] * 4,
        [
            fixed(GROUP, D),
            ROWS_F,
            ROWS_F,
            fixed(HALF, 2 * BROWS, D),
            fixed(HALF, 2 * BROWS, D),
            fixed(D, D),
            fixed(1, FF),
            fixed(8, D),
        ],
        [
            ROWMAJOR,
            shape((GROUP, D), f32),
            ROWMAJOR,
            shape((HALF, 2 * BROWS, D)),
            shape((HALF, 2 * BROWS, D)),
            shape((D, D)),
            shape((1, FF), f32),
            shape((8, D), f32),
        ],
        [
            pltpu.VMEM((GROUP, FF), bf16),
            pltpu.VMEM((GROUP, FF), bf16),
            pltpu.VMEM((GROUP, D), bf16),
            pltpu.VMEM((GROUP, D), bf16),
            pltpu.VMEM((FR, FF), f32),
            pltpu.VMEM((FR, D), f32),
            pltpu.VMEM((D, D), f32),
            pltpu.VMEM((D, D), f32),
        ],
        32 << 30,
        info,
        oct_,
        n1,
        wb,
        wf,
        vecs,
        b1,
        *cotangent_pieces,
    )
    y_pieces = from_unit(y_out)
    if boxed:
        ffn_a, send_a, ffn_b, send_b = route_one(info, keep_ffn, dp_swap(send_ffn, 1))
        recv_a, recv_b = dp_swap(send_a, 2), dp_swap(send_b, 4)
        gc = tie(gc, send_a)

    dqct, dkc, dvc = attend_back(info, qct, kc, vc, gc, oct_, *cross_saved, True)
    if boxed:
        recv_a, recv_b, ffn_a, ffn_b = tie((recv_a, recv_b, ffn_a, ffn_b), dqct)
        ffn_a, send_a, ffn_b, send_b = route_two(info, ffn_a, recv_a, ffn_b, recv_b)
        recv_a, recv_b = dp_swap(send_a, 4), dp_swap(send_b, 2)
        g_co = tie(g_co, send_a)
    layer_output, *m_and_rest = call(
        cross_post_kernel,
        "cross_post",
        (PIECES,),
        [SMEM, BLOCKS_IN, COLS, ROWS, ROWS, ROWS, ROWS, ROWS, ONES, COLS]
        + [OUT_W, fixed(BLOCKS, BROWS, D), fixed(8, D), fixed(D, D)],
        [BATCH, ROWS, ROWS, ROWS, fixed(4 * D, D), fixed(D, D), fixed(8, D)],
        [
            shape((micro, PIECE, D), f32),
            ROWMAJOR,
            shape((GROUP, D), f32),
            ROWMAJOR,
            shape((4 * D, D)),
            shape((D, D)),
            shape((8, D), f32),
        ],
        [pltpu.VMEM((D, D), f32)] * 4,
        9 << 30,
        info,
        y_pieces,
        dqct,
        dkc,
        dvc,
        mem,
        d2,
        n1,
        inv1,
        ot,
        wa,
        wb,
        vecs,
        g_co,
    )
    m_out, d1, go, g_cross, g_wo, g_vec_one = m_and_rest
    m_pieces = from_unit(m_out)
    if boxed:
        recv_a, recv_b, ffn_a, ffn_b = tie((recv_a, recv_b, ffn_a, ffn_b), d1)
        ffn_pieces = turns(route_three(info, ffn_a, recv_a, ffn_b, recv_b))
        go = tie(go, ffn_pieces[0])
    g_vec = g_vec + g_vec_one
    if boxed:
        columns = g_vec.reshape(8, BLOCKS, SMALL).transpose(1, 2, 0)
        columns = jnp.pad(columns, ((0, 0), (0, 0), (0, LANES - 8)))
        first = jnp.pad(g_b1.reshape(BLOCKS, 1, rows), ((0, 0), (0, SMALL - 1), (0, LANES - rows)))
        g_small = jnp.concatenate([columns, first], axis=2).astype(bf16)
    else:
        g_small = jnp.zeros((BLOCKS, SMALL, 2 * LANES), bf16)
        small_grads = jnp.concatenate(
            [g_b1.reshape(owners, rows), g_vec[6].reshape(owners, out_rows)]
            + [g_vec[n].reshape(owners, out_rows) for n in range(6)],
            axis=1,
        )
    dqt, dk, dv = attend_back(info, qt, k, v, go, ot, *self_saved, False)
    if boxed:
        d1 = tie(d1, ffn_pieces, m_pieces)
    last_rows = 2 * BROWS + SMALL
    t_out, keep_last, send_last = call(
        self_post_kernel,
        "self_post",
        (PIECES,),
        [SMEM, COLS, ROWS, ROWS, ROWS, ROWS, fixed(3 * BLOCKS // 4, BROWS, D), fixed(D, D), fixed(4 * D, D), fixed(BLOCKS, SMALL, 2 * LANES)],
        [ROWS] + [fixed(HALF, last_rows, D)] * 2,
        [ROWMAJOR] + [shape((HALF, last_rows, D))] * 2,
        [pltpu.VMEM((D, D), f32)] * 3,
        4 << 30,
        info,
        dqt,
        dk,
        dv,
        x,
        d1,
        wa,
        g_wo,
        g_cross,
        g_small,
    )
    t_pieces = from_unit(t_out)
    if boxed:
        recv_last = dp_swap(send_last, 1)
        near, send_a, far, send_b = route_one(info, keep_last, recv_last)
        recv_a, recv_b = dp_swap(send_a, 2), dp_swap(send_b, 4)

    def whole_blocks(keep, send):
        both = jnp.stack([keep, send]).reshape(2, 4, 4, -1, D)
        return both.transpose(1, 0, 2, 3, 4).reshape(BLOCKS, -1, D)

    def owned(array):
        return lax.psum_scatter(array, axes, scatter_dimension=0, tiled=True)[0].astype(f32)

    if boxed:
        ffn_part = route_four(tie(ffn_pieces, send_a))
        memory_grad = unpack(info, tie(m_pieces, send_a), micro)
        near = tie(near, ffn_part, memory_grad)
        near, send_a, far, send_b = route_two(info, near, recv_a, far, recv_b)
        recv_a, recv_b = dp_swap(send_a, 4), dp_swap(send_b, 2)
        input_grad = unpack(info, tie(t_pieces, send_a), micro)
        near = tie(near, input_grad)
        last_pieces = turns(route_three(info, near, recv_a, far, recv_b))
        self_attn_grad, cross_attn_grad, gain_grad, bias_grad, out_bias, in_bias = route_last(
            last_pieces, rows, out_rows
        )
    else:
        memory_grad = unpack(info, m_pieces, micro)
        input_grad = unpack(info, t_pieces, micro)
        ffn = whole_blocks(keep_ffn, send_ffn)
        second = ffn[:, BROWS:].reshape(owners, rows, D)
        first = ffn[:, :BROWS].reshape(BLOCKS, 4, BROWS // 4, D).transpose(1, 0, 2, 3)
        first = first.reshape(4, owners, in_rows, D).transpose(1, 0, 2, 3)
        ffn_part = owned(jnp.concatenate([first.reshape(owners, rows, D), second], axis=1))
        rest = whole_blocks(keep_last, send_last)
        self_attn_grad = owned(rest[:, :BROWS].reshape(owners, rows, D))
        cross_attn_grad = owned(rest[:, BROWS : 2 * BROWS].reshape(owners, rows, D))
        small_out = owned(small_grads)
        at = rows + out_rows
        norm_part = small_out[at : at + 6 * out_rows].reshape(6, out_rows)
        gain_grad, bias_grad = norm_part[:3], norm_part[3:]
        in_bias, out_bias = small_out[:rows], small_out[rows:at]
    ffn_in_grad = ffn_part[:rows].reshape(4, in_rows, D).transpose(1, 0, 2).reshape(in_rows, FF)
    return (
        layer_output,
        input_grad,
        memory_grad,
        self_attn_grad,
        cross_attn_grad,
        ffn_in_grad,
        in_bias.reshape(rows),
        ffn_part[rows:],
        out_bias.reshape(out_rows),
        gain_grad.T,
        bias_grad.T,
    )


def solution(mesh):
    rows = P(None, ("dp", "fsdp"), None)
    group = P(None, "dp", None)
    shard = P(("dp", "fsdp"), None)
    flat = P(("dp", "fsdp"))
    in_specs = (rows,) * 3 + (group,) * 3 + (shard, shard, shard, flat, shard, flat, shard, shard)
    out_specs = (rows,) * 3 + (shard, shard, shard, flat, shard, flat, shard, shard)
    return jax.shard_map(local, mesh=mesh, in_specs=in_specs, out_specs=out_specs, check_vma=False)
```
